512 devices in a mesh: sec: 8 (over y), rad: 16 (over z, x_hi), ax: 4 (over x_lo, core).
Axes of the slice: x: 4 (x_hi: 2, x_lo: 2; x = x_hi * 2 + x_lo), y: 8, z: 8, core: 2. Of those that a mesh axis runs over, the one named last changes fastest.
Arguments:
- state: float32 [5, 8, 1024, 2048], P(None, 'ax', 'rad', 'sec'), may hold values from -1.6 to 4, as said below
- coarsen: int32 [16], replicated, may hold values from 1 to 16, as said below
Outputs:
- tendency: float32 [5, 8, 1024, 2048], P(None, 'ax', 'rad', 'sec')
The draws below stay inside these ranges and needn't reach their ends.
Inputs may be any that keep to these rules, and one draw needn't show every extreme that they name: `coarsen`: each entry is a power of two; cycle 0 takes 16 and cycle 16 - 1 takes 1. state[0] (density) lies in 0.6 to 1.4, the momenta in -1.6 to 1.6, state[4] (energy) in 2.5 to 4.0.
All inputs are finite; a program needn't handle non-finite values.
Results may differ from the reference program's by a relative error of at most 0.0003.
Values sent between devices are 32-bit elements; how exact they have to be, the bound alone decides.
A program may use at most 64 MiB of HBM per device.

```python
import math
import jax
import jax.numpy as jnp
from jax import lax

NT = 2048
NR = 1024
R_NEAR = 16
FMAX = 16
NA = 8


def draw_state(key, part):
    subkeys = jax.random.split(key, 3)
    grid_shape = (NA, NR, NT)
    density = jax.random.uniform(subkeys[0], grid_shape, minval=0.6, maxval=1.4)
    momenta = jnp.clip(0.4 * jax.random.normal(subkeys[1], (3,) + grid_shape), -1.6, 1.6)
    energy = jax.random.uniform(subkeys[2], grid_shape, minval=2.5, maxval=4.0)
    return jnp.concatenate([density[None], momenta, energy[None]], axis=0).astype(jnp.float32)


def draw_coarsen(key, part):
    levels = jax.random.randint(key, (R_NEAR,), 0, FMAX.bit_length()).astype(jnp.int32)
    factors = jnp.left_shift(jnp.ones((R_NEAR,), jnp.int32), levels)
    factors = factors.at[0].set(FMAX).at[R_NEAR - 1].set(1)
    return factors.astype(jnp.int32)


def setup_inputs(seed: int = 0) -> dict:
    seeds = jax.random.split(jax.random.key(seed), 3)
    state = draw_state(jax.random.fold_in(seeds[2], 71), 0)
    coarsen = draw_coarsen(jax.random.fold_in(seeds[2], 71), 0)
    return dict(state=state, coarsen=coarsen)


GAMMA = 1.4
KAPPA = 1.44


def primitive(plane):
    density = plane[0]
    mom_ax = plane[1]
    mom_rad = plane[2]
    mom_az = plane[3]
    energy = plane[4]
    vel_ax = mom_ax / density
    vel_rad = mom_rad / density
    vel_az = mom_az / density
    pressure = (GAMMA - 1.0) * (energy - 0.5 * (mom_ax * vel_ax + mom_rad * vel_rad + mom_az * vel_az))
    return mom_ax, mom_rad, mom_az, energy, vel_ax, vel_rad, vel_az, pressure


def axial_flux(plane):
    mom_ax, mom_rad, mom_az, energy, vel_ax, vel_rad, vel_az, pressure = primitive(plane)
    return jnp.stack([mom_ax, mom_ax * vel_ax + pressure, mom_rad * vel_ax, mom_az * vel_ax, (energy + pressure) * vel_ax])


def reference(state, coarsen):
    dtheta = 2.0 * math.pi / NT
    radius = (jnp.arange(NR, dtype=jnp.float32) + 0.5)[:, None]

    def flux_at(index):
        clipped = jnp.clip(index, 0, NA - 1).astype(jnp.int32)
        plane = lax.dynamic_index_in_dim(state, clipped, axis=1, keepdims=False)
        valid = ((index >= 0) & (index < NA)).astype(jnp.float32)
        return axial_flux(plane) * valid

    def one_plane(index):
        plane = lax.dynamic_index_in_dim(state, index, axis=1, keepdims=False)
        mom_ax, mom_rad, mom_az, energy, vel_ax, vel_rad, vel_az, pressure = primitive(plane)
        flux_rad = jnp.stack([mom_rad, mom_ax * vel_rad, mom_rad * vel_rad + pressure, mom_az * vel_rad, (energy + pressure) * vel_rad]) * radius
        flux_az = jnp.stack([mom_az, mom_ax * vel_az, mom_rad * vel_az, mom_az * vel_az + pressure, (energy + pressure) * vel_az])
        result = -(flux_at(index + 1) - flux_at(index - 1)) * 0.5
        padded_rad = jnp.pad(flux_rad, ((0, 0), (1, 1), (0, 0)))
        result = result - (padded_rad[:, 2:] - padded_rad[:, :-2]) * 0.5 / radius
        result = result - (jnp.roll(flux_az, -1, axis=2) - jnp.roll(flux_az, 1, axis=2)) * 0.5 / (radius * dtheta)
        zero_part = jnp.zeros_like(pressure)
        source = jnp.stack([zero_part, zero_part, (pressure + mom_az * vel_az) / radius, -(mom_rad * vel_az) / radius, zero_part])
        return result + source

    tendency = lax.map(one_plane, jnp.arange(NA, dtype=jnp.int32))
    tendency = jnp.transpose(tendency, (1, 0, 2, 3))
    cycle_rows = []
    for cycle_index in range(R_NEAR):
        cycle_line = tendency[:, :, cycle_index, :]
        smoothed = jnp.zeros_like(cycle_line)
        for power in range(FMAX.bit_length()):
            factor = 2 ** power
            blocks = NT // factor
            coarse = cycle_line.reshape(5, NA, blocks, factor).sum(axis=-1) / factor
            stiffness = KAPPA / (factor * dtheta) ** 2
            wavenumber = jnp.arange(blocks // 2 + 1, dtype=jnp.float32)
            denominator = 1.0 + 4.0 * stiffness * jnp.sin(math.pi * wavenumber / blocks) ** 2
            solved = jnp.fft.irfft(jnp.fft.rfft(coarse, axis=-1) / denominator, n=blocks, axis=-1)
            expanded = jnp.repeat(solved, factor, axis=-1).astype(jnp.float32)
            smoothed = jnp.where(coarsen[cycle_index] == factor, expanded, smoothed)
        cycle_rows.append(smoothed)
    near_axis = jnp.stack(cycle_rows, axis=2)
    return jnp.concatenate([near_axis, tendency[:, :, R_NEAR:, :]], axis=2)
```

```python
import functools
import math

import jax
import jax.numpy as jnp
from jax import lax
from jax.experimental import pallas as pl
from jax.experimental.pallas import tpu as pltpu
from jax.sharding import PartitionSpec as P

GAMMA = 1.4
KAPPA = 1.44
NEAR = 16
FACTORS = (1, 2, 4, 8, 16)
SHIFTS = (1, 2, 4, 8, 16, 32, 64)
MESH = pl.DeviceIdType.MESH
CHUNKS = 4


def filter_constants(total_cells):
    dtheta = 2.0 * math.pi / total_cells
    out = {}
    for f in FACTORS:
        beta = KAPPA / (f * dtheta) ** 2
        half = 0.5 / beta
        gap = math.sqrt(half * (2.0 + half)) - half
        out[f] = (1.0 - gap, math.log1p(-gap), 1.0 / (1.0 + 2.0 * beta * gap))
    return out


def primitive(d, mx, mr, mt, e):
    inv = 1.0 / d
    ux, ur, ut = mx * inv, mr * inv, mt * inv
    p = (GAMMA - 1.0) * (e - 0.5 * (mx * ux + mr * ur + mt * ut))
    return ux, ur, ut, p


def by_factor(fv, values):
    out = jnp.full(fv.shape, values[0], jnp.float32)
    for f, v in zip(FACTORS[1:], values[1:]):
        out = jnp.where(fv == f, jnp.float32(v), out)
    return out


def kernel(
    nsec, nrad, nax,
    coarsen_ref, state_ref, out_ref,
    st, fx, rg, hz, ghost, rad_send, rad_recv, sec_send, sec_recv,
    coef_f, coef_b, near_c, near_a, near_b, car_send, car_keep, car_recv,
    load_sem, ax_ssem, ax_rsem, rad_ssem, rad_rsem, sec_ssem, sec_rsem, car_ssem, car_rsem,
):
    fields, planes, rows, cells = st.shape
    total = cells * nsec
    dtheta = 2.0 * math.pi / total
    tiles = rows // 8
    crow = rows // CHUNKS
    sec, rad, ax = lax.axis_index("sec"), lax.axis_index("rad"), lax.axis_index("ax")
    near = rad == 0

    barrier = pltpu.get_barrier_semaphore()

    def greet(where):
        pl.semaphore_signal(barrier, inc=1, device_id=where, device_id_type=MESH)

    sides = ((ax > 0, {"ax": ax - 1}), (ax < nax - 1, {"ax": ax + 1}))
    rads = ((rad > 0, {"rad": rad - 1}), (rad < nrad - 1, {"rad": rad + 1}))
    others = [{"sec": lax.rem(sec + k, nsec)} for k in range(1, nsec)]
    for cond, where in sides + rads:
        pl.when(cond)(functools.partial(greet, where))
    greet(others[0])
    greet(others[-1])

    @pl.when(near)
    def _():
        for where in others[1:-1]:
            greet(where)

    loads = []
    for c in range(CHUNKS):
        part = pl.ds(c * crow, crow)
        copy = pltpu.make_async_copy(state_ref.at[:, :, part, :], st.at[:, :, part, :], load_sem.at[c])
        copy.start()
        loads.append(copy)

    lane = lax.broadcasted_iota(jnp.int32, (8, 128), 1)
    consts = filter_constants(total)

    def factors():
        row16 = lax.broadcasted_iota(jnp.int32, (NEAR, 128), 0)
        fv = jnp.full((NEAR, 128), 1, jnp.int32)
        for i in range(NEAR):
            fv = jnp.where(row16 == i, coarsen_ref[i], fv)
        return fv

    @pl.when(near)
    def _():
        fv = factors()
        lane16 = lax.broadcasted_iota(jnp.int32, (NEAR, 128), 1)
        for n, d in enumerate(SHIFTS):
            step = by_factor(fv, [math.exp(consts[f][1] * (d // f)) if d >= f else 0.0 for f in FACTORS])
            coef_f[n] = jnp.where(lane16 >= d, step, 0.0)
            coef_b[n] = jnp.where(lane16 < 128 - d, step, 0.0)

    count = 2 + (rad > 0).astype(jnp.int32) + (rad < nrad - 1).astype(jnp.int32)
    count = count + (ax > 0).astype(jnp.int32) + (ax < nax - 1).astype(jnp.int32)
    count = count + jnp.where(near, nsec - 3, 0)
    pl.semaphore_wait(barrier, count)

    def ax_copy(side, c):
        part = pl.ds(c * crow, crow)
        return pltpu.make_async_remote_copy(
            src_ref=state_ref.at[:, (planes - 1) if side == 1 else 0, part, :],
            dst_ref=ghost.at[1 - side, :, part, :],
            send_sem=ax_ssem.at[side, c],
            recv_sem=ax_rsem.at[1 - side, c],
            device_id=sides[side][1],
            device_id_type=MESH,
        )

    for c in range(CHUNKS):
        for side in (0, 1):
            pl.when(sides[side][0])(lambda side=side, c=c: ax_copy(side, c).start())

    for copy in loads:
        copy.wait()

    row8 = lax.broadcasted_iota(jnp.int32, (8, cells), 0)

    def radius(t):
        return (rad * rows + t * 8 + row8).astype(jnp.float32) + 0.5

    def fluxes(t, carry):
        first, last = carry
        part = pl.ds(pl.multiple_of(t * 8, 8), 8)
        padded = pl.ds(pl.multiple_of(t * 8 + 8, 8), 8)
        half_r = 0.5 * radius(t)
        for p in range(planes):
            d, mx, mr, mt, e = [st[k, p, part, :] for k in range(fields)]
            ux, ur, ut, pr = primitive(d, mx, mr, mt, e)
            ep = e + pr
            hx = 0.5 * ux
            for k, v in enumerate((0.5 * mx, mx * hx + 0.5 * pr, mr * hx, mt * hx, ep * hx)):
                fx[k, p, part, :] = v
            gr = half_r * ur
            for k, v in enumerate((half_r * mr, mx * gr, mr * gr + half_r * pr, mt * gr, ep * gr)):
                rg[k, p, padded, :] = v
            s = 0.5 / dtheta
            gt = s * ut
            for k, v in enumerate((s * mt, mx * gt, mr * gt, mt * gt + s * pr, ep * gt)):
                hz[k, p, part, :] = v
                slot = (k * planes + p) * tiles + t
                here = lane == slot
                first = jnp.where(here, pltpu.roll(v[:, :128], slot, 1), first)
                last = jnp.where(here, pltpu.roll(v[:, cells - 128:], slot + 1, 1), last)
        return first, last

    zero = jnp.zeros((8, 128), jnp.float32)
    first, last = lax.fori_loop(0, tiles, fluxes, (zero, zero))
    sec_send[0] = first
    sec_send[1] = last

    def sec_copy(side):
        return pltpu.make_async_remote_copy(
            src_ref=sec_send.at[side],
            dst_ref=sec_recv.at[1 - side],
            send_sem=sec_ssem.at[side],
            recv_sem=sec_rsem.at[1 - side],
            device_id=others[-1] if side == 0 else others[0],
            device_id_type=MESH,
        )

    sec_copy(0).start()
    sec_copy(1).start()

    for k in range(fields):
        for p in range(planes):
            slot = k * planes + p
            rad_send[0, slot:slot + 1, :] = rg[k, p, 8:9, :]
            rad_send[1, slot:slot + 1, :] = rg[k, p, rows + 7:rows + 8, :]

    def rad_copy(side):
        return pltpu.make_async_remote_copy(
            src_ref=rad_send.at[side],
            dst_ref=rad_recv.at[1 - side],
            send_sem=rad_ssem.at[side],
            recv_sem=rad_rsem.at[1 - side],
            device_id=rads[side][1],
            device_id_type=MESH,
        )

    for side in (0, 1):
        pl.when(rads[side][0])(lambda side=side: rad_copy(side).start())

    sec_copy(1).wait_recv()
    sec_copy(0).wait_recv()
    for side in (0, 1):
        edge = 7 if side == 0 else rows + 8

        @pl.when(rads[side][0])
        def _():
            rad_copy(1 - side).wait_recv()
            for k in range(fields):
                for p in range(planes):
                    slot = k * planes + p
                    rg[k, p, edge:edge + 1, :] = rad_recv[side, slot:slot + 1, :]

        @pl.when(jnp.logical_not(rads[side][0]))
        def _():
            for k in range(fields):
                for p in range(planes):
                    rg[k, p, edge:edge + 1, :] = jnp.zeros((1, cells), jnp.float32)

    wide = lax.broadcasted_iota(jnp.int32, (rows, cells), 1)
    before = sec_recv[0]
    after = sec_recv[1]
    place = rad * rows + lax.broadcasted_iota(jnp.int32, (rows, cells), 0)
    inv_r = 1.0 / (place.astype(jnp.float32) + 0.5)

    def edges(packed, slot, to):
        column = [pltpu.roll(packed, (to - slot - t) % 128, 1) for t in range(tiles)]
        column = jnp.concatenate(column, axis=0)
        return jnp.concatenate([column, column], axis=1)

    for p in range(planes):
        for k in range(fields):
            h = hz[k, p]
            slot = (k * planes + p) * tiles
            left = jnp.where(wide == 0, edges(before, slot, 0), pltpu.roll(h, 1, 1))
            right = jnp.where(wide == cells - 1, edges(after, slot, 127), pltpu.roll(h, cells - 1, 1))
            v = left - right
            v = v + (rg[k, p, 7:rows + 7, :] - rg[k, p, 9:rows + 9, :])
            if k == 2:
                v = v + (2.0 * dtheta) * hz[3, p]
            if k == 3:
                v = v - (2.0 * dtheta) * hz[2, p]
            v = v * inv_r
            v = v - fx[k, 1] if p == 0 else v + fx[k, 0]
            out_ref[k, p] = v

    def axial(c):
        for side in (0, 1):
            @pl.when(sides[side][0])
            def _():
                ax_copy(1 - side, c).wait_recv()
                part = pl.ds(c * crow, crow)
                d, mx, mr, mt, e = [ghost[side, k, part, :] for k in range(fields)]
                ux, ur, ut, pr = primitive(d, mx, mr, mt, e)
                s = 0.5 if side == 0 else -0.5
                hx = s * ux
                for k, v in enumerate((s * mx, mx * hx + s * pr, mr * hx, mt * hx, (e + pr) * hx)):
                    out_ref[k, side, part, :] += v

    def car_copy(k):
        return pltpu.make_async_remote_copy(
            src_ref=car_send,
            dst_ref=car_recv.at[k],
            send_sem=car_ssem.at[k],
            recv_sem=car_rsem.at[k],
            device_id=others[k - 1],
            device_id_type=MESH,
        )

    def pack_rates():
        half = by_factor(factors(), [math.exp(consts[f][1] * (128 // f)) for f in FACTORS])
        return jnp.where(lane % 2 == 0, half[0:8], half[8:16])

    npack = fields * planes * 2

    axial(0)

    @pl.when(near)
    def _():
        fv = factors()
        lane3 = lax.broadcasted_iota(jnp.int32, (planes, NEAR, 128), 2)
        fv3 = jnp.broadcast_to(fv[None], (planes, NEAR, 128))
        ends, keeps = zero, zero
        for k in range(fields):
            for half in (0, 1):
                x = out_ref[k, :, 0:NEAR, half * 128:(half + 1) * 128]
                for d in (1, 2, 4, 8):
                    swap = jnp.where((lane3 & d) == 0, pltpu.roll(x, 128 - d, 2), pltpu.roll(x, d, 2))
                    x = jnp.where(fv3 > d, 0.5 * (x + swap), x)
                a, b = x, x
                for n, d in enumerate(SHIFTS):
                    a = a + coef_f[n][None] * pltpu.roll(a, d, 2)
                    b = b + coef_b[n][None] * pltpu.roll(b, 128 - d, 2)
                near_c[half, k] = a + b - x
                for p in range(planes):
                    for rt in (0, 1):
                        u = (k * planes + p) * 2 + rt
                        tail = pltpu.roll(a[p, rt * 8:rt * 8 + 8, :], (u + 1) % 128, 1)
                        head = pltpu.roll(b[p, rt * 8:rt * 8 + 8, :], npack + u, 1)
                        if half == 1:
                            ends = jnp.where(lane == u, tail, ends)
                            keeps = jnp.where(lane == npack + u, head, keeps)
                        else:
                            keeps = jnp.where(lane == u, tail, keeps)
                            ends = jnp.where(lane == npack + u, head, ends)
        car_send[...] = ends + pack_rates() * keeps
        car_keep[...] = keeps
        for k in range(1, nsec):
            car_copy(k).start()

    for c in range(1, CHUNKS):
        axial(c)

    @pl.when(near)
    def _():
        rate = pack_rates()
        sector = rate * rate
        power = [jnp.ones_like(sector)]
        for k in range(nsec):
            power.append(power[-1] * sector)
        forward = lane < npack
        total_in = power[nsec - 1] * car_send[...]
        for k in range(1, nsec):
            car_copy(k).wait_recv()
            total_in = total_in + jnp.where(forward, power[k - 1], power[nsec - 1 - k]) * car_recv[k]
        total_in = total_in / (1.0 - power[nsec])
        inner = car_keep[...] + rate * total_in
        fv = factors()
        inv_f = by_factor(fv, [1.0 / f for f in FACTORS])
        logs = by_factor(fv, [consts[f][1] for f in FACTORS])
        scale = by_factor(fv, [consts[f][2] for f in FACTORS])
        lane16 = lax.broadcasted_iota(jnp.int32, (NEAR, 128), 1).astype(jnp.float32)
        block = jnp.floor(lane16 * inv_f)
        grow = scale * jnp.exp(logs * (block + 1.0))
        fall = scale * jnp.exp(logs * (128.0 * inv_f - block))
        for k in range(fields):
            for p in range(planes):
                for rt in (0, 1):
                    u = (k * planes + p) * 2 + rt
                    part = slice(rt * 8, rt * 8 + 8)
                    for half in (0, 1):
                        src_f, src_b = (total_in, inner) if half == 0 else (inner, total_in)
                        cf = jnp.broadcast_to(src_f[:, u:u + 1], (8, 128))
                        cb = jnp.broadcast_to(src_b[:, npack + u:npack + u + 1], (8, 128))
                        w = scale[part] * near_c[half, k, p, part, :] + grow[part] * cf + fall[part] * cb
                        out_ref[k, p, part, half * 128:(half + 1) * 128] = w

        for k in range(1, nsec):
            car_copy(k).wait_send()

    sec_copy(0).wait_send()
    sec_copy(1).wait_send()
    for side in (0, 1):
        pl.when(rads[side][0])(lambda side=side: rad_copy(side).wait_send())
        for c in range(CHUNKS):
            pl.when(sides[side][0])(lambda side=side, c=c: ax_copy(side, c).wait_send())


def body(state, coarsen):
    fields, planes, rows, cells = state.shape
    nsec, nrad, nax = lax.axis_size("sec"), lax.axis_size("rad"), lax.axis_size("ax")
    block = (fields, planes, rows, cells)
    f32 = jnp.float32
    dma = pltpu.SemaphoreType.DMA
    return pl.pallas_call(
        functools.partial(kernel, nsec, nrad, nax),
        out_shape=jax.ShapeDtypeStruct(block, f32),
        in_specs=[
            pl.BlockSpec(memory_space=pltpu.SMEM),
            pl.BlockSpec(memory_space=pltpu.HBM),
        ],
        out_specs=pl.BlockSpec(memory_space=pltpu.VMEM),
        scratch_shapes=[
            pltpu.VMEM(block, f32),
            pltpu.VMEM(block, f32),
            pltpu.VMEM((fields, planes, rows + 16, cells), f32),
            pltpu.VMEM(block, f32),
            pltpu.VMEM((2, fields, rows, cells), f32),
            pltpu.VMEM((2, fields * planes, cells), f32),
            pltpu.VMEM((2, fields * planes, cells), f32),
            pltpu.VMEM((2, 8, 128), f32),
            pltpu.VMEM((2, 8, 128), f32),
            pltpu.VMEM((len(SHIFTS), NEAR, 128), f32),
            pltpu.VMEM((len(SHIFTS), NEAR, 128), f32),
            pltpu.VMEM((2, fields, planes, NEAR, 128), f32),
            pltpu.VMEM((8, 128), f32),
            pltpu.VMEM((8, 128), f32),
            pltpu.VMEM((8, 128), f32),
            pltpu.VMEM((8, 128), f32),
            pltpu.VMEM((nsec, 8, 128), f32),
            dma((CHUNKS,)),
            dma((2, CHUNKS)),
            dma((2, CHUNKS)),
            dma((2,)),
            dma((2,)),
            dma((2,)),
            dma((2,)),
            dma((nsec,)),
            dma((nsec,)),
        ],
        compiler_params=pltpu.CompilerParams(
            collective_id=0, has_side_effects=True, vmem_limit_bytes=32 * 1024 * 1024
        ),
        cost_estimate=pl.CostEstimate(flops=4_000_000, bytes_accessed=2_000_000, transcendentals=0),
    )(coarsen, state)


def solution(mesh):
    return jax.shard_map(
        body,
        mesh=mesh,
        in_specs=(P(None, "ax", "rad", "sec"), P()),
        out_specs=P(None, "ax", "rad", "sec"),
        check_vma=False,
    )
```

```python
import functools
import math

import jax
import jax.numpy as jnp
from jax import lax
from jax.experimental import pallas as pl
from jax.experimental.pallas import tpu as pltpu
from jax.sharding import PartitionSpec as P

GAMMA = 1.4
KAPPA = 1.44
NEAR = 16
FACTORS = (1, 2, 4, 8, 16)
SHIFTS = (1, 2, 4, 8, 16, 32, 64)
MESH = pl.DeviceIdType.MESH
CHUNKS = 4


def filter_constants(total_cells):
    dtheta = 2.0 * math.pi / total_cells
    out = {}
    for f in FACTORS:
        beta = KAPPA / (f * dtheta) ** 2
        half = 0.5 / beta
        gap = math.sqrt(half * (2.0 + half)) - half
        out[f] = (1.0 - gap, math.log1p(-gap), 1.0 / (1.0 + 2.0 * beta * gap))
    return out


def primitive(d, mx, mr, mt, e):
    inv = 1.0 / d
    ux, ur, ut = mx * inv, mr * inv, mt * inv
    p = (GAMMA - 1.0) * (e - 0.5 * (mx * ux + mr * ur + mt * ut))
    return ux, ur, ut, p


def by_factor(fv, values):
    out = jnp.full(fv.shape, values[0], jnp.float32)
    for f, v in zip(FACTORS[1:], values[1:]):
        out = jnp.where(fv == f, jnp.float32(v), out)
    return out


def kernel(
    nsec, nrad, nax,
    coarsen_ref, state_ref, out_ref,
    st, fx, rg, hz, ghost, rad_send, rad_recv, sec_send, sec_recv,
    coef_f, coef_b, weigh_f, weigh_b, near_c, packet, keep_ref, inbox,
    load_sem, ax_ssem, ax_rsem, rad_ssem, rad_rsem, sec_ssem, sec_rsem, packet_ssem, packet_rsem,
):
    fields, planes, rows, cells = st.shape
    total = cells * nsec
    dtheta = 2.0 * math.pi / total
    tiles = rows // 8
    crow = rows // CHUNKS
    sec, rad, ax = lax.axis_index("sec"), lax.axis_index("rad"), lax.axis_index("ax")
    near = rad == 0

    barrier = pltpu.get_barrier_semaphore()

    def greet(where):
        pl.semaphore_signal(barrier, inc=1, device_id=where, device_id_type=MESH)

    sides = ((ax > 0, {"ax": ax - 1}), (ax < nax - 1, {"ax": ax + 1}))
    rads = ((rad > 0, {"rad": rad - 1}), (rad < nrad - 1, {"rad": rad + 1}))
    others = [{"sec": lax.rem(sec + k, nsec)} for k in range(1, nsec)]
    for cond, where in sides + rads:
        pl.when(cond)(functools.partial(greet, where))
    greet(others[0])
    greet(others[-1])

    @pl.when(near)
    def _():
        for where in others[1:-1]:
            greet(where)
        for cond, where in sides:
            @pl.when(cond)
            def _():
                for other in others:
                    greet({**where, **other})

    loads = []
    for c in range(CHUNKS):
        part = pl.ds(c * crow, crow)
        copy = pltpu.make_async_copy(state_ref.at[:, :, part, :], st.at[:, :, part, :], load_sem.at[c])
        copy.start()
        loads.append(copy)

    lane = lax.broadcasted_iota(jnp.int32, (8, 128), 1)
    consts = filter_constants(total)

    def factors():
        row16 = lax.broadcasted_iota(jnp.int32, (NEAR, 128), 0)
        fv = jnp.full((NEAR, 128), 1, jnp.int32)
        for i in range(NEAR):
            fv = jnp.where(row16 == i, coarsen_ref[i], fv)
        return fv

    @pl.when(near)
    def _():
        fv = factors()
        lane16 = lax.broadcasted_iota(jnp.int32, (NEAR, 128), 1)
        for n, d in enumerate(SHIFTS):
            step = by_factor(fv, [math.exp(consts[f][1] * (d // f)) if d >= f else 0.0 for f in FACTORS])
            coef_f[n] = jnp.where(lane16 >= d, step, 0.0)
            coef_b[n] = jnp.where(lane16 < 128 - d, step, 0.0)
        fw = jnp.concatenate([fv, fv], axis=1)
        share = by_factor(fw, [1.0 / f for f in FACTORS])
        logs = by_factor(fw, [consts[f][1] for f in FACTORS])
        block = lax.broadcasted_iota(jnp.int32, (NEAR, cells), 1).astype(jnp.float32)
        block = jnp.floor(block * share)
        weigh_f[...] = share * jnp.exp(logs * (cells * share - 1.0 - block))
        weigh_b[...] = share * jnp.exp(logs * block)
        for side in (0, 1):
            @pl.when(jnp.logical_not(sides[side][0]))
            def _():
                inbox[2 * side] = jnp.zeros((nsec, 8, 128), jnp.float32)

    for side in (0, 1):
        edge = 7 if side == 0 else rows + 8

        @pl.when(jnp.logical_not(rads[side][0]))
        def _():
            for k in range(fields):
                for p in range(planes):
                    rg[k, p, edge:edge + 1, :] = jnp.zeros((1, cells), jnp.float32)

    for copy in loads:
        copy.wait()

    row8 = lax.broadcasted_iota(jnp.int32, (8, cells), 0)

    def radius(t):
        return (rad * rows + t * 8 + row8).astype(jnp.float32) + 0.5

    def fluxes(t, carry):
        first, last = carry
        part = pl.ds(pl.multiple_of(t * 8, 8), 8)
        padded = pl.ds(pl.multiple_of(t * 8 + 8, 8), 8)
        half_r = 0.5 * radius(t)
        for p in range(planes):
            d, mx, mr, mt, e = [st[k, p, part, :] for k in range(fields)]
            ux, ur, ut, pr = primitive(d, mx, mr, mt, e)
            ep = e + pr
            hx = 0.5 * ux
            for k, v in enumerate((0.5 * mx, mx * hx + 0.5 * pr, mr * hx, mt * hx, ep * hx)):
                fx[k, p, part, :] = v
            gr = half_r * ur
            for k, v in enumerate((half_r * mr, mx * gr, mr * gr + half_r * pr, mt * gr, ep * gr)):
                rg[k, p, padded, :] = v
            s = 0.5 / dtheta
            gt = s * ut
            for k, v in enumerate((s * mt, mx * gt, mr * gt, mt * gt + s * pr, ep * gt)):
                hz[k, p, part, :] = v
                slot = (k * planes + p) * tiles + t
                here = lane == slot
                first = jnp.where(here, pltpu.roll(v[:, :128], slot, 1), first)
                last = jnp.where(here, pltpu.roll(v[:, cells - 128:], slot + 1, 1), last)
        return first, last

    zero = jnp.zeros((8, 128), jnp.float32)
    first, last = lax.fori_loop(0, tiles, fluxes, (zero, zero))
    npack = fields * planes * 2

    def rhs(k, p, size, left, right, inv_r):
        part = slice(0, size)
        v = left - right
        v = v + (rg[k, p, 7:size + 7, :] - rg[k, p, 9:size + 9, :])
        if k == 2:
            v = v + (2.0 * dtheta) * hz[3, p, part, :]
        if k == 3:
            v = v - (2.0 * dtheta) * hz[2, p, part, :]
        v = v * inv_r
        return v - fx[k, 1, part, :] if p == 0 else v + fx[k, 0, part, :]

    def inverse_radius(size):
        place = rad * rows + lax.broadcasted_iota(jnp.int32, (size, cells), 0)
        return 1.0 / (place.astype(jnp.float32) + 0.5)

    @pl.when(near)
    def _():
        wide = lax.broadcasted_iota(jnp.int32, (NEAR, cells), 1)
        inv_r = inverse_radius(NEAR)
        wf, wb = weigh_f[...], weigh_b[...]
        pack = zero

        def put(pack, group, u, column):
            return jnp.where(lane == group * npack + u, jnp.broadcast_to(column, (8, 128)), pack)

        def total(v):
            return jnp.sum(v[:, :128] + v[:, 128:], axis=1, keepdims=True)

        for k in range(fields):
            for p in range(planes):
                h = hz[k, p, 0:NEAR, :]
                left = jnp.where(wide == 0, 0.0, pltpu.roll(h, 1, 1))
                right = jnp.where(wide == cells - 1, 0.0, pltpu.roll(h, cells - 1, 1))
                v = rhs(k, p, NEAR, left, right, inv_r)
                beside = fx[k, 1, 0:NEAR, :] if p == 0 else -fx[k, 0, 0:NEAR, :]
                columns = (
                    total(v * wf), total(v * wb), h[:, cells - 1:], h[:, :1],
                    total(beside * wf), total(beside * wb),
                )
                for rt in (0, 1):
                    u = (k * planes + p) * 2 + rt
                    for group, column in enumerate(columns):
                        pack = put(pack, group, u, column[rt * 8:rt * 8 + 8])
        packet[...] = pack
        inbox[1, 0] = pack

    count = (rad > 0).astype(jnp.int32) + (rad < nrad - 1).astype(jnp.int32)
    beside = (ax > 0).astype(jnp.int32) + (ax < nax - 1).astype(jnp.int32)
    count = count + jnp.where(near, nsec - 1 + nsec * beside, 2 + beside)
    pl.semaphore_wait(barrier, count)

    def packet_copy(to, k):
        where = {"sec": lax.rem(sec + k, nsec), "ax": ax + (to - 1)}
        return pltpu.make_async_remote_copy(
            src_ref=packet,
            dst_ref=inbox.at[2 - to, k],
            send_sem=packet_ssem.at[to, k],
            recv_sem=packet_rsem.at[2 - to, k],
            device_id=where,
            device_id_type=MESH,
        )

    far_first = sorted(range(nsec), key=lambda k: -min(k, nsec - k))

    def packets(act):
        for k in far_first:
            if k:
                act(1, k)
        for side in (0, 1):
            @pl.when(sides[side][0])
            def _():
                for k in far_first:
                    act(2 * side, k)

    @pl.when(near)
    def _():
        packets(lambda to, k: packet_copy(to, k).start())

    sec_send[0] = first
    sec_send[1] = last

    def sec_copy(side):
        return pltpu.make_async_remote_copy(
            src_ref=sec_send.at[side],
            dst_ref=sec_recv.at[1 - side],
            send_sem=sec_ssem.at[side],
            recv_sem=sec_rsem.at[1 - side],
            device_id=others[-1] if side == 0 else others[0],
            device_id_type=MESH,
        )

    sec_copy(0).start()
    sec_copy(1).start()

    for k in range(fields):
        for p in range(planes):
            slot = k * planes + p
            rad_send[0, slot:slot + 1, :] = rg[k, p, 8:9, :]
            rad_send[1, slot:slot + 1, :] = rg[k, p, rows + 7:rows + 8, :]

    def rad_copy(side):
        return pltpu.make_async_remote_copy(
            src_ref=rad_send.at[side],
            dst_ref=rad_recv.at[1 - side],
            send_sem=rad_ssem.at[side],
            recv_sem=rad_rsem.at[1 - side],
            device_id=rads[side][1],
            device_id_type=MESH,
        )

    for side in (0, 1):
        pl.when(rads[side][0])(lambda side=side: rad_copy(side).start())

    def ax_copy(side, c):
        part = pl.ds(c * crow, crow)
        return pltpu.make_async_remote_copy(
            src_ref=state_ref.at[:, (planes - 1) if side == 1 else 0, part, :],
            dst_ref=ghost.at[1 - side, :, part, :],
            send_sem=ax_ssem.at[side, c],
            recv_sem=ax_rsem.at[1 - side, c],
            device_id=sides[side][1],
            device_id_type=MESH,
        )

    for c in range(CHUNKS):
        for side in (0, 1):
            pl.when(sides[side][0])(lambda side=side, c=c: ax_copy(side, c).start())

    sec_copy(1).wait_recv()
    sec_copy(0).wait_recv()
    for side in (0, 1):
        edge = 7 if side == 0 else rows + 8

        @pl.when(rads[side][0])
        def _():
            rad_copy(1 - side).wait_recv()
            for k in range(fields):
                for p in range(planes):
                    slot = k * planes + p
                    rg[k, p, edge:edge + 1, :] = rad_recv[side, slot:slot + 1, :]

    wide = lax.broadcasted_iota(jnp.int32, (rows, cells), 1)
    before = sec_recv[0]
    after = sec_recv[1]
    inv_r = inverse_radius(rows)

    def edges(packed, slot, to):
        column = [pltpu.roll(packed, (to - slot - t) % 128, 1) for t in range(tiles)]
        column = jnp.concatenate(column, axis=0)
        return jnp.concatenate([column, column], axis=1)

    for p in range(planes):
        for k in range(fields):
            h = hz[k, p]
            slot = (k * planes + p) * tiles
            left = jnp.where(wide == 0, edges(before, slot, 0), pltpu.roll(h, 1, 1))
            right = jnp.where(wide == cells - 1, edges(after, slot, 127), pltpu.roll(h, cells - 1, 1))
            out_ref[k, p] = rhs(k, p, rows, left, right, inv_r)

    def axial(c):
        for side in (0, 1):
            @pl.when(sides[side][0])
            def _():
                ax_copy(1 - side, c).wait_recv()
                part = pl.ds(c * crow, crow)
                d, mx, mr, mt, e = [ghost[side, k, part, :] for k in range(fields)]
                ux, ur, ut, pr = primitive(d, mx, mr, mt, e)
                s = 0.5 if side == 0 else -0.5
                hx = s * ux
                for k, v in enumerate((s * mx, mx * hx + s * pr, mr * hx, mt * hx, (e + pr) * hx)):
                    out_ref[k, side, part, :] += v

    axial(0)

    @pl.when(near)
    def _():
        fv = factors()
        lane3 = lax.broadcasted_iota(jnp.int32, (planes, NEAR, 128), 2)
        fv3 = jnp.broadcast_to(fv[None], (planes, NEAR, 128))
        keeps = zero
        for k in range(fields):
            for half in (0, 1):
                x = out_ref[k, :, 0:NEAR, half * 128:(half + 1) * 128]
                for d in (1, 2, 4, 8):
                    swap = jnp.where((lane3 & d) == 0, pltpu.roll(x, 128 - d, 2), pltpu.roll(x, d, 2))
                    x = jnp.where(fv3 > d, 0.5 * (x + swap), x)
                a, b = x, x
                for n, d in enumerate(SHIFTS):
                    a = a + coef_f[n][None] * pltpu.roll(a, d, 2)
                    b = b + coef_b[n][None] * pltpu.roll(b, 128 - d, 2)
                near_c[half, k] = a + b - x
                for p in range(planes):
                    for rt in (0, 1):
                        u = (k * planes + p) * 2 + rt
                        if half == 0:
                            tail = pltpu.roll(a[p, rt * 8:rt * 8 + 8, :], (u + 1) % 128, 1)
                            keeps = jnp.where(lane == u, tail, keeps)
                        else:
                            head = pltpu.roll(b[p, rt * 8:rt * 8 + 8, :], npack + u, 1)
                            keeps = jnp.where(lane == npack + u, head, keeps)
        keep_ref[...] = keeps

    for c in range(1, CHUNKS):
        axial(c)

    @pl.when(near)
    def _():
        fv = factors()
        packed = jnp.where(lane % 2 == 0, fv[0:8], fv[8:16])
        rate = by_factor(packed, [math.exp(consts[f][1] * (128 // f)) for f in FACTORS])

        def by_distance(m):
            logs = [consts[f][1] * (cells // f) for f in FACTORS]
            return by_factor(packed, [math.exp(g * (m - 1)) / -math.expm1(g * nsec) for g in logs])

        ahead = [None] + [by_distance(m) for m in range(1, nsec + 1)]
        back = [None] + [ahead[nsec - m] for m in range(1, nsec)] + [ahead[nsec]]
        row = (lane % 2) * 8 + lax.broadcasted_iota(jnp.int32, (8, 128), 0)
        edge = by_factor(packed, [1.0 / f for f in FACTORS]) / (row.astype(jnp.float32) + 0.5)
        across = edge * by_factor(packed, [math.exp(consts[f][1] * (cells // f - 1)) for f in FACTORS])
        group = lane // npack
        sum_f, sum_b, sum_x = zero, zero, zero
        packets(lambda to, k: packet_copy(2 - to, k).wait_recv())
        for m in range(1, nsec + 1):
            k = m % nsec
            prev, after_m = (m - 1) or nsec, m % nsec + 1
            own = inbox[1, k]
            sum_f += own * jnp.where(group == 0, ahead[m], jnp.where(group == 2, across * ahead[prev], -edge * ahead[after_m]))
            sum_b += own * jnp.where(group == 1, back[m], jnp.where(group == 2, edge * back[prev], -across * back[after_m]))
            both = jnp.where(lane % 4 < 2, inbox[0, k], inbox[2, k])
            sum_x += both * jnp.where(group == 4, ahead[m], back[m])

        def down(v, groups):
            return pltpu.roll(v, 128 - groups * npack, 1)

        sum_f = sum_f + down(sum_f, 2) + down(sum_f, 3)
        sum_b = sum_b + down(sum_b, 1) + down(sum_b, 2)
        total_in = jnp.where(group == 0, sum_f, sum_b) + down(sum_x, 4)
        inner = keep_ref[...] + rate * total_in
        inv_f = by_factor(fv, [1.0 / f for f in FACTORS])
        logs = by_factor(fv, [consts[f][1] for f in FACTORS])
        scale = by_factor(fv, [consts[f][2] for f in FACTORS])
        lane16 = lax.broadcasted_iota(jnp.int32, (NEAR, 128), 1).astype(jnp.float32)
        block = jnp.floor(lane16 * inv_f)
        grow = scale * jnp.exp(logs * (block + 1.0))
        fall = scale * jnp.exp(logs * (128.0 * inv_f - block))
        for k in range(fields):
            for p in range(planes):
                for rt in (0, 1):
                    u = (k * planes + p) * 2 + rt
                    part = slice(rt * 8, rt * 8 + 8)
                    for half in (0, 1):
                        src_f, src_b = (total_in, inner) if half == 0 else (inner, total_in)
                        cf = jnp.broadcast_to(src_f[:, u:u + 1], (8, 128))
                        cb = jnp.broadcast_to(src_b[:, npack + u:npack + u + 1], (8, 128))
                        w = scale[part] * near_c[half, k, p, part, :] + grow[part] * cf + fall[part] * cb
                        out_ref[k, p, part, half * 128:(half + 1) * 128] = w

        packets(lambda to, k: packet_copy(to, k).wait_send())

    sec_copy(0).wait_send()
    sec_copy(1).wait_send()
    for side in (0, 1):
        pl.when(rads[side][0])(lambda side=side: rad_copy(side).wait_send())
        for c in range(CHUNKS):
            pl.when(sides[side][0])(lambda side=side, c=c: ax_copy(side, c).wait_send())


def body(state, coarsen):
    fields, planes, rows, cells = state.shape
    nsec, nrad, nax = lax.axis_size("sec"), lax.axis_size("rad"), lax.axis_size("ax")
    block = (fields, planes, rows, cells)
    f32 = jnp.float32
    dma = pltpu.SemaphoreType.DMA
    return pl.pallas_call(
        functools.partial(kernel, nsec, nrad, nax),
        out_shape=pltpu.VMEM(block, f32),
        in_specs=[
            pl.BlockSpec(memory_space=pltpu.SMEM),
            pl.BlockSpec(memory_space=pltpu.HBM),
        ],
        out_specs=pl.BlockSpec(memory_space=pltpu.VMEM),
        scratch_shapes=[
            pltpu.VMEM(block, f32),
            pltpu.VMEM(block, f32),
            pltpu.VMEM((fields, planes, rows + 16, cells), f32),
            pltpu.VMEM(block, f32),
            pltpu.VMEM((2, fields, rows, cells), f32),
            pltpu.VMEM((2, fields * planes, cells), f32),
            pltpu.VMEM((2, fields * planes, cells), f32),
            pltpu.VMEM((2, 8, 128), f32),
            pltpu.VMEM((2, 8, 128), f32),
            pltpu.VMEM((len(SHIFTS), NEAR, 128), f32),
            pltpu.VMEM((len(SHIFTS), NEAR, 128), f32),
            pltpu.VMEM((NEAR, cells), f32),
            pltpu.VMEM((NEAR, cells), f32),
            pltpu.VMEM((2, fields, planes, NEAR, 128), f32),
            pltpu.VMEM((8, 128), f32),
            pltpu.VMEM((8, 128), f32),
            pltpu.VMEM((3, nsec, 8, 128), f32),
            dma((CHUNKS,)),
            dma((2, CHUNKS)),
            dma((2, CHUNKS)),
            dma((2,)),
            dma((2,)),
            dma((2,)),
            dma((2,)),
            dma((3, nsec)),
            dma((3, nsec)),
        ],
        compiler_params=pltpu.CompilerParams(
            collective_id=0, has_side_effects=True, vmem_limit_bytes=32 * 1024 * 1024
        ),
        cost_estimate=pl.CostEstimate(flops=4_000_000, bytes_accessed=2_000_000, transcendentals=0),
    )(pltpu.with_memory_space_constraint(coarsen, pltpu.HBM), pltpu.with_memory_space_constraint(state, pltpu.HBM))


def solution(mesh):
    return jax.shard_map(
        body,
        mesh=mesh,
        in_specs=(P(None, "ax", "rad", "sec"), P()),
        out_specs=P(None, "ax", "rad", "sec"),
        check_vma=False,
    )
```

```python
import functools
import math

import jax
import jax.numpy as jnp
from jax import lax
from jax.experimental import pallas as pl
from jax.experimental.pallas import tpu as pltpu
from jax.sharding import PartitionSpec as P

GAMMA = 1.4
KAPPA = 1.44
NEAR = 16
FACTORS = (1, 2, 4, 8, 16)
SHIFTS = (1, 2, 4, 8, 16, 32, 64)
MESH = pl.DeviceIdType.MESH
CHUNKS = 4


def filter_constants(total_cells):
    dtheta = 2.0 * math.pi / total_cells
    out = {}
    for f in FACTORS:
        beta = KAPPA / (f * dtheta) ** 2
        half = 0.5 / beta
        gap = math.sqrt(half * (2.0 + half)) - half
        out[f] = (1.0 - gap, math.log1p(-gap), 1.0 / (1.0 + 2.0 * beta * gap))
    return out


def primitive(d, mx, mr, mt, e):
    inv = 1.0 / d
    ux, ur, ut = mx * inv, mr * inv, mt * inv
    p = (GAMMA - 1.0) * (e - 0.5 * (mx * ux + mr * ur + mt * ut))
    return ux, ur, ut, p


def by_factor(fv, values):
    out = jnp.full(fv.shape, values[0], jnp.float32)
    for f, v in zip(FACTORS[1:], values[1:]):
        out = jnp.where(fv == f, jnp.float32(v), out)
    return out


def kernel(
    nsec, nrad, nax,
    coarsen_hbm, state_ref, out_ref,
    coarsen_ref, coarsen_sem, st, fx, rg, hz, ghost, rad_send, rad_recv, sec_send, sec_recv,
    coef_f, coef_b, weigh_f, weigh_b, spread, rate_ref, weights, near_c, packet, keep_ref, inbox,
    load_sem, ax_ssem, ax_rsem, rad_ssem, rad_rsem, sec_ssem, sec_rsem, packet_ssem, packet_rsem,
    ax_ready, rad_ready, sec_ready, packet_ready,
):
    fields, planes, rows, cells = st.shape
    total = cells * nsec
    dtheta = 2.0 * math.pi / total
    tiles = rows // 8
    crow = rows // CHUNKS
    sec, rad, ax = lax.axis_index("sec"), lax.axis_index("rad"), lax.axis_index("ax")
    near = rad == 0

    loads = []
    for c in range(CHUNKS):
        part = pl.ds(c * crow, crow)
        copy = pltpu.make_async_copy(state_ref.at[:, :, part, :], st.at[:, :, part, :], load_sem.at[c])
        copy.start()
        loads.append(copy)

    factor_load = pltpu.make_async_copy(coarsen_hbm, coarsen_ref, coarsen_sem)
    pl.when(near)(factor_load.start)

    def slow(s, r, a):
        return (s == 0) & (r == 0) & (a == 0)

    def rank(s, a):
        turn = jnp.where(s < nsec // 2, s, nsec + nsec // 2 - 1 - s)
        step = jnp.where(a == 0, 3, jnp.where(a == 1, 0, jnp.where(a == 2, 2, 1)))
        return 4 * turn + step + jnp.where(slow(s, rad, a), 1000, 0)

    mine = rank(sec, ax)
    barrier = pltpu.get_barrier_semaphore()

    def signal(sem, where):
        pl.semaphore_signal(sem, inc=1, device_id=where, device_id_type=MESH)

    sides = [
        (there, {"ax": a}, there & (rank(sec, a) < mine), there & (rank(sec, a) > mine), there & slow(sec, rad, a))
        for there, a in ((ax > 0, ax - 1), (ax < nax - 1, ax + 1))
    ]
    rads = [
        (rad > 0, {"rad": rad - 1}, (rad > 0) & ~slow(sec, rad - 1, ax), slow(sec, rad - 1, ax)),
        (rad < nrad - 1, {"rad": rad + 1}, slow(sec, rad, ax), (rad < nrad - 1) & ~slow(sec, rad, ax)),
    ]
    secs = [
        (True, {"sec": s}, rank(s, ax) < mine, rank(s, ax) > mine)
        for s in (lax.rem(sec + nsec - 1, nsec), lax.rem(sec + 1, nsec))
    ]
    far = ~near
    for _, where, _, later, *_ in rads + sides:
        pl.when(later)(functools.partial(signal, barrier, where))
    for _, where, _, later in secs:
        pl.when(far & later)(functools.partial(signal, barrier, where))

    tardy = slow(sec, rad, ax)
    turn = jnp.where(sec < nsec // 2, sec, nsec + nsec // 2 - 1 - sec)
    reach = near & (ax <= 1) & (sec != 0)

    def span(to, earlier):
        if not earlier:
            return jnp.where(tardy, nsec, turn + 1), nsec
        return jnp.where(tardy | (ax + to == 1), 1, 0), jnp.where(tardy, nsec, turn)

    def there(to):
        return near if to == 1 else near & sides[to // 2][0]

    def size(to, earlier):
        lo, hi = span(to, earlier)
        return jnp.where(there(to), jnp.maximum(hi - lo, 0), 0)

    def visit(earlier, act):
        for to in (1, 0, 2):
            def step(t, carry):
                s = jnp.where(t < nsec // 2, t, nsec + nsec // 2 - 1 - t)
                act(to, s, ax + (to - 1))
                return carry

            @pl.when(there(to))
            def _():
                lax.fori_loop(*span(to, earlier), step, 0)

    visit(False, lambda to, s, a: signal(barrier, {"sec": s, "ax": a}))
    pl.when(reach)(lambda: signal(barrier, {"sec": 0, "ax": 0}))

    def number(flags):
        return sum(jnp.where(flag, 1, 0) for flag in flags)

    count = number(v[2] for v in rads + sides)
    count = count + jnp.where(near, sum(size(to, True) for to in range(3)), number(v[2] for v in secs))
    pl.when(count > 0)(lambda: pl.semaphore_wait(barrier, count))

    for ready, pairs in ((ax_ready, sides), (sec_ready, secs), (rad_ready, rads)):
        for side in (0, 1):
            pl.when(pairs[side][2])(functools.partial(signal, ready.at[1 - side], pairs[side][1]))

    visit(True, lambda to, s, a: signal(packet_ready.at[jnp.where(tardy, 1, 0)], {"sec": s, "ax": a}))

    def ax_copy(side, c):
        part = pl.ds(c * crow, crow)
        return pltpu.make_async_remote_copy(
            src_ref=state_ref.at[:, (planes - 1) if side == 1 else 0, part, :],
            dst_ref=ghost.at[1 - side, :, part, :],
            send_sem=ax_ssem.at[side, c],
            recv_sem=ax_rsem.at[1 - side, c],
            device_id=sides[side][1],
            device_id_type=MESH,
        )

    def answered(ready, send):
        pl.semaphore_wait(ready, 1)
        send()

    def send_ax(side, chunks):
        for c in chunks:
            ax_copy(side, c).start()

    head, tail = range(4), range(4, CHUNKS)
    odd = ax % 2
    for side in (0, 1):
        pl.when(sides[side][2] & (odd != side))(functools.partial(send_ax, side, range(CHUNKS)))
        pl.when(sides[side][2] & (odd == side))(functools.partial(send_ax, side, head))
    for side in (0, 1):
        pl.when(sides[side][3] & (odd == side))(
            lambda side=side: answered(ax_ready.at[side], functools.partial(send_ax, side, head))
        )

    lane = lax.broadcasted_iota(jnp.int32, (8, 128), 1)
    consts = filter_constants(total)

    def factors():
        row16 = lax.broadcasted_iota(jnp.int32, (NEAR, 128), 0)
        fv = jnp.full((NEAR, 128), 1, jnp.int32)
        for i in range(NEAR):
            fv = jnp.where(row16 == i, coarsen_ref[i], fv)
        return fv

    @pl.when(near)
    def _():
        factor_load.wait()
        fv = factors()
        lane16 = lax.broadcasted_iota(jnp.int32, (NEAR, 128), 1)
        for n, d in enumerate(SHIFTS):
            step = by_factor(fv, [math.exp(consts[f][1] * (d // f)) if d >= f else 0.0 for f in FACTORS])
            coef_f[n] = jnp.where(lane16 >= d, step, 0.0)
            coef_b[n] = jnp.where(lane16 < 128 - d, step, 0.0)
        fw = jnp.concatenate([fv, fv], axis=1)
        share = by_factor(fw, [1.0 / f for f in FACTORS])
        logs = by_factor(fw, [consts[f][1] for f in FACTORS])
        block = lax.broadcasted_iota(jnp.int32, (NEAR, cells), 1).astype(jnp.float32)
        block = jnp.floor(block * share)
        weigh_f[...] = share * jnp.exp(logs * (cells * share - 1.0 - block))
        weigh_b[...] = share * jnp.exp(logs * block)
        scale = by_factor(fv, [consts[f][2] for f in FACTORS])
        share, logs, block = share[:, :128], logs[:, :128], block[:, :128]
        spread[0] = scale * jnp.exp(logs * (block + 1.0))
        spread[1] = scale * jnp.exp(logs * (128.0 * share - block))
        spread[2] = scale
        packed = jnp.where(lane % 2 == 0, fv[0:8], fv[8:16])
        rate_ref[...] = by_factor(packed, [math.exp(consts[f][1] * (128 // f)) for f in FACTORS])

        def by_distance(m):
            logs = [consts[f][1] * (cells // f) for f in FACTORS]
            return by_factor(packed, [math.exp(g * (m - 1)) / -math.expm1(g * nsec) for g in logs])

        ahead = [None] + [by_distance(m) for m in range(1, nsec + 1)]
        back = [None] + [ahead[nsec - m] for m in range(1, nsec)] + [ahead[nsec]]
        row = (lane % 2) * 8 + lax.broadcasted_iota(jnp.int32, (8, 128), 0)
        edge = by_factor(packed, [1.0 / f for f in FACTORS]) / (row.astype(jnp.float32) + 0.5)
        across = edge * by_factor(packed, [math.exp(consts[f][1] * (cells // f - 1)) for f in FACTORS])
        group = lane // (fields * planes * 2)
        for m in range(1, nsec + 1):
            prev, after_m = (m - 1) or nsec, m % nsec + 1
            k = m % nsec
            weights[0, k] = jnp.where(group == 0, ahead[m], jnp.where(group == 2, across * ahead[prev], -edge * ahead[after_m]))
            weights[1, k] = jnp.where(group == 1, back[m], jnp.where(group == 2, edge * back[prev], -across * back[after_m]))
            weights[2, k] = jnp.where(group == 4, ahead[m], back[m])
        for side in (0, 1):
            @pl.when(jnp.logical_not(sides[side][0]))
            def _():
                inbox[2 * side] = jnp.zeros((nsec, 8, 128), jnp.float32)

    for k in range(fields):
        for p in range(planes):
            for edge in (7, rows + 8):
                rg[k, p, edge:edge + 1, :] = jnp.zeros((1, cells), jnp.float32)

    for copy in loads:
        copy.wait()

    row8 = lax.broadcasted_iota(jnp.int32, (8, cells), 0)

    def radius(t):
        return (rad * rows + t * 8 + row8).astype(jnp.float32) + 0.5

    def fluxes(t, carry):
        first, last = carry
        part = pl.ds(pl.multiple_of(t * 8, 8), 8)
        padded = pl.ds(pl.multiple_of(t * 8 + 8, 8), 8)
        half_r = 0.5 * radius(t)
        for p in range(planes):
            d, mx, mr, mt, e = [st[k, p, part, :] for k in range(fields)]
            ux, ur, ut, pr = primitive(d, mx, mr, mt, e)
            ep = e + pr
            hx = 0.5 * ux
            for k, v in enumerate((0.5 * mx, mx * hx + 0.5 * pr, mr * hx, mt * hx, ep * hx)):
                fx[k, p, part, :] = v
            gr = half_r * ur
            for k, v in enumerate((half_r * mr, mx * gr, mr * gr + half_r * pr, mt * gr, ep * gr)):
                rg[k, p, padded, :] = v
            s = 0.5 / dtheta
            gt = s * ut
            for k, v in enumerate((s * mt, mx * gt, mr * gt, mt * gt + s * pr, ep * gt)):
                hz[k, p, part, :] = v
                slot = (k * planes + p) * tiles + t
                here = lane == slot
                first = jnp.where(here, pltpu.roll(v[:, :128], slot, 1), first)
                last = jnp.where(here, pltpu.roll(v[:, cells - 128:], slot + 1, 1), last)
        return first, last

    zero = jnp.zeros((8, 128), jnp.float32)
    first, last = lax.fori_loop(0, tiles, fluxes, (zero, zero))
    npack = fields * planes * 2

    def rhs(k, p, size, inv_r):
        part = slice(0, size)
        wide = lax.broadcasted_iota(jnp.int32, (size, cells), 1)
        h = hz[k, p, part, :]
        v = jnp.where(wide == 0, 0.0, pltpu.roll(h, 1, 1)) - jnp.where(wide == cells - 1, 0.0, pltpu.roll(h, cells - 1, 1))
        v = v + (rg[k, p, 7:size + 7, :] - rg[k, p, 9:size + 9, :])
        if k == 2:
            v = v + (2.0 * dtheta) * hz[3, p, part, :]
        if k == 3:
            v = v - (2.0 * dtheta) * hz[2, p, part, :]
        v = v * inv_r
        return v - fx[k, 1, part, :] if p == 0 else v + fx[k, 0, part, :]

    def inverse_radius(size):
        place = rad * rows + lax.broadcasted_iota(jnp.int32, (size, cells), 0)
        return 1.0 / (place.astype(jnp.float32) + 0.5)

    @pl.when(near)
    def _():
        inv_r = inverse_radius(NEAR)
        wf, wb = weigh_f[...], weigh_b[...]
        pack = zero

        def put(pack, group, u, column):
            return jnp.where(lane == group * npack + u, jnp.broadcast_to(column, (8, 128)), pack)

        def total(v):
            return jnp.sum(v[:, :128] + v[:, 128:], axis=1, keepdims=True)

        for k in range(fields):
            for p in range(planes):
                h = hz[k, p, 0:NEAR, :]
                v = rhs(k, p, NEAR, inv_r)
                beside = fx[k, 1, 0:NEAR, :] if p == 0 else -fx[k, 0, 0:NEAR, :]
                columns = (
                    total(v * wf), total(v * wb), h[:, cells - 1:], h[:, :1],
                    total(beside * wf), total(beside * wb),
                )
                for rt in (0, 1):
                    u = (k * planes + p) * 2 + rt
                    for group, column in enumerate(columns):
                        pack = put(pack, group, u, column[rt * 8:rt * 8 + 8])
        packet[...] = pack
        inbox[1, 0] = pack

    def packet_copy(to, s, a):
        return pltpu.make_async_remote_copy(
            src_ref=packet,
            dst_ref=inbox.at[2 - to, lax.rem(s - sec + nsec, nsec)],
            send_sem=packet_ssem.at[to],
            recv_sem=packet_rsem.at[2 - to],
            device_id={"sec": s, "ax": a},
            device_id_type=MESH,
        )

    def packet_to(to, s, a):
        packet_copy(to, s, a).start()

    def all_packets(to):
        box = inbox.at[to] if to != 1 else inbox.at[1, pl.ds(1, nsec - 1)]
        return pltpu.make_async_remote_copy(
            src_ref=box,
            dst_ref=box,
            send_sem=packet_ssem.at[to],
            recv_sem=packet_rsem.at[to],
            device_id={"sec": lax.rem(sec + 1, nsec)},
            device_id_type=MESH,
        )

    visit(True, packet_to)
    for side in (0, 1):
        pl.when(near & sides[side][2])(functools.partial(packet_to, 2 * side, sec, ax + 2 * side - 1))

    sec_send[0] = first
    sec_send[1] = last

    def sec_copy(side):
        return pltpu.make_async_remote_copy(
            src_ref=sec_send.at[side],
            dst_ref=sec_recv.at[1 - side],
            send_sem=sec_ssem.at[side],
            recv_sem=sec_rsem.at[1 - side],
            device_id=secs[side][1],
            device_id_type=MESH,
        )


    for k in range(fields):
        for p in range(planes):
            slot = k * planes + p
            rad_send[0, slot:slot + 1, :] = rg[k, p, 8:9, :]
            rad_send[1, slot:slot + 1, :] = rg[k, p, rows + 7:rows + 8, :]

    def rad_copy(side):
        return pltpu.make_async_remote_copy(
            src_ref=rad_send.at[side],
            dst_ref=rad_recv.at[1 - side],
            send_sem=rad_ssem.at[side],
            recv_sem=rad_rsem.at[1 - side],
            device_id=rads[side][1],
            device_id_type=MESH,
        )

    for side in (0, 1):
        pl.when(secs[side][2])(lambda side=side: sec_copy(side).start())
        pl.when(rads[side][2])(lambda side=side: rad_copy(side).start())
    for side in (0, 1):
        pl.when(secs[side][3])(lambda side=side: answered(sec_ready.at[side], sec_copy(side).start))
    for side in (0, 1):
        pl.when(sides[side][0] & (odd == side))(functools.partial(send_ax, side, tail))
    for side in (0, 1):
        pl.when(sides[side][3] & (odd != side) & ~sides[side][4])(
            lambda side=side: answered(ax_ready.at[side], functools.partial(send_ax, side, range(CHUNKS)))
        )

    inv_r = inverse_radius(rows)
    for p in range(planes):
        for k in range(fields):
            out_ref[k, p] = rhs(k, p, rows, inv_r)

    for side in (0, 1):
        pl.when(rads[side][3])(lambda side=side: answered(rad_ready.at[side], rad_copy(side).start))

    @pl.when(near)
    def _():
        for side in (0, 1):
            pl.when(sides[side][3] & ~sides[side][4])(functools.partial(packet_to, 2 * side, sec, ax + 2 * side - 1))
        answers = sum(size(to, False) for to in range(3))
        pl.when(answers > 0)(lambda: pl.semaphore_wait(packet_ready.at[0], answers))

    visit(False, packet_to)

    sec_copy(1).wait_recv()
    sec_copy(0).wait_recv()
    before = sec_recv[0]
    after = sec_recv[1]
    thin = lax.broadcasted_iota(jnp.int32, (rows, 128), 1)

    def edges(packed, slot, to):
        column = [pltpu.roll(packed, (to - slot - t) % 128, 1) for t in range(tiles)]
        return jnp.concatenate(column, axis=0) * inv_r[:, :128]

    for p in range(planes):
        for k in range(fields):
            slot = (k * planes + p) * tiles
            out_ref[k, p, :, :128] += jnp.where(thin == 0, edges(before, slot, 0), 0.0)
            out_ref[k, p, :, cells - 128:] -= jnp.where(thin == 127, edges(after, slot, 127), 0.0)

    def axial(c):
        for side in (0, 1):
            @pl.when(sides[side][0])
            def _():
                ax_copy(1 - side, c).wait_recv()
                part = pl.ds(c * crow, crow)
                d, mx, mr, mt, e = [ghost[side, k, part, :] for k in range(fields)]
                ux, ur, ut, pr = primitive(d, mx, mr, mt, e)
                s = 0.5 if side == 0 else -0.5
                hx = s * ux
                for k, v in enumerate((s * mx, mx * hx + s * pr, mr * hx, mt * hx, (e + pr) * hx)):
                    out_ref[k, side, part, :] += v

    @pl.when(sides[0][4])
    def _():
        answered(ax_ready.at[0], functools.partial(send_ax, 0, range(CHUNKS)))
        packet_to(0, sec, ax - 1)

    axial(0)

    @pl.when(near)
    def _():
        fv = factors()
        lane3 = lax.broadcasted_iota(jnp.int32, (planes, NEAR, 128), 2)
        fv3 = jnp.broadcast_to(fv[None], (planes, NEAR, 128))
        keeps = zero
        scale = spread[2]
        for k in range(fields):
            for half in (0, 1):
                x = out_ref[k, :, 0:NEAR, half * 128:(half + 1) * 128]
                for d in (1, 2, 4, 8):
                    swap = jnp.where((lane3 & d) == 0, pltpu.roll(x, 128 - d, 2), pltpu.roll(x, d, 2))
                    x = jnp.where(fv3 > d, 0.5 * (x + swap), x)
                a, b = x, x
                for n, d in enumerate(SHIFTS):
                    a = a + coef_f[n][None] * pltpu.roll(a, d, 2)
                    b = b + coef_b[n][None] * pltpu.roll(b, 128 - d, 2)
                near_c[half, k] = scale[None] * (a + b - x)
                for p in range(planes):
                    for rt in (0, 1):
                        u = (k * planes + p) * 2 + rt
                        if half == 0:
                            tail = pltpu.roll(a[p, rt * 8:rt * 8 + 8, :], (u + 1) % 128, 1)
                            keeps = jnp.where(lane == u, tail, keeps)
                        else:
                            head = pltpu.roll(b[p, rt * 8:rt * 8 + 8, :], npack + u, 1)
                            keeps = jnp.where(lane == npack + u, head, keeps)
        keep_ref[...] = keeps

        @pl.when(reach)
        def _():
            pl.semaphore_wait(packet_ready.at[1], 1)
            packet_to(jnp.where(ax == 0, 1, 0), 0, 0)

    for c in range(1, CHUNKS):
        axial(c)

    @pl.when(near)
    def _():
        group = lane // npack
        sum_f, sum_b, sum_x = zero, zero, zero
        all_packets(1).wait_recv()
        for side in (0, 1):
            pl.when(sides[side][0])(all_packets(2 * side).wait_recv)
        for m in range(nsec):
            sum_f += inbox[1, m] * weights[0, m]
            sum_b += inbox[1, m] * weights[1, m]
            sum_x += jnp.where(lane % 4 < 2, inbox[0, m], inbox[2, m]) * weights[2, m]

        def down(v, groups):
            return pltpu.roll(v, 128 - groups * npack, 1)

        sum_f = sum_f + down(sum_f, 2) + down(sum_f, 3)
        sum_b = sum_b + down(sum_b, 1) + down(sum_b, 2)
        total_in = jnp.where(group == 0, sum_f, sum_b) + down(sum_x, 4)
        inner = keep_ref[...] + rate_ref[...] * total_in
        for k in range(fields):
            for p in range(planes):
                for rt in (0, 1):
                    u = (k * planes + p) * 2 + rt
                    part = slice(rt * 8, rt * 8 + 8)
                    for half in (0, 1):
                        src_f, src_b = (total_in, inner) if half == 0 else (inner, total_in)
                        cf = jnp.broadcast_to(src_f[:, u:u + 1], (8, 128))
                        cb = jnp.broadcast_to(src_b[:, npack + u:npack + u + 1], (8, 128))
                        w = near_c[half, k, p, part, :] + spread[0, part, :] * cf + spread[1, part, :] * cb
                        out_ref[k, p, part, half * 128:(half + 1) * 128] = w

    for side in (0, 1):
        @pl.when(rads[side][0])
        def _():
            rad_copy(1 - side).wait_recv()
            row = 0 if side == 0 else rows - 1
            sign = 1.0 if side == 0 else -1.0
            for k in range(fields):
                for p in range(planes):
                    slot = k * planes + p
                    out_ref[k, p, row:row + 1, :] += (sign * inv_r[row:row + 1, :]) * rad_recv[side, slot:slot + 1, :]

    @pl.when(near)
    def _():
        all_packets(1).wait_send()
        for side in (0, 1):
            pl.when(sides[side][0])(all_packets(2 * side).wait_send)

    sec_copy(0).wait_send()
    sec_copy(1).wait_send()
    for side in (0, 1):
        pl.when(rads[side][0])(lambda side=side: rad_copy(side).wait_send())
        for c in range(CHUNKS):
            pl.when(sides[side][0])(lambda side=side, c=c: ax_copy(side, c).wait_send())


def body(state, coarsen):
    fields, planes, rows, cells = state.shape
    nsec, nrad, nax = lax.axis_size("sec"), lax.axis_size("rad"), lax.axis_size("ax")
    block = (fields, planes, rows, cells)
    f32 = jnp.float32
    dma = pltpu.SemaphoreType.DMA
    return pl.pallas_call(
        functools.partial(kernel, nsec, nrad, nax),
        out_shape=pltpu.VMEM(block, f32),
        in_specs=[
            pl.BlockSpec(memory_space=pltpu.HBM),
            pl.BlockSpec(memory_space=pltpu.HBM),
        ],
        out_specs=pl.BlockSpec(memory_space=pltpu.VMEM),
        scratch_shapes=[
            pltpu.SMEM((NEAR,), jnp.int32),
            dma(()),
            pltpu.VMEM(block, f32),
            pltpu.VMEM(block, f32),
            pltpu.VMEM((fields, planes, rows + 16, cells), f32),
            pltpu.VMEM(block, f32),
            pltpu.VMEM((2, fields, rows, cells), f32),
            pltpu.VMEM((2, fields * planes, cells), f32),
            pltpu.VMEM((2, fields * planes, cells), f32),
            pltpu.VMEM((2, 8, 128), f32),
            pltpu.VMEM((2, 8, 128), f32),
            pltpu.VMEM((len(SHIFTS), NEAR, 128), f32),
            pltpu.VMEM((len(SHIFTS), NEAR, 128), f32),
            pltpu.VMEM((NEAR, cells), f32),
            pltpu.VMEM((NEAR, cells), f32),
            pltpu.VMEM((3, NEAR, 128), f32),
            pltpu.VMEM((8, 128), f32),
            pltpu.VMEM((3, nsec, 8, 128), f32),
            pltpu.VMEM((2, fields, planes, NEAR, 128), f32),
            pltpu.VMEM((8, 128), f32),
            pltpu.VMEM((8, 128), f32),
            pltpu.VMEM((3, nsec, 8, 128), f32),
            dma((CHUNKS,)),
            dma((2, CHUNKS)),
            dma((2, CHUNKS)),
            dma((2,)),
            dma((2,)),
            dma((2,)),
            dma((2,)),
            dma((3,)),
            dma((3,)),
            pltpu.SemaphoreType.REGULAR((2,)),
            pltpu.SemaphoreType.REGULAR((2,)),
            pltpu.SemaphoreType.REGULAR((2,)),
            pltpu.SemaphoreType.REGULAR((2,)),
        ],
        compiler_params=pltpu.CompilerParams(
            collective_id=0, has_side_effects=True, vmem_limit_bytes=32 * 1024 * 1024
        ),
        cost_estimate=pl.CostEstimate(flops=4_000_000, bytes_accessed=2_000_000, transcendentals=0),
    )(pltpu.with_memory_space_constraint(coarsen, pltpu.HBM), pltpu.with_memory_space_constraint(state, pltpu.HBM))


def solution(mesh):
    return jax.shard_map(
        body,
        mesh=mesh,
        in_specs=(P(None, "ax", "rad", "sec"), P()),
        out_specs=P(None, "ax", "rad", "sec"),
        check_vma=False,
    )
```

```python
import functools
import math

import jax
import jax.numpy as jnp
from jax import lax
from jax.experimental import pallas as pl
from jax.experimental.pallas import tpu as pltpu
from jax.sharding import PartitionSpec as P

GAMMA = 1.4
KAPPA = 1.44
NEAR = 16
FACTORS = (1, 2, 4, 8, 16)
SHIFTS = (1, 2, 4, 8, 16, 32, 64)
MESH = pl.DeviceIdType.MESH
CHUNKS = 4


def filter_constants(total_cells):
    dtheta = 2.0 * math.pi / total_cells
    out = {}
    for f in FACTORS:
        beta = KAPPA / (f * dtheta) ** 2
        half = 0.5 / beta
        gap = math.sqrt(half * (2.0 + half)) - half
        out[f] = (1.0 - gap, math.log1p(-gap), 1.0 / (1.0 + 2.0 * beta * gap))
    return out


def primitive(d, mx, mr, mt, e):
    inv = 1.0 / d
    ux, ur, ut = mx * inv, mr * inv, mt * inv
    p = (GAMMA - 1.0) * (e - 0.5 * (mx * ux + mr * ur + mt * ut))
    return ux, ur, ut, p


def by_factor(fv, values):
    out = jnp.full(fv.shape, values[0], jnp.float32)
    for f, v in zip(FACTORS[1:], values[1:]):
        out = jnp.where(fv == f, jnp.float32(v), out)
    return out


def kernel(
    nsec, nrad, nax,
    coarsen_hbm, state_ref, out_ref,
    coarsen_ref, coarsen_sem, st, fx, rg, hz, ghost, rad_send, rad_recv, sec_send, sec_recv,
    coef_f, coef_b, weigh_f, weigh_b, spread, rate_ref, weights, near_c, packet, keep_ref, inbox,
    load_sem, ax_ssem, ax_rsem, rad_ssem, rad_rsem, sec_ssem, sec_rsem, packet_ssem, packet_rsem,
    ax_ready, rad_ready, sec_ready, packet_ready,
):
    fields, planes, rows, cells = st.shape
    total = cells * nsec
    dtheta = 2.0 * math.pi / total
    tiles = rows // 8
    crow = rows // CHUNKS
    sec, rad, ax = lax.axis_index("sec"), lax.axis_index("rad"), lax.axis_index("ax")
    near = rad == 0

    loads = []
    for c in range(CHUNKS):
        part = pl.ds(c * crow, crow)
        copy = pltpu.make_async_copy(state_ref.at[:, :, part, :], st.at[:, :, part, :], load_sem.at[c])
        copy.start()
        loads.append(copy)

    factor_load = pltpu.make_async_copy(coarsen_hbm, coarsen_ref, coarsen_sem)
    pl.when(near)(factor_load.start)

    def slow(s, r, a):
        return (s == 0) & (r == 0) & (a == 0)

    def rank(s, a):
        turn = jnp.where(s < nsec // 2, s, nsec + nsec // 2 - 1 - s)
        step = jnp.where(a == 0, 3, jnp.where(a == 1, 0, jnp.where(a == 2, 2, 1)))
        return 4 * turn + step + jnp.where(slow(s, rad, a), 1000, 0)

    mine = rank(sec, ax)
    barrier = pltpu.get_barrier_semaphore()

    def signal(sem, where):
        pl.semaphore_signal(sem, inc=1, device_id=where, device_id_type=MESH)

    sides = [
        (there, {"ax": a}, there & (rank(sec, a) < mine), there & (rank(sec, a) > mine), there & slow(sec, rad, a))
        for there, a in ((ax > 0, ax - 1), (ax < nax - 1, ax + 1))
    ]
    rads = [
        (rad > 0, {"rad": rad - 1}, (rad > 0) & ~slow(sec, rad - 1, ax), slow(sec, rad - 1, ax)),
        (rad < nrad - 1, {"rad": rad + 1}, slow(sec, rad, ax), (rad < nrad - 1) & ~slow(sec, rad, ax)),
    ]
    secs = [
        (True, {"sec": s}, rank(s, ax) < mine, rank(s, ax) > mine, slow(s, rad, ax))
        for s in (lax.rem(sec + nsec - 1, nsec), lax.rem(sec + 1, nsec))
    ]
    far = ~near
    for _, where, _, later, *_ in rads + sides:
        pl.when(later)(functools.partial(signal, barrier, where))
    for _, where, _, later, _ in secs:
        pl.when(far & later)(functools.partial(signal, barrier, where))

    tardy = slow(sec, rad, ax)
    turn = jnp.where(sec < nsec // 2, sec, nsec + nsec // 2 - 1 - sec)
    reach = near & (ax <= 1) & (sec != 0)

    def span(to, earlier):
        if not earlier:
            return jnp.where(tardy, nsec, turn + 1), nsec
        return jnp.where(tardy | (ax + to == 1), 1, 0), jnp.where(tardy, nsec, turn)

    def there(to):
        return near if to == 1 else near & sides[to // 2][0]

    def size(to, earlier):
        lo, hi = span(to, earlier)
        return jnp.where(there(to), jnp.maximum(hi - lo, 0), 0)

    def visit(earlier, act):
        for to in (1, 0, 2):
            def step(t, carry):
                s = jnp.where(t < nsec // 2, t, nsec + nsec // 2 - 1 - t)
                act(to, s, ax + (to - 1))
                return carry

            @pl.when(there(to))
            def _():
                lax.fori_loop(*span(to, earlier), step, 0)

    visit(False, lambda to, s, a: signal(barrier, {"sec": s, "ax": a}))
    pl.when(reach)(lambda: signal(barrier, {"sec": 0, "ax": 0}))

    def number(flags):
        return sum(jnp.where(flag, 1, 0) for flag in flags)

    count = number(v[2] for v in rads + sides)
    count = count + jnp.where(near, sum(size(to, True) for to in range(3)), number(v[2] for v in secs))
    pl.when(count > 0)(lambda: pl.semaphore_wait(barrier, count))

    for ready, pairs in ((ax_ready, sides), (sec_ready, secs), (rad_ready, rads)):
        for side in (0, 1):
            pl.when(pairs[side][2])(functools.partial(signal, ready.at[1 - side], pairs[side][1]))

    visit(True, lambda to, s, a: signal(packet_ready.at[jnp.where(tardy, 1, 0)], {"sec": s, "ax": a}))

    def ax_copy(side, c):
        part = pl.ds(c * crow, crow)
        return pltpu.make_async_remote_copy(
            src_ref=state_ref.at[:, (planes - 1) if side == 1 else 0, part, :],
            dst_ref=ghost.at[1 - side, :, part, :],
            send_sem=ax_ssem.at[side, c],
            recv_sem=ax_rsem.at[1 - side, c],
            device_id=sides[side][1],
            device_id_type=MESH,
        )

    def answered(ready, send):
        pl.semaphore_wait(ready, 1)
        send()

    def send_ax(side, chunks):
        for c in chunks:
            ax_copy(side, c).start()

    odd = ax % 2
    for side in (0, 1):
        pl.when(sides[side][2] & (odd != side))(functools.partial(send_ax, side, range(CHUNKS)))
        pl.when(sides[side][2] & (odd == side))(functools.partial(send_ax, side, range(CHUNKS)))
    for side in (0, 1):
        pl.when(sides[side][3] & (odd == side))(
            lambda side=side: answered(ax_ready.at[side], functools.partial(send_ax, side, range(CHUNKS)))
        )

    lane = lax.broadcasted_iota(jnp.int32, (8, 128), 1)
    consts = filter_constants(total)

    def factors():
        row16 = lax.broadcasted_iota(jnp.int32, (NEAR, 128), 0)
        fv = jnp.full((NEAR, 128), 1, jnp.int32)
        for i in range(NEAR):
            fv = jnp.where(row16 == i, coarsen_ref[i], fv)
        return fv

    @pl.when(near)
    def _():
        factor_load.wait()
        fv = factors()
        lane16 = lax.broadcasted_iota(jnp.int32, (NEAR, 128), 1)
        for n, d in enumerate(SHIFTS):
            step = by_factor(fv, [math.exp(consts[f][1] * (d // f)) if d >= f else 0.0 for f in FACTORS])
            coef_f[n] = jnp.where(lane16 >= d, step, 0.0)
            coef_b[n] = jnp.where(lane16 < 128 - d, step, 0.0)
        fw = jnp.concatenate([fv, fv], axis=1)
        share = by_factor(fw, [1.0 / f for f in FACTORS])
        logs = by_factor(fw, [consts[f][1] for f in FACTORS])
        block = lax.broadcasted_iota(jnp.int32, (NEAR, cells), 1).astype(jnp.float32)
        block = jnp.floor(block * share)
        weigh_f[...] = share * jnp.exp(logs * (cells * share - 1.0 - block))
        weigh_b[...] = share * jnp.exp(logs * block)
        scale = by_factor(fv, [consts[f][2] for f in FACTORS])
        share, logs, block = share[:, :128], logs[:, :128], block[:, :128]
        spread[0] = scale * jnp.exp(logs * (block + 1.0))
        spread[1] = scale * jnp.exp(logs * (128.0 * share - block))
        spread[2] = scale
        packed = jnp.where(lane % 2 == 0, fv[0:8], fv[8:16])
        rate_ref[...] = by_factor(packed, [math.exp(consts[f][1] * (128 // f)) for f in FACTORS])

        def by_distance(m):
            logs = [consts[f][1] * (cells // f) for f in FACTORS]
            return by_factor(packed, [math.exp(g * (m - 1)) / -math.expm1(g * nsec) for g in logs])

        ahead = [None] + [by_distance(m) for m in range(1, nsec + 1)]
        back = [None] + [ahead[nsec - m] for m in range(1, nsec)] + [ahead[nsec]]
        row = (lane % 2) * 8 + lax.broadcasted_iota(jnp.int32, (8, 128), 0)
        edge = by_factor(packed, [1.0 / f for f in FACTORS]) / (row.astype(jnp.float32) + 0.5)
        across = edge * by_factor(packed, [math.exp(consts[f][1] * (cells // f - 1)) for f in FACTORS])
        group = lane // (fields * planes * 2)
        direct = edge * by_factor(packed, [math.exp(-consts[f][1]) for f in FACTORS])
        for m in range(1, nsec + 1):
            prev, after_m = (m - 1) or nsec, m % nsec + 1
            k = m % nsec
            from_last, from_first = across * ahead[prev], -edge * ahead[after_m]
            to_last, to_first = edge * back[prev], -across * back[after_m]
            if m == 1:
                from_last = from_last + direct
            if m == nsec - 1:
                to_first = to_first - direct
            weights[0, k] = jnp.where(group == 0, ahead[m], jnp.where(group == 2, from_last, from_first))
            weights[1, k] = jnp.where(group == 1, back[m], jnp.where(group == 2, to_last, to_first))
            weights[2, k] = jnp.where(group == 4, ahead[m], back[m])
        for side in (0, 1):
            @pl.when(jnp.logical_not(sides[side][0]))
            def _():
                inbox[2 * side] = jnp.zeros((nsec, 8, 128), jnp.float32)

    for k in range(fields):
        for p in range(planes):
            for edge in (7, rows + 8):
                rg[k, p, edge:edge + 1, :] = jnp.zeros((1, cells), jnp.float32)

    for copy in loads:
        copy.wait()

    row8 = lax.broadcasted_iota(jnp.int32, (8, cells), 0)

    def radius(t):
        return (rad * rows + t * 8 + row8).astype(jnp.float32) + 0.5

    def fluxes(t, carry):
        first, last = carry
        part = pl.ds(pl.multiple_of(t * 8, 8), 8)
        padded = pl.ds(pl.multiple_of(t * 8 + 8, 8), 8)
        half_r = 0.5 * radius(t)
        for p in range(planes):
            d, mx, mr, mt, e = [st[k, p, part, :] for k in range(fields)]
            ux, ur, ut, pr = primitive(d, mx, mr, mt, e)
            ep = e + pr
            hx = 0.5 * ux
            for k, v in enumerate((0.5 * mx, mx * hx + 0.5 * pr, mr * hx, mt * hx, ep * hx)):
                fx[k, p, part, :] = v
            gr = half_r * ur
            for k, v in enumerate((half_r * mr, mx * gr, mr * gr + half_r * pr, mt * gr, ep * gr)):
                rg[k, p, padded, :] = v
            s = 0.5 / dtheta
            gt = s * ut
            for k, v in enumerate((s * mt, mx * gt, mr * gt, mt * gt + s * pr, ep * gt)):
                hz[k, p, part, :] = v
                slot = (k * planes + p) * tiles + t
                here = lane == slot
                first = jnp.where(here, pltpu.roll(v[:, :128], slot, 1), first)
                last = jnp.where(here, pltpu.roll(v[:, cells - 128:], slot + 1, 1), last)
        return first, last

    zero = jnp.zeros((8, 128), jnp.float32)
    first, last = lax.fori_loop(0, tiles, fluxes, (zero, zero))
    npack = fields * planes * 2

    def rhs(k, p, size, inv_r):
        part = slice(0, size)
        wide = lax.broadcasted_iota(jnp.int32, (size, cells), 1)
        h = hz[k, p, part, :]
        v = jnp.where(wide == 0, 0.0, pltpu.roll(h, 1, 1)) - jnp.where(wide == cells - 1, 0.0, pltpu.roll(h, cells - 1, 1))
        v = v + (rg[k, p, 7:size + 7, :] - rg[k, p, 9:size + 9, :])
        if k == 2:
            v = v + (2.0 * dtheta) * hz[3, p, part, :]
        if k == 3:
            v = v - (2.0 * dtheta) * hz[2, p, part, :]
        v = v * inv_r
        return v - fx[k, 1, part, :] if p == 0 else v + fx[k, 0, part, :]

    def inverse_radius(size):
        place = rad * rows + lax.broadcasted_iota(jnp.int32, (size, cells), 0)
        return 1.0 / (place.astype(jnp.float32) + 0.5)

    sec_send[0] = first
    sec_send[1] = last

    def sec_copy(side):
        return pltpu.make_async_remote_copy(
            src_ref=sec_send.at[side],
            dst_ref=sec_recv.at[1 - side],
            send_sem=sec_ssem.at[side],
            recv_sem=sec_rsem.at[1 - side],
            device_id=secs[side][1],
            device_id_type=MESH,
        )


    for k in range(fields):
        for p in range(planes):
            slot = k * planes + p
            rad_send[0, slot:slot + 1, :] = rg[k, p, 8:9, :]
            rad_send[1, slot:slot + 1, :] = rg[k, p, rows + 7:rows + 8, :]

    def rad_copy(side):
        return pltpu.make_async_remote_copy(
            src_ref=rad_send.at[side],
            dst_ref=rad_recv.at[1 - side],
            send_sem=rad_ssem.at[side],
            recv_sem=rad_rsem.at[1 - side],
            device_id=rads[side][1],
            device_id_type=MESH,
        )

    for side in (0, 1):
        pl.when(secs[side][2])(lambda side=side: sec_copy(side).start())
        pl.when(rads[side][2])(lambda side=side: rad_copy(side).start())
    @pl.when(near)
    def _():
        inv_r = inverse_radius(NEAR)
        wf, wb = weigh_f[...], weigh_b[...]
        pack = zero
        terms = {}

        def halves(v):
            return v[:, :128] + v[:, 128:]

        for k in range(fields):
            for p in range(planes):
                h = hz[k, p, 0:NEAR, :]
                v = rhs(k, p, NEAR, inv_r)
                beside = fx[k, 1, 0:NEAR, :] if p == 0 else -fx[k, 0, 0:NEAR, :]
                sums = {0: halves(v * wf), 1: halves(v * wb), 4: halves(beside * wf), 5: halves(beside * wb)}
                for rt in (0, 1):
                    u = (k * planes + p) * 2 + rt
                    part = slice(rt * 8, rt * 8 + 8)
                    for group, v_sum in sums.items():
                        terms[group * npack + u] = v_sum[part]
                    at = 2 * npack + u
                    pack = jnp.where(lane == at, pltpu.roll(h[part, cells - 128:], at + 1, 1), pack)
                    at = 3 * npack + u
                    pack = jnp.where(lane == at, pltpu.roll(h[part, :128], at, 1), pack)
        width = 1
        while width < 128:
            high = (lane & width) != 0
            merged = {}
            for i in range(64 // width):
                x, y = terms.get(2 * i), terms.get(2 * i + 1)
                if x is not None and y is not None:
                    merged[i] = jnp.where(high, y, x) + pltpu.roll(jnp.where(high, x, y), width, 1)
                elif x is not None or y is not None:
                    x = y if x is None else x
                    merged[i] = x + pltpu.roll(x, width, 1)
            terms, width = merged, width * 2
        middle = (lane >= 2 * npack) & (lane < 4 * npack)
        pack = jnp.where(middle, pack, terms[0])
        packet[...] = pack
        inbox[1, 0] = pack

    def packet_copy(to, s, a):
        return pltpu.make_async_remote_copy(
            src_ref=packet,
            dst_ref=inbox.at[2 - to, lax.rem(s - sec + nsec, nsec)],
            send_sem=packet_ssem.at[to],
            recv_sem=packet_rsem.at[2 - to],
            device_id={"sec": s, "ax": a},
            device_id_type=MESH,
        )

    def packet_to(to, s, a):
        packet_copy(to, s, a).start()

    def all_packets(to):
        box = inbox.at[to] if to != 1 else inbox.at[1, pl.ds(1, nsec - 1)]
        return pltpu.make_async_remote_copy(
            src_ref=box,
            dst_ref=box,
            send_sem=packet_ssem.at[to],
            recv_sem=packet_rsem.at[to],
            device_id={"sec": lax.rem(sec + 1, nsec)},
            device_id_type=MESH,
        )

    visit(True, packet_to)
    for side in (0, 1):
        pl.when(near & sides[side][2])(functools.partial(packet_to, 2 * side, sec, ax + 2 * side - 1))

    for side in (0, 1):
        pl.when(sides[side][3] & (odd != side) & ~sides[side][4])(
            lambda side=side: answered(ax_ready.at[side], functools.partial(send_ax, side, range(CHUNKS)))
        )
    for side in (0, 1):
        pl.when(secs[side][3] & ~secs[side][4])(lambda side=side: answered(sec_ready.at[side], sec_copy(side).start))

    inv_r = inverse_radius(rows)
    for p in range(planes):
        for k in range(fields):
            out_ref[k, p] = rhs(k, p, rows, inv_r)

    pl.when(rads[1][3])(lambda: answered(rad_ready.at[1], rad_copy(1).start))

    @pl.when(near)
    def _():
        for side in (0, 1):
            pl.when(sides[side][3] & ~sides[side][4])(functools.partial(packet_to, 2 * side, sec, ax + 2 * side - 1))
        answers = sum(size(to, False) for to in range(3))
        pl.when(answers > 0)(lambda: pl.semaphore_wait(packet_ready.at[0], answers))

    visit(False, packet_to)

    @pl.when(sides[0][4])
    def _():
        answered(ax_ready.at[0], functools.partial(send_ax, 0, range(CHUNKS)))
        packet_to(0, sec, ax - 1)

    @pl.when(reach)
    def _():
        pl.semaphore_wait(packet_ready.at[1], 1)
        packet_to(jnp.where(ax == 0, 1, 0), 0, 0)

    for side in (0, 1):
        pl.when(secs[side][4])(lambda side=side: answered(sec_ready.at[side], sec_copy(side).start))

    def axial(c):
        for side in (0, 1):
            @pl.when(sides[side][0])
            def _():
                ax_copy(1 - side, c).wait_recv()
                part = pl.ds(c * crow, crow)
                d, mx, mr, mt, e = [ghost[side, k, part, :] for k in range(fields)]
                ux, ur, ut, pr = primitive(d, mx, mr, mt, e)
                s = 0.5 if side == 0 else -0.5
                hx = s * ux
                for k, v in enumerate((s * mx, mx * hx + s * pr, mr * hx, mt * hx, (e + pr) * hx)):
                    out_ref[k, side, part, :] += v

    axial(0)

    @pl.when(near)
    def _():
        fv = factors()
        lane3 = lax.broadcasted_iota(jnp.int32, (planes, NEAR, 128), 2)
        fv3 = jnp.broadcast_to(fv[None], (planes, NEAR, 128))
        keeps = zero
        scale = spread[2]
        for k in range(fields):
            for half in (0, 1):
                x = out_ref[k, :, 0:NEAR, half * 128:(half + 1) * 128]
                for d in (1, 2, 4, 8):
                    swap = jnp.where((lane3 & d) == 0, pltpu.roll(x, 128 - d, 2), pltpu.roll(x, d, 2))
                    x = jnp.where(fv3 > d, 0.5 * (x + swap), x)
                a, b = x, x
                for n, d in enumerate(SHIFTS):
                    a = a + coef_f[n][None] * pltpu.roll(a, d, 2)
                    b = b + coef_b[n][None] * pltpu.roll(b, 128 - d, 2)
                near_c[half, k] = scale[None] * (a + b - x)
                for p in range(planes):
                    for rt in (0, 1):
                        u = (k * planes + p) * 2 + rt
                        if half == 0:
                            tail = pltpu.roll(a[p, rt * 8:rt * 8 + 8, :], (u + 1) % 128, 1)
                            keeps = jnp.where(lane == u, tail, keeps)
                        else:
                            head = pltpu.roll(b[p, rt * 8:rt * 8 + 8, :], npack + u, 1)
                            keeps = jnp.where(lane == npack + u, head, keeps)
        keep_ref[...] = keeps

    sec_copy(1).wait_recv()
    sec_copy(0).wait_recv()
    before = sec_recv[0]
    after = sec_recv[1]
    thin = lax.broadcasted_iota(jnp.int32, (rows, 128), 1)

    def edges(packed, slot, to):
        column = [pltpu.roll(packed, (to - slot - t) % 128, 1) for t in range(tiles)]
        return jnp.concatenate(column, axis=0) * inv_r[:, :128]

    for p in range(planes):
        for k in range(fields):
            slot = (k * planes + p) * tiles
            out_ref[k, p, :, :128] += jnp.where(thin == 0, edges(before, slot, 0), 0.0)
            out_ref[k, p, :, cells - 128:] -= jnp.where(thin == 127, edges(after, slot, 127), 0.0)

    for c in range(1, CHUNKS):
        axial(c)

    @pl.when(near)
    def _():
        group = lane // npack
        sum_f, sum_b, sum_x = zero, zero, zero
        all_packets(1).wait_recv()
        for side in (0, 1):
            pl.when(sides[side][0])(all_packets(2 * side).wait_recv)
        for m in range(nsec):
            sum_f += inbox[1, m] * weights[0, m]
            sum_b += inbox[1, m] * weights[1, m]
            sum_x += jnp.where(lane % 4 < 2, inbox[0, m], inbox[2, m]) * weights[2, m]

        def down(v, groups):
            return pltpu.roll(v, 128 - groups * npack, 1)

        sum_f = sum_f + down(sum_f, 2) + down(sum_f, 3)
        sum_b = sum_b + down(sum_b, 1) + down(sum_b, 2)
        total_in = jnp.where(group == 0, sum_f, sum_b) + down(sum_x, 4)
        inner = keep_ref[...] + rate_ref[...] * total_in
        for k in range(fields):
            for p in range(planes):
                for rt in (0, 1):
                    u = (k * planes + p) * 2 + rt
                    part = slice(rt * 8, rt * 8 + 8)
                    for half in (0, 1):
                        src_f, src_b = (total_in, inner) if half == 0 else (inner, total_in)
                        cf = jnp.broadcast_to(src_f[:, u:u + 1], (8, 128))
                        cb = jnp.broadcast_to(src_b[:, npack + u:npack + u + 1], (8, 128))
                        w = near_c[half, k, p, part, :] + spread[0, part, :] * cf + spread[1, part, :] * cb
                        out_ref[k, p, part, half * 128:(half + 1) * 128] = w

    pl.when(rads[0][3])(lambda: answered(rad_ready.at[0], rad_copy(0).start))
    for side in (0, 1):
        @pl.when(rads[side][0])
        def _():
            rad_copy(1 - side).wait_recv()
            row = 0 if side == 0 else rows - 1
            sign = 1.0 if side == 0 else -1.0
            for k in range(fields):
                for p in range(planes):
                    slot = k * planes + p
                    out_ref[k, p, row:row + 1, :] += (sign * inv_r[row:row + 1, :]) * rad_recv[side, slot:slot + 1, :]

    @pl.when(near)
    def _():
        all_packets(1).wait_send()
        for side in (0, 1):
            pl.when(sides[side][0])(all_packets(2 * side).wait_send)

    sec_copy(0).wait_send()
    sec_copy(1).wait_send()
    for side in (0, 1):
        pl.when(rads[side][0])(lambda side=side: rad_copy(side).wait_send())
        for c in range(CHUNKS):
            pl.when(sides[side][0])(lambda side=side, c=c: ax_copy(side, c).wait_send())


def body(state, coarsen):
    fields, planes, rows, cells = state.shape
    nsec, nrad, nax = lax.axis_size("sec"), lax.axis_size("rad"), lax.axis_size("ax")
    block = (fields, planes, rows, cells)
    f32 = jnp.float32
    dma = pltpu.SemaphoreType.DMA
    return pl.pallas_call(
        functools.partial(kernel, nsec, nrad, nax),
        out_shape=pltpu.VMEM(block, f32),
        in_specs=[
            pl.BlockSpec(memory_space=pltpu.HBM),
            pl.BlockSpec(memory_space=pltpu.HBM),
        ],
        out_specs=pl.BlockSpec(memory_space=pltpu.VMEM),
        scratch_shapes=[
            pltpu.SMEM((NEAR,), jnp.int32),
            dma(()),
            pltpu.VMEM(block, f32),
            pltpu.VMEM(block, f32),
            pltpu.VMEM((fields, planes, rows + 16, cells), f32),
            pltpu.VMEM(block, f32),
            pltpu.VMEM((2, fields, rows, cells), f32),
            pltpu.VMEM((2, fields * planes, cells), f32),
            pltpu.VMEM((2, fields * planes, cells), f32),
            pltpu.VMEM((2, 8, 128), f32),
            pltpu.VMEM((2, 8, 128), f32),
            pltpu.VMEM((len(SHIFTS), NEAR, 128), f32),
            pltpu.VMEM((len(SHIFTS), NEAR, 128), f32),
            pltpu.VMEM((NEAR, cells), f32),
            pltpu.VMEM((NEAR, cells), f32),
            pltpu.VMEM((3, NEAR, 128), f32),
            pltpu.VMEM((8, 128), f32),
            pltpu.VMEM((3, nsec, 8, 128), f32),
            pltpu.VMEM((2, fields, planes, NEAR, 128), f32),
            pltpu.VMEM((8, 128), f32),
            pltpu.VMEM((8, 128), f32),
            pltpu.VMEM((3, nsec, 8, 128), f32),
            dma((CHUNKS,)),
            dma((2, CHUNKS)),
            dma((2, CHUNKS)),
            dma((2,)),
            dma((2,)),
            dma((2,)),
            dma((2,)),
            dma((3,)),
            dma((3,)),
            pltpu.SemaphoreType.REGULAR((2,)),
            pltpu.SemaphoreType.REGULAR((2,)),
            pltpu.SemaphoreType.REGULAR((2,)),
            pltpu.SemaphoreType.REGULAR((2,)),
        ],
        compiler_params=pltpu.CompilerParams(
            collective_id=0, has_side_effects=True, vmem_limit_bytes=32 * 1024 * 1024
        ),
        cost_estimate=pl.CostEstimate(flops=4_000_000, bytes_accessed=2_000_000, transcendentals=0),
    )(pltpu.with_memory_space_constraint(coarsen, pltpu.HBM), pltpu.with_memory_space_constraint(state, pltpu.HBM))


def solution(mesh):
    return jax.shard_map(
        body,
        mesh=mesh,
        in_specs=(P(None, "ax", "rad", "sec"), P()),
        out_specs=P(None, "ax", "rad", "sec"),
        check_vma=False,
    )
```

```python
import functools
import math

import jax
import jax.numpy as jnp
from jax import lax
from jax.experimental import pallas as pl
from jax.experimental.pallas import tpu as pltpu
from jax.sharding import PartitionSpec as P

GAMMA = 1.4
KAPPA = 1.44
NEAR = 16
FACTORS = (1, 2, 4, 8, 16)
SHIFTS = (1, 2, 4, 8, 16, 32, 64)
MESH = pl.DeviceIdType.MESH
CHUNKS = 4


def filter_constants(total_cells):
    dtheta = 2.0 * math.pi / total_cells
    out = {}
    for f in FACTORS:
        beta = KAPPA / (f * dtheta) ** 2
        half = 0.5 / beta
        gap = math.sqrt(half * (2.0 + half)) - half
        out[f] = (1.0 - gap, math.log1p(-gap), 1.0 / (1.0 + 2.0 * beta * gap))
    return out


def primitive(d, mx, mr, mt, e):
    inv = 1.0 / d
    ux, ur, ut = mx * inv, mr * inv, mt * inv
    p = (GAMMA - 1.0) * (e - 0.5 * (mx * ux + mr * ur + mt * ut))
    return ux, ur, ut, p


def by_factor(fv, values):
    out = jnp.full(fv.shape, values[0], jnp.float32)
    for f, v in zip(FACTORS[1:], values[1:]):
        out = jnp.where(fv == f, jnp.float32(v), out)
    return out


def kernel(
    nsec, nrad, nax,
    coarsen_hbm, state_ref, out_ref,
    coarsen_ref, coarsen_sem, st, fx, rg, hz, ghost, rad_send, rad_recv, sec_send, sec_recv,
    coef_f, coef_b, weigh_f, weigh_b, spread, rate_ref, weights, near_c, packet, keep_ref, inbox,
    load_sem, ax_ssem, ax_rsem, rad_ssem, rad_rsem, sec_ssem, sec_rsem, packet_ssem, packet_rsem,
    ax_ready, rad_ready, sec_ready, packet_ready,
):
    fields, planes, rows, cells = st.shape
    total = cells * nsec
    dtheta = 2.0 * math.pi / total
    tiles = rows // 8
    crow = rows // CHUNKS
    sec, rad, ax = lax.axis_index("sec"), lax.axis_index("rad"), lax.axis_index("ax")
    near = rad == 0

    loads = []
    for c in range(CHUNKS):
        part = pl.ds(c * crow, crow)
        copy = pltpu.make_async_copy(state_ref.at[:, :, part, :], st.at[:, :, part, :], load_sem.at[c])
        copy.start()
        loads.append(copy)

    factor_load = pltpu.make_async_copy(coarsen_hbm, coarsen_ref, coarsen_sem)
    pl.when(near)(factor_load.start)

    def slow(s, r, a):
        return (s == 0) & (r == 0) & (a == 0)

    def rank(s, a):
        turn = jnp.where(s < nsec // 2, s, nsec + nsec // 2 - 1 - s)
        step = jnp.where(a == 0, 3, jnp.where(a == 1, 0, jnp.where(a == 2, 2, 1)))
        return 4 * turn + step + jnp.where(slow(s, rad, a), 1000, 0)

    mine = rank(sec, ax)
    barrier = pltpu.get_barrier_semaphore()

    def signal(sem, where):
        pl.semaphore_signal(sem, inc=1, device_id=where, device_id_type=MESH)

    sides = [
        (there, {"ax": a}, there & (rank(sec, a) < mine), there & (rank(sec, a) > mine), there & slow(sec, rad, a))
        for there, a in ((ax > 0, ax - 1), (ax < nax - 1, ax + 1))
    ]
    rads = [
        (rad > 0, {"rad": rad - 1}, (rad > 0) & ~slow(sec, rad - 1, ax), slow(sec, rad - 1, ax)),
        (rad < nrad - 1, {"rad": rad + 1}, slow(sec, rad, ax), (rad < nrad - 1) & ~slow(sec, rad, ax)),
    ]
    secs = [
        (True, {"sec": s}, rank(s, ax) < mine, rank(s, ax) > mine, slow(s, rad, ax))
        for s in (lax.rem(sec + nsec - 1, nsec), lax.rem(sec + 1, nsec))
    ]
    far = ~near
    for _, where, _, later, *_ in rads + sides:
        pl.when(later)(functools.partial(signal, barrier, where))
    for _, where, _, later, _ in secs:
        pl.when(far & later)(functools.partial(signal, barrier, where))

    tardy = slow(sec, rad, ax)
    turn = jnp.where(sec < nsec // 2, sec, nsec + nsec // 2 - 1 - sec)
    reach = near & (ax <= 1) & (sec != 0)

    def span(to, earlier):
        if not earlier:
            return jnp.where(tardy, nsec, turn + 1), nsec
        return jnp.where(tardy | (ax + to == 1), 1, 0), jnp.where(tardy, nsec, turn)

    def there(to):
        return near if to == 1 else near & sides[to // 2][0]

    def size(to, earlier):
        lo, hi = span(to, earlier)
        return jnp.where(there(to), jnp.maximum(hi - lo, 0), 0)

    def visit(earlier, act):
        for to in (1, 0, 2):
            def step(t, carry):
                s = jnp.where(t < nsec // 2, t, nsec + nsec // 2 - 1 - t)
                act(to, s, ax + (to - 1))
                return carry

            @pl.when(there(to))
            def _():
                lax.fori_loop(*span(to, earlier), step, 0)

    visit(False, lambda to, s, a: signal(barrier, {"sec": s, "ax": a}))
    pl.when(reach)(lambda: signal(barrier, {"sec": 0, "ax": 0}))

    lane = lax.broadcasted_iota(jnp.int32, (8, 128), 1)
    consts = filter_constants(total)

    def factors():
        row16 = lax.broadcasted_iota(jnp.int32, (NEAR, 128), 0)
        fv = jnp.full((NEAR, 128), 1, jnp.int32)
        for i in range(NEAR):
            fv = jnp.where(row16 == i, coarsen_ref[i], fv)
        return fv

    @pl.when(near)
    def _():
        factor_load.wait()
        fv = factors()
        lane16 = lax.broadcasted_iota(jnp.int32, (NEAR, 128), 1)
        for n, d in enumerate(SHIFTS):
            step = by_factor(fv, [math.exp(consts[f][1] * (d // f)) if d >= f else 0.0 for f in FACTORS])
            coef_f[n] = jnp.where(lane16 >= d, step, 0.0)
            coef_b[n] = jnp.where(lane16 < 128 - d, step, 0.0)
        fw = jnp.concatenate([fv, fv], axis=1)
        share = by_factor(fw, [1.0 / f for f in FACTORS])
        logs = by_factor(fw, [consts[f][1] for f in FACTORS])
        block = lax.broadcasted_iota(jnp.int32, (NEAR, cells), 1).astype(jnp.float32)
        block = jnp.floor(block * share)
        weigh_f[...] = share * jnp.exp(logs * (cells * share - 1.0 - block))
        weigh_b[...] = share * jnp.exp(logs * block)
        scale = by_factor(fv, [consts[f][2] for f in FACTORS])
        share, logs, block = share[:, :128], logs[:, :128], block[:, :128]
        spread[0] = scale * jnp.exp(logs * (block + 1.0))
        spread[1] = scale * jnp.exp(logs * (128.0 * share - block))
        spread[2] = scale
        packed = jnp.where(lane % 2 == 0, fv[0:8], fv[8:16])
        rate_ref[...] = by_factor(packed, [math.exp(consts[f][1] * (128 // f)) for f in FACTORS])

        def by_distance(m):
            logs = [consts[f][1] * (cells // f) for f in FACTORS]
            return by_factor(packed, [math.exp(g * (m - 1)) / -math.expm1(g * nsec) for g in logs])

        ahead = [None] + [by_distance(m) for m in range(1, nsec + 1)]
        back = [None] + [ahead[nsec - m] for m in range(1, nsec)] + [ahead[nsec]]
        row = (lane % 2) * 8 + lax.broadcasted_iota(jnp.int32, (8, 128), 0)
        edge = by_factor(packed, [1.0 / f for f in FACTORS]) / (row.astype(jnp.float32) + 0.5)
        across = edge * by_factor(packed, [math.exp(consts[f][1] * (cells // f - 1)) for f in FACTORS])
        group = lane // (fields * planes * 2)
        direct = edge * by_factor(packed, [math.exp(-consts[f][1]) for f in FACTORS])
        for m in range(1, nsec + 1):
            prev, after_m = (m - 1) or nsec, m % nsec + 1
            k = m % nsec
            from_last, from_first = across * ahead[prev], -edge * ahead[after_m]
            to_last, to_first = edge * back[prev], -across * back[after_m]
            if m == 1:
                from_last = from_last + direct
            if m == nsec - 1:
                to_first = to_first - direct
            weights[0, k] = jnp.where(group == 0, ahead[m], jnp.where(group == 2, from_last, from_first))
            weights[1, k] = jnp.where(group == 1, back[m], jnp.where(group == 2, to_last, to_first))
            weights[2, k] = jnp.where(group == 4, ahead[m], back[m])
        for side in (0, 1):
            @pl.when(jnp.logical_not(sides[side][0]))
            def _():
                inbox[2 * side] = jnp.zeros((nsec, 8, 128), jnp.float32)

    for k in range(fields):
        for p in range(planes):
            for edge in (7, rows + 8):
                rg[k, p, edge:edge + 1, :] = jnp.zeros((1, cells), jnp.float32)

    for copy in loads[:2]:
        copy.wait()

    row8 = lax.broadcasted_iota(jnp.int32, (8, cells), 0)

    def radius(t):
        return (rad * rows + t * 8 + row8).astype(jnp.float32) + 0.5

    def fluxes(t, carry):
        first, last = carry
        part = pl.ds(pl.multiple_of(t * 8, 8), 8)
        padded = pl.ds(pl.multiple_of(t * 8 + 8, 8), 8)
        half_r = 0.5 * radius(t)
        for p in range(planes):
            d, mx, mr, mt, e = [st[k, p, part, :] for k in range(fields)]
            ux, ur, ut, pr = primitive(d, mx, mr, mt, e)
            ep = e + pr
            hx = 0.5 * ux
            for k, v in enumerate((0.5 * mx, mx * hx + 0.5 * pr, mr * hx, mt * hx, ep * hx)):
                fx[k, p, part, :] = v
            gr = half_r * ur
            for k, v in enumerate((half_r * mr, mx * gr, mr * gr + half_r * pr, mt * gr, ep * gr)):
                rg[k, p, padded, :] = v
            s = 0.5 / dtheta
            gt = s * ut
            for k, v in enumerate((s * mt, mx * gt, mr * gt, mt * gt + s * pr, ep * gt)):
                hz[k, p, part, :] = v
                slot = (k * planes + p) * tiles + t
                here = lane == slot
                first = jnp.where(here, pltpu.roll(v[:, :128], slot, 1), first)
                last = jnp.where(here, pltpu.roll(v[:, cells - 128:], slot + 1, 1), last)
        return first, last

    zero = jnp.zeros((8, 128), jnp.float32)
    first, last = lax.fori_loop(0, NEAR // 8 + 1, fluxes, (zero, zero))
    npack = fields * planes * 2

    def rhs(k, p, size, inv_r):
        part = slice(0, size)
        wide = lax.broadcasted_iota(jnp.int32, (size, cells), 1)
        h = hz[k, p, part, :]
        v = jnp.where(wide == 0, 0.0, pltpu.roll(h, 1, 1)) - jnp.where(wide == cells - 1, 0.0, pltpu.roll(h, cells - 1, 1))
        v = v + (rg[k, p, 7:size + 7, :] - rg[k, p, 9:size + 9, :])
        if k == 2:
            v = v + (2.0 * dtheta) * hz[3, p, part, :]
        if k == 3:
            v = v - (2.0 * dtheta) * hz[2, p, part, :]
        v = v * inv_r
        return v - fx[k, 1, part, :] if p == 0 else v + fx[k, 0, part, :]

    def inverse_radius(size):
        place = rad * rows + lax.broadcasted_iota(jnp.int32, (size, cells), 0)
        return 1.0 / (place.astype(jnp.float32) + 0.5)

    def number(flags):
        return sum(jnp.where(flag, 1, 0) for flag in flags)

    count = number(v[2] for v in rads + sides)
    count = count + jnp.where(near, sum(size(to, True) for to in range(3)), number(v[2] for v in secs))
    pl.when(count > 0)(lambda: pl.semaphore_wait(barrier, count))

    for ready, pairs in ((ax_ready, sides), (sec_ready, secs), (rad_ready, rads)):
        for side in (0, 1):
            pl.when(pairs[side][2])(functools.partial(signal, ready.at[1 - side], pairs[side][1]))

    def ax_copy(side, c):
        part = pl.ds(c * crow, crow)
        return pltpu.make_async_remote_copy(
            src_ref=state_ref.at[:, (planes - 1) if side == 1 else 0, part, :],
            dst_ref=ghost.at[1 - side, :, part, :],
            send_sem=ax_ssem.at[side, c],
            recv_sem=ax_rsem.at[1 - side, c],
            device_id=sides[side][1],
            device_id_type=MESH,
        )

    def answered(ready, send):
        pl.semaphore_wait(ready, 1)
        send()

    def send_ax(side, chunks):
        for c in chunks:
            ax_copy(side, c).start()

    odd = ax % 2
    for side in (0, 1):
        pl.when(sides[side][2] & (odd != side))(functools.partial(send_ax, side, range(CHUNKS)))
    visit(True, lambda to, s, a: signal(packet_ready.at[jnp.where(tardy, 1, 0)], {"sec": s, "ax": a}))
    for side in (0, 1):
        pl.when(sides[side][2] & (odd == side))(functools.partial(send_ax, side, range(CHUNKS)))
    @pl.when(near)
    def _():
        inv_r = inverse_radius(NEAR)
        wf, wb = weigh_f[...], weigh_b[...]
        pack = zero
        terms = {}

        def halves(v):
            return v[:, :128] + v[:, 128:]

        for k in range(fields):
            for p in range(planes):
                h = hz[k, p, 0:NEAR, :]
                v = rhs(k, p, NEAR, inv_r)
                beside = fx[k, 1, 0:NEAR, :] if p == 0 else -fx[k, 0, 0:NEAR, :]
                sums = {0: halves(v * wf), 1: halves(v * wb), 4: halves(beside * wf), 5: halves(beside * wb)}
                for rt in (0, 1):
                    u = (k * planes + p) * 2 + rt
                    part = slice(rt * 8, rt * 8 + 8)
                    for group, v_sum in sums.items():
                        terms[group * npack + u] = v_sum[part]
                    at = 2 * npack + u
                    pack = jnp.where(lane == at, pltpu.roll(h[part, cells - 128:], at + 1, 1), pack)
                    at = 3 * npack + u
                    pack = jnp.where(lane == at, pltpu.roll(h[part, :128], at, 1), pack)
        width = 1
        while width < 128:
            high = (lane & width) != 0
            merged = {}
            for i in range(64 // width):
                x, y = terms.get(2 * i), terms.get(2 * i + 1)
                if x is not None and y is not None:
                    merged[i] = jnp.where(high, y, x) + pltpu.roll(jnp.where(high, x, y), width, 1)
                elif x is not None or y is not None:
                    x = y if x is None else x
                    merged[i] = x + pltpu.roll(x, width, 1)
            terms, width = merged, width * 2
        middle = (lane >= 2 * npack) & (lane < 4 * npack)
        pack = jnp.where(middle, pack, terms[0])
        packet[...] = pack
        inbox[1, 0] = pack

    def packet_copy(to, s, a):
        return pltpu.make_async_remote_copy(
            src_ref=packet,
            dst_ref=inbox.at[2 - to, lax.rem(s - sec + nsec, nsec)],
            send_sem=packet_ssem.at[to],
            recv_sem=packet_rsem.at[2 - to],
            device_id={"sec": s, "ax": a},
            device_id_type=MESH,
        )

    def packet_to(to, s, a):
        packet_copy(to, s, a).start()

    def all_packets(to):
        box = inbox.at[to] if to != 1 else inbox.at[1, pl.ds(1, nsec - 1)]
        return pltpu.make_async_remote_copy(
            src_ref=box,
            dst_ref=box,
            send_sem=packet_ssem.at[to],
            recv_sem=packet_rsem.at[to],
            device_id={"sec": lax.rem(sec + 1, nsec)},
            device_id_type=MESH,
        )

    for side in (0, 1):
        pl.when(near & sides[side][2])(functools.partial(packet_to, 2 * side, sec, ax + 2 * side - 1))
    visit(True, packet_to)

    for copy in loads[2:]:
        copy.wait()
    first, last = lax.fori_loop(NEAR // 8 + 1, tiles, fluxes, (first, last))
    sec_send[0] = first
    sec_send[1] = last

    def sec_copy(side):
        return pltpu.make_async_remote_copy(
            src_ref=sec_send.at[side],
            dst_ref=sec_recv.at[1 - side],
            send_sem=sec_ssem.at[side],
            recv_sem=sec_rsem.at[1 - side],
            device_id=secs[side][1],
            device_id_type=MESH,
        )


    for k in range(fields):
        for p in range(planes):
            slot = k * planes + p
            rad_send[0, slot:slot + 1, :] = rg[k, p, 8:9, :]
            rad_send[1, slot:slot + 1, :] = rg[k, p, rows + 7:rows + 8, :]

    def rad_copy(side):
        return pltpu.make_async_remote_copy(
            src_ref=rad_send.at[side],
            dst_ref=rad_recv.at[1 - side],
            send_sem=rad_ssem.at[side],
            recv_sem=rad_rsem.at[1 - side],
            device_id=rads[side][1],
            device_id_type=MESH,
        )

    for side in (0, 1):
        pl.when(secs[side][2])(lambda side=side: sec_copy(side).start())
        pl.when(rads[side][2])(lambda side=side: rad_copy(side).start())
    for side in (0, 1):
        pl.when(sides[side][3] & (odd == side))(
            lambda side=side: answered(ax_ready.at[side], functools.partial(send_ax, side, range(CHUNKS)))
        )
    for side in (0, 1):
        pl.when(sides[side][3] & (odd != side) & ~sides[side][4])(
            lambda side=side: answered(ax_ready.at[side], functools.partial(send_ax, side, range(CHUNKS)))
        )
    for side in (0, 1):
        pl.when(secs[side][3] & ~secs[side][4])(lambda side=side: answered(sec_ready.at[side], sec_copy(side).start))

    inv_r = inverse_radius(rows)
    for p in range(planes):
        for k in range(fields):
            out_ref[k, p] = rhs(k, p, rows, inv_r)

    pl.when(rads[1][3])(lambda: answered(rad_ready.at[1], rad_copy(1).start))

    @pl.when(near)
    def _():
        for side in (0, 1):
            pl.when(sides[side][3] & ~sides[side][4])(functools.partial(packet_to, 2 * side, sec, ax + 2 * side - 1))
        answers = sum(size(to, False) for to in range(3))
        pl.when(answers > 0)(lambda: pl.semaphore_wait(packet_ready.at[0], answers))

    visit(False, packet_to)

    def axial(c, both=(0, 1)):
        for side in both:
            @pl.when(sides[side][0])
            def _():
                ax_copy(1 - side, c).wait_recv()
                part = pl.ds(c * crow, crow)
                d, mx, mr, mt, e = [ghost[side, k, part, :] for k in range(fields)]
                ux, ur, ut, pr = primitive(d, mx, mr, mt, e)
                s = 0.5 if side == 0 else -0.5
                hx = s * ux
                for k, v in enumerate((s * mx, mx * hx + s * pr, mr * hx, mt * hx, (e + pr) * hx)):
                    out_ref[k, side, part, :] += v

    def scan(p):
        fv = factors()
        lane16 = lax.broadcasted_iota(jnp.int32, (NEAR, 128), 1)
        keeps = zero
        scale = spread[2]
        for k in range(fields):
            for half in (0, 1):
                x = out_ref[k, p, 0:NEAR, half * 128:(half + 1) * 128]
                for d in (1, 2, 4, 8):
                    swap = jnp.where((lane16 & d) == 0, pltpu.roll(x, 128 - d, 1), pltpu.roll(x, d, 1))
                    x = jnp.where(fv > d, 0.5 * (x + swap), x)
                a, b = x, x
                for n, d in enumerate(SHIFTS):
                    a = a + coef_f[n] * pltpu.roll(a, d, 1)
                    b = b + coef_b[n] * pltpu.roll(b, 128 - d, 1)
                near_c[half, k, p] = scale * (a + b - x)
                for rt in (0, 1):
                    u = (k * planes + p) * 2 + rt
                    if half == 0:
                        tail = pltpu.roll(a[rt * 8:rt * 8 + 8], (u + 1) % 128, 1)
                        keeps = jnp.where(lane == u, tail, keeps)
                    else:
                        head = pltpu.roll(b[rt * 8:rt * 8 + 8], npack + u, 1)
                        keeps = jnp.where(lane == npack + u, head, keeps)
        keep_ref[...] = keeps if p == planes - 1 else keep_ref[...] + keeps

    axial(0, (1,))
    pl.when(near)(functools.partial(scan, 1))

    @pl.when(sides[0][4])
    def _():
        answered(ax_ready.at[0], functools.partial(send_ax, 0, range(CHUNKS)))
        packet_to(0, sec, ax - 1)

    @pl.when(reach)
    def _():
        pl.semaphore_wait(packet_ready.at[1], 1)
        packet_to(jnp.where(ax == 0, 1, 0), 0, 0)

    for side in (0, 1):
        pl.when(secs[side][4])(lambda side=side: answered(sec_ready.at[side], sec_copy(side).start))

    axial(0, (0,))
    pl.when(near)(functools.partial(scan, 0))

    sec_copy(1).wait_recv()
    sec_copy(0).wait_recv()
    before = sec_recv[0]
    after = sec_recv[1]
    thin = lax.broadcasted_iota(jnp.int32, (rows, 128), 1)

    def edges(packed, slot, to):
        column = [pltpu.roll(packed, (to - slot - t) % 128, 1) for t in range(tiles)]
        return jnp.concatenate(column, axis=0) * inv_r[:, :128]

    for p in range(planes):
        for k in range(fields):
            slot = (k * planes + p) * tiles
            out_ref[k, p, :, :128] += jnp.where(thin == 0, edges(before, slot, 0), 0.0)
            out_ref[k, p, :, cells - 128:] -= jnp.where(thin == 127, edges(after, slot, 127), 0.0)

    for c in range(1, CHUNKS):
        axial(c)

    @pl.when(near)
    def _():
        group = lane // npack
        sum_f, sum_b, sum_x = zero, zero, zero
        all_packets(1).wait_recv()
        for side in (0, 1):
            pl.when(sides[side][0])(all_packets(2 * side).wait_recv)
        for m in range(nsec):
            sum_f += inbox[1, m] * weights[0, m]
            sum_b += inbox[1, m] * weights[1, m]
            sum_x += jnp.where(lane % 4 < 2, inbox[0, m], inbox[2, m]) * weights[2, m]

        def down(v, groups):
            return pltpu.roll(v, 128 - groups * npack, 1)

        sum_f = sum_f + down(sum_f, 2) + down(sum_f, 3)
        sum_b = sum_b + down(sum_b, 1) + down(sum_b, 2)
        total_in = jnp.where(group == 0, sum_f, sum_b) + down(sum_x, 4)
        inner = keep_ref[...] + rate_ref[...] * total_in
        for k in range(fields):
            for p in range(planes):
                for rt in (0, 1):
                    u = (k * planes + p) * 2 + rt
                    part = slice(rt * 8, rt * 8 + 8)
                    for half in (0, 1):
                        src_f, src_b = (total_in, inner) if half == 0 else (inner, total_in)
                        cf = jnp.broadcast_to(src_f[:, u:u + 1], (8, 128))
                        cb = jnp.broadcast_to(src_b[:, npack + u:npack + u + 1], (8, 128))
                        w = near_c[half, k, p, part, :] + spread[0, part, :] * cf + spread[1, part, :] * cb
                        out_ref[k, p, part, half * 128:(half + 1) * 128] = w

    pl.when(rads[0][3])(lambda: answered(rad_ready.at[0], rad_copy(0).start))
    for side in (0, 1):
        @pl.when(rads[side][0])
        def _():
            rad_copy(1 - side).wait_recv()
            row = 0 if side == 0 else rows - 1
            sign = 1.0 if side == 0 else -1.0
            for k in range(fields):
                for p in range(planes):
                    slot = k * planes + p
                    out_ref[k, p, row:row + 1, :] += (sign * inv_r[row:row + 1, :]) * rad_recv[side, slot:slot + 1, :]

    @pl.when(near)
    def _():
        all_packets(1).wait_send()
        for side in (0, 1):
            pl.when(sides[side][0])(all_packets(2 * side).wait_send)

    sec_copy(0).wait_send()
    sec_copy(1).wait_send()
    for side in (0, 1):
        pl.when(rads[side][0])(lambda side=side: rad_copy(side).wait_send())
        for c in range(CHUNKS):
            pl.when(sides[side][0])(lambda side=side, c=c: ax_copy(side, c).wait_send())


def body(state, coarsen):
    fields, planes, rows, cells = state.shape
    nsec, nrad, nax = lax.axis_size("sec"), lax.axis_size("rad"), lax.axis_size("ax")
    block = (fields, planes, rows, cells)
    f32 = jnp.float32
    dma = pltpu.SemaphoreType.DMA
    return pl.pallas_call(
        functools.partial(kernel, nsec, nrad, nax),
        out_shape=pltpu.VMEM(block, f32),
        in_specs=[
            pl.BlockSpec(memory_space=pltpu.HBM),
            pl.BlockSpec(memory_space=pltpu.HBM),
        ],
        out_specs=pl.BlockSpec(memory_space=pltpu.VMEM),
        scratch_shapes=[
            pltpu.SMEM((NEAR,), jnp.int32),
            dma(()),
            pltpu.VMEM(block, f32),
            pltpu.VMEM(block, f32),
            pltpu.VMEM((fields, planes, rows + 16, cells), f32),
            pltpu.VMEM(block, f32),
            pltpu.VMEM((2, fields, rows, cells), f32),
            pltpu.VMEM((2, fields * planes, cells), f32),
            pltpu.VMEM((2, fields * planes, cells), f32),
            pltpu.VMEM((2, 8, 128), f32),
            pltpu.VMEM((2, 8, 128), f32),
            pltpu.VMEM((len(SHIFTS), NEAR, 128), f32),
            pltpu.VMEM((len(SHIFTS), NEAR, 128), f32),
            pltpu.VMEM((NEAR, cells), f32),
            pltpu.VMEM((NEAR, cells), f32),
            pltpu.VMEM((3, NEAR, 128), f32),
            pltpu.VMEM((8, 128), f32),
            pltpu.VMEM((3, nsec, 8, 128), f32),
            pltpu.VMEM((2, fields, planes, NEAR, 128), f32),
            pltpu.VMEM((8, 128), f32),
            pltpu.VMEM((8, 128), f32),
            pltpu.VMEM((3, nsec, 8, 128), f32),
            dma((CHUNKS,)),
            dma((2, CHUNKS)),
            dma((2, CHUNKS)),
            dma((2,)),
            dma((2,)),
            dma((2,)),
            dma((2,)),
            dma((3,)),
            dma((3,)),
            pltpu.SemaphoreType.REGULAR((2,)),
            pltpu.SemaphoreType.REGULAR((2,)),
            pltpu.SemaphoreType.REGULAR((2,)),
            pltpu.SemaphoreType.REGULAR((2,)),
        ],
        compiler_params=pltpu.CompilerParams(
            collective_id=0, has_side_effects=True, vmem_limit_bytes=32 * 1024 * 1024
        ),
        cost_estimate=pl.CostEstimate(flops=4_000_000, bytes_accessed=2_000_000, transcendentals=0),
    )(pltpu.with_memory_space_constraint(coarsen, pltpu.HBM), pltpu.with_memory_space_constraint(state, pltpu.HBM))


def solution(mesh):
    return jax.shard_map(
        body,
        mesh=mesh,
        in_specs=(P(None, "ax", "rad", "sec"), P()),
        out_specs=P(None, "ax", "rad", "sec"),
        check_vma=False,
    )
```

```python
import functools
import math

import jax
import jax.numpy as jnp
from jax import lax
from jax.experimental import pallas as pl
from jax.experimental.pallas import tpu as pltpu
from jax.sharding import PartitionSpec as P

GAMMA = 1.4
KAPPA = 1.44
NEAR = 16
FACTORS = (1, 2, 4, 8, 16)
SHIFTS = (1, 2, 4, 8, 16, 32, 64)
MESH = pl.DeviceIdType.MESH
CHUNKS = 4


def filter_constants(total_cells):
    dtheta = 2.0 * math.pi / total_cells
    out = {}
    for f in FACTORS:
        beta = KAPPA / (f * dtheta) ** 2
        half = 0.5 / beta
        gap = math.sqrt(half * (2.0 + half)) - half
        out[f] = (1.0 - gap, math.log1p(-gap), 1.0 / (1.0 + 2.0 * beta * gap))
    return out


def primitive(d, mx, mr, mt, e):
    inv = 1.0 / d
    ux, ur, ut = mx * inv, mr * inv, mt * inv
    p = (GAMMA - 1.0) * (e - 0.5 * (mx * ux + mr * ur + mt * ut))
    return ux, ur, ut, p


def by_factor(fv, values):
    out = jnp.full(fv.shape, values[0], jnp.float32)
    for f, v in zip(FACTORS[1:], values[1:]):
        out = jnp.where(fv == f, jnp.float32(v), out)
    return out


def kernel(
    nsec, nrad, nax,
    coarsen_hbm, state_ref, out_ref,
    coarsen_ref, coarsen_sem, st, fx, rg, hz, ghost, rad_send, rad_recv, sec_send, sec_recv,
    coef_f, coef_b, weigh_f, weigh_b, spread, rate_ref, weights, near_c, packet, keep_ref, inbox,
    load_sem, ax_ssem, ax_rsem, rad_ssem, rad_rsem, sec_ssem, sec_rsem, packet_ssem, packet_rsem,
    ax_ready, rad_ready, sec_ready, packet_ready,
):
    fields, planes, rows, cells = st.shape
    total = cells * nsec
    dtheta = 2.0 * math.pi / total
    tiles = rows // 8
    crow = rows // CHUNKS
    sec, rad, ax = lax.axis_index("sec"), lax.axis_index("rad"), lax.axis_index("ax")
    near = rad == 0

    loads = []
    for c in range(CHUNKS):
        part = pl.ds(c * crow, crow)
        copy = pltpu.make_async_copy(state_ref.at[:, :, part, :], st.at[:, :, part, :], load_sem.at[c])
        copy.start()
        loads.append(copy)

    factor_load = pltpu.make_async_copy(coarsen_hbm, coarsen_ref, coarsen_sem)
    pl.when(near)(factor_load.start)

    def slow(s, r, a):
        return (s == 0) & (r == 0) & (a == 0)

    def rank(s, a):
        turn = jnp.where(s < nsec // 2, s, nsec + nsec // 2 - 1 - s)
        step = jnp.where(a == 0, 3, jnp.where(a == 1, 0, jnp.where(a == 2, 2, 1)))
        return 4 * turn + step + jnp.where(slow(s, rad, a), 1000, 0)

    mine = rank(sec, ax)
    barrier = pltpu.get_barrier_semaphore()

    def signal(sem, where):
        pl.semaphore_signal(sem, inc=1, device_id=where, device_id_type=MESH)

    sides = [
        (there, {"ax": a}, there & (rank(sec, a) < mine), there & (rank(sec, a) > mine), there & slow(sec, rad, a))
        for there, a in ((ax > 0, ax - 1), (ax < nax - 1, ax + 1))
    ]
    rads = [
        (rad > 0, {"rad": rad - 1}, (rad > 0) & ~slow(sec, rad - 1, ax), slow(sec, rad - 1, ax)),
        (rad < nrad - 1, {"rad": rad + 1}, slow(sec, rad, ax), (rad < nrad - 1) & ~slow(sec, rad, ax)),
    ]
    secs = [
        (True, {"sec": s}, rank(s, ax) < mine, rank(s, ax) > mine, slow(s, rad, ax))
        for s in (lax.rem(sec + nsec - 1, nsec), lax.rem(sec + 1, nsec))
    ]
    far = ~near
    for _, where, _, later, *_ in rads + sides:
        pl.when(later)(functools.partial(signal, barrier, where))
    for _, where, _, later, _ in secs:
        pl.when(far & later)(functools.partial(signal, barrier, where))

    tardy = slow(sec, rad, ax)
    turn = jnp.where(sec < nsec // 2, sec, nsec + nsec // 2 - 1 - sec)
    reach = near & (ax <= 1) & (sec != 0)

    middle = turn == 3
    after = (turn >= 4) & (turn < 7)

    def spans(to, kind):
        first = jnp.where(tardy | (ax + to == 1), 1, 0)
        upto = jnp.where(tardy, nsec, turn)
        beyond = jnp.where(tardy, nsec, turn + 1)
        if kind == "greet":
            return (beyond, nsec), (jnp.where(after, 3, 0), jnp.where(after, 4, 0))
        if kind == "answer":
            return (first, jnp.where(after, 3, upto)), (jnp.where(after, 4, 0), jnp.where(after, turn, 0))
        if kind == "early":
            return (first, upto), (jnp.where(middle, 4, 0), jnp.where(middle, 7, 0))
        return (beyond, jnp.where(middle, 4, nsec)), (jnp.where(middle, 7, 0), jnp.where(middle, nsec, 0))

    def there(to):
        return near if to == 1 else near & sides[to // 2][0]

    def size(to, kind):
        return jnp.where(there(to), sum(jnp.maximum(hi - lo, 0) for lo, hi in spans(to, kind)), 0)

    def visit(kind, act):
        for to in (1, 0, 2):
            def step(t, carry):
                s = jnp.where(t < nsec // 2, t, nsec + nsec // 2 - 1 - t)
                act(to, s, ax + (to - 1))
                return carry

            @pl.when(there(to))
            def _():
                for lo, hi in spans(to, kind):
                    lax.fori_loop(lo, hi, step, 0)

    visit("greet", lambda to, s, a: signal(barrier, {"sec": s, "ax": a}))
    pl.when(reach)(lambda: signal(barrier, {"sec": 0, "ax": 0}))

    lane = lax.broadcasted_iota(jnp.int32, (8, 128), 1)
    consts = filter_constants(total)

    def factors():
        row16 = lax.broadcasted_iota(jnp.int32, (NEAR, 128), 0)
        fv = jnp.full((NEAR, 128), 1, jnp.int32)
        for i in range(NEAR):
            fv = jnp.where(row16 == i, coarsen_ref[i], fv)
        return fv

    @pl.when(near)
    def _():
        factor_load.wait()
        fv = factors()
        lane16 = lax.broadcasted_iota(jnp.int32, (NEAR, 128), 1)
        for n, d in enumerate(SHIFTS):
            step = by_factor(fv, [math.exp(consts[f][1] * (d // f)) if d >= f else 0.0 for f in FACTORS])
            coef_f[n] = jnp.where(lane16 >= d, step, 0.0)
            coef_b[n] = jnp.where(lane16 < 128 - d, step, 0.0)
        fw = jnp.concatenate([fv, fv], axis=1)
        share = by_factor(fw, [1.0 / f for f in FACTORS])
        logs = by_factor(fw, [consts[f][1] for f in FACTORS])
        block = lax.broadcasted_iota(jnp.int32, (NEAR, cells), 1).astype(jnp.float32)
        block = jnp.floor(block * share)
        wide = lax.broadcasted_iota(jnp.int32, (NEAR, cells), 1)
        inv_r = 1.0 / (lax.broadcasted_iota(jnp.int32, (NEAR, cells), 0).astype(jnp.float32) + 0.5)
        for ref, power in ((weigh_f, cells * share - 1.0 - block), (weigh_b, block)):
            w = share * jnp.exp(logs * power)
            ref[0] = w
            ref[1] = w * inv_r
            ref[2] = inv_r * (
                jnp.where(wide == cells - 1, 0.0, pltpu.roll(w, cells - 1, 1)) - jnp.where(wide == 0, 0.0, pltpu.roll(w, 1, 1))
            )
        scale = by_factor(fv, [consts[f][2] for f in FACTORS])
        share, logs, block = share[:, :128], logs[:, :128], block[:, :128]
        spread[0] = scale * jnp.exp(logs * (block + 1.0))
        spread[1] = scale * jnp.exp(logs * (128.0 * share - block))
        spread[2] = scale
        packed = jnp.where(lane % 2 == 0, fv[0:8], fv[8:16])
        rate_ref[...] = by_factor(packed, [math.exp(consts[f][1] * (128 // f)) for f in FACTORS])

        def by_distance(m):
            logs = [consts[f][1] * (cells // f) for f in FACTORS]
            return by_factor(packed, [math.exp(g * (m - 1)) / -math.expm1(g * nsec) for g in logs])

        ahead = [None] + [by_distance(m) for m in range(1, nsec + 1)]
        back = [None] + [ahead[nsec - m] for m in range(1, nsec)] + [ahead[nsec]]
        row = (lane % 2) * 8 + lax.broadcasted_iota(jnp.int32, (8, 128), 0)
        edge = by_factor(packed, [1.0 / f for f in FACTORS]) / (row.astype(jnp.float32) + 0.5)
        across = edge * by_factor(packed, [math.exp(consts[f][1] * (cells // f - 1)) for f in FACTORS])
        group = lane // (fields * planes * 2)
        direct = edge * by_factor(packed, [math.exp(-consts[f][1]) for f in FACTORS])
        for m in range(1, nsec + 1):
            prev, after_m = (m - 1) or nsec, m % nsec + 1
            k = m % nsec
            from_last, from_first = across * ahead[prev], -edge * ahead[after_m]
            to_last, to_first = edge * back[prev], -across * back[after_m]
            if m == 1:
                from_last = from_last + direct
            if m == nsec - 1:
                to_first = to_first - direct
            weights[0, k] = jnp.where(group == 0, ahead[m], jnp.where(group == 2, from_last, from_first))
            weights[1, k] = jnp.where(group == 1, back[m], jnp.where(group == 2, to_last, to_first))
            weights[2, k] = jnp.where(group == 4, ahead[m], back[m])
        for side in (0, 1):
            @pl.when(jnp.logical_not(sides[side][0]))
            def _():
                inbox[2 * side] = jnp.zeros((nsec, 8, 128), jnp.float32)

    for k in range(fields):
        for p in range(planes):
            for edge in (7, rows + 8):
                rg[k, p, edge:edge + 1, :] = jnp.zeros((1, cells), jnp.float32)

    for copy in loads[:2]:
        copy.wait()

    row8 = lax.broadcasted_iota(jnp.int32, (8, cells), 0)

    def radius(t):
        return (rad * rows + t * 8 + row8).astype(jnp.float32) + 0.5

    def fluxes(t, carry):
        first, last = carry
        part = pl.ds(pl.multiple_of(t * 8, 8), 8)
        padded = pl.ds(pl.multiple_of(t * 8 + 8, 8), 8)
        half_r = 0.5 * radius(t)
        for p in range(planes):
            d, mx, mr, mt, e = [st[k, p, part, :] for k in range(fields)]
            ux, ur, ut, pr = primitive(d, mx, mr, mt, e)
            ep = e + pr
            hx = 0.5 * ux
            for k, v in enumerate((0.5 * mx, mx * hx + 0.5 * pr, mr * hx, mt * hx, ep * hx)):
                fx[k, p, part, :] = v
            gr = half_r * ur
            for k, v in enumerate((half_r * mr, mx * gr, mr * gr + half_r * pr, mt * gr, ep * gr)):
                rg[k, p, padded, :] = v
            s = 0.5 / dtheta
            gt = s * ut
            for k, v in enumerate((s * mt, mx * gt, mr * gt, mt * gt + s * pr, ep * gt)):
                hz[k, p, part, :] = v
                slot = (k * planes + p) * tiles + t
                here = lane == slot
                first = jnp.where(here, pltpu.roll(v[:, :128], slot, 1), first)
                last = jnp.where(here, pltpu.roll(v[:, cells - 128:], slot + 1, 1), last)
        return first, last

    zero = jnp.zeros((8, 128), jnp.float32)
    first, last = lax.fori_loop(0, NEAR // 8 + 1, fluxes, (zero, zero))
    npack = fields * planes * 2

    def rhs(k, p, size, inv_r):
        part = slice(0, size)
        wide = lax.broadcasted_iota(jnp.int32, (size, cells), 1)
        h = hz[k, p, part, :]
        v = jnp.where(wide == 0, 0.0, pltpu.roll(h, 1, 1)) - jnp.where(wide == cells - 1, 0.0, pltpu.roll(h, cells - 1, 1))
        v = v + (rg[k, p, 7:size + 7, :] - rg[k, p, 9:size + 9, :])
        if k == 2:
            v = v + (2.0 * dtheta) * hz[3, p, part, :]
        if k == 3:
            v = v - (2.0 * dtheta) * hz[2, p, part, :]
        v = v * inv_r
        return v - fx[k, 1, part, :] if p == 0 else v + fx[k, 0, part, :]

    def inverse_radius(size):
        place = rad * rows + lax.broadcasted_iota(jnp.int32, (size, cells), 0)
        return 1.0 / (place.astype(jnp.float32) + 0.5)

    def number(flags):
        return sum(jnp.where(flag, 1, 0) for flag in flags)

    count = number(v[2] for v in rads + sides)
    count = count + jnp.where(near, sum(size(to, "early") for to in range(3)), number(v[2] for v in secs))
    pl.when(count > 0)(lambda: pl.semaphore_wait(barrier, count))

    for ready, pairs in ((ax_ready, sides), (sec_ready, secs), (rad_ready, rads)):
        for side in (0, 1):
            pl.when(pairs[side][2])(functools.partial(signal, ready.at[1 - side], pairs[side][1]))

    def ax_copy(side, c):
        part = pl.ds(c * crow, crow)
        return pltpu.make_async_remote_copy(
            src_ref=state_ref.at[:, (planes - 1) if side == 1 else 0, part, :],
            dst_ref=ghost.at[1 - side, :, part, :],
            send_sem=ax_ssem.at[side, c],
            recv_sem=ax_rsem.at[1 - side, c],
            device_id=sides[side][1],
            device_id_type=MESH,
        )

    def answered(ready, send):
        pl.semaphore_wait(ready, 1)
        send()

    def send_ax(side, chunks):
        for c in chunks:
            ax_copy(side, c).start()

    odd = ax % 2
    for side in (0, 1):
        pl.when(sides[side][2] & (odd != side))(functools.partial(send_ax, side, range(CHUNKS)))
    visit("answer", lambda to, s, a: signal(packet_ready.at[jnp.where(tardy, 1, 0)], {"sec": s, "ax": a}))
    for side in (0, 1):
        pl.when(sides[side][2] & (odd == side))(functools.partial(send_ax, side, range(CHUNKS)))
    @pl.when(near)
    def _():
        pack = zero
        terms = {}

        def halves(v):
            return v[:, :128] + v[:, 128:]

        for k in range(fields):
            for p in range(planes):
                h = hz[k, p, 0:NEAR, :]
                g = rg[k, p, 7:NEAR + 7, :] - rg[k, p, 9:NEAR + 9, :]
                if k == 2:
                    g = g + (2.0 * dtheta) * hz[3, p, 0:NEAR, :]
                if k == 3:
                    g = g - (2.0 * dtheta) * hz[2, p, 0:NEAR, :]
                beside = fx[k, 1, 0:NEAR, :] if p == 0 else -fx[k, 0, 0:NEAR, :]
                sums = {}
                for n, w in enumerate((weigh_f, weigh_b)):
                    sums[4 + n] = halves(beside * w[0])
                    sums[n] = halves(g * w[1] + h * w[2]) - sums[4 + n]
                for rt in (0, 1):
                    u = (k * planes + p) * 2 + rt
                    part = slice(rt * 8, rt * 8 + 8)
                    for group, v_sum in sums.items():
                        terms[group * npack + u] = v_sum[part]
                    at = 2 * npack + u
                    pack = jnp.where(lane == at, pltpu.roll(h[part, cells - 128:], at + 1, 1), pack)
                    at = 3 * npack + u
                    pack = jnp.where(lane == at, pltpu.roll(h[part, :128], at, 1), pack)
        width = 1
        while width < 128:
            high = (lane & width) != 0
            merged = {}
            for i in range(64 // width):
                x, y = terms.get(2 * i), terms.get(2 * i + 1)
                if x is not None and y is not None:
                    merged[i] = jnp.where(high, y, x) + pltpu.roll(jnp.where(high, x, y), width, 1)
                elif x is not None or y is not None:
                    x = y if x is None else x
                    merged[i] = x + pltpu.roll(x, width, 1)
            terms, width = merged, width * 2
        middle = (lane >= 2 * npack) & (lane < 4 * npack)
        pack = jnp.where(middle, pack, terms[0])
        packet[...] = pack
        inbox[1, 0] = pack

    def packet_copy(to, s, a):
        return pltpu.make_async_remote_copy(
            src_ref=packet,
            dst_ref=inbox.at[2 - to, lax.rem(s - sec + nsec, nsec)],
            send_sem=packet_ssem.at[to],
            recv_sem=packet_rsem.at[2 - to],
            device_id={"sec": s, "ax": a},
            device_id_type=MESH,
        )

    def packet_to(to, s, a):
        packet_copy(to, s, a).start()

    def all_packets(to):
        box = inbox.at[to] if to != 1 else inbox.at[1, pl.ds(1, nsec - 1)]
        return pltpu.make_async_remote_copy(
            src_ref=box,
            dst_ref=box,
            send_sem=packet_ssem.at[to],
            recv_sem=packet_rsem.at[to],
            device_id={"sec": lax.rem(sec + 1, nsec)},
            device_id_type=MESH,
        )

    for side in (0, 1):
        pl.when(near & sides[side][2])(functools.partial(packet_to, 2 * side, sec, ax + 2 * side - 1))
    visit("early", packet_to)

    for copy in loads[2:]:
        copy.wait()
    first, last = lax.fori_loop(NEAR // 8 + 1, tiles, fluxes, (first, last))
    sec_send[0] = first
    sec_send[1] = last

    def sec_copy(side):
        return pltpu.make_async_remote_copy(
            src_ref=sec_send.at[side],
            dst_ref=sec_recv.at[1 - side],
            send_sem=sec_ssem.at[side],
            recv_sem=sec_rsem.at[1 - side],
            device_id=secs[side][1],
            device_id_type=MESH,
        )


    for k in range(fields):
        for p in range(planes):
            slot = k * planes + p
            rad_send[0, slot:slot + 1, :] = rg[k, p, 8:9, :]
            rad_send[1, slot:slot + 1, :] = rg[k, p, rows + 7:rows + 8, :]

    def rad_copy(side):
        return pltpu.make_async_remote_copy(
            src_ref=rad_send.at[side],
            dst_ref=rad_recv.at[1 - side],
            send_sem=rad_ssem.at[side],
            recv_sem=rad_rsem.at[1 - side],
            device_id=rads[side][1],
            device_id_type=MESH,
        )

    for side in (0, 1):
        pl.when(secs[side][2])(lambda side=side: sec_copy(side).start())
        pl.when(rads[side][2])(lambda side=side: rad_copy(side).start())
    for side in (0, 1):
        pl.when(sides[side][3] & (odd == side))(
            lambda side=side: answered(ax_ready.at[side], functools.partial(send_ax, side, range(CHUNKS)))
        )
    for side in (0, 1):
        pl.when(sides[side][3] & (odd != side) & ~sides[side][4])(
            lambda side=side: answered(ax_ready.at[side], functools.partial(send_ax, side, range(CHUNKS)))
        )
    for side in (0, 1):
        pl.when(secs[side][3] & ~secs[side][4])(lambda side=side: answered(sec_ready.at[side], sec_copy(side).start))

    inv_r = inverse_radius(rows)
    for p in range(planes):
        for k in range(fields):
            out_ref[k, p] = rhs(k, p, rows, inv_r)

    pl.when(rads[1][3])(lambda: answered(rad_ready.at[1], rad_copy(1).start))

    @pl.when(near)
    def _():
        for side in (0, 1):
            pl.when(sides[side][3] & ~sides[side][4])(functools.partial(packet_to, 2 * side, sec, ax + 2 * side - 1))
        answers = sum(size(to, "late") for to in range(3))
        pl.when(answers > 0)(lambda: pl.semaphore_wait(packet_ready.at[0], answers))

    visit("late", packet_to)

    def axial(c, both=(0, 1)):
        for side in both:
            @pl.when(sides[side][0])
            def _():
                ax_copy(1 - side, c).wait_recv()
                part = pl.ds(c * crow, crow)
                d, mx, mr, mt, e = [ghost[side, k, part, :] for k in range(fields)]
                ux, ur, ut, pr = primitive(d, mx, mr, mt, e)
                s = 0.5 if side == 0 else -0.5
                hx = s * ux
                for k, v in enumerate((s * mx, mx * hx + s * pr, mr * hx, mt * hx, (e + pr) * hx)):
                    out_ref[k, side, part, :] += v

    def scan(p):
        fv = factors()
        lane16 = lax.broadcasted_iota(jnp.int32, (NEAR, 128), 1)
        keeps = zero
        scale = spread[2]
        for k in range(fields):
            for half in (0, 1):
                x = out_ref[k, p, 0:NEAR, half * 128:(half + 1) * 128]
                for d in (1, 2, 4, 8):
                    swap = jnp.where((lane16 & d) == 0, pltpu.roll(x, 128 - d, 1), pltpu.roll(x, d, 1))
                    x = jnp.where(fv > d, 0.5 * (x + swap), x)
                a, b = x, x
                for n, d in enumerate(SHIFTS):
                    a = a + coef_f[n] * pltpu.roll(a, d, 1)
                    b = b + coef_b[n] * pltpu.roll(b, 128 - d, 1)
                near_c[half, k, p] = scale * (a + b - x)
                for rt in (0, 1):
                    u = (k * planes + p) * 2 + rt
                    if half == 0:
                        tail = pltpu.roll(a[rt * 8:rt * 8 + 8], (u + 1) % 128, 1)
                        keeps = jnp.where(lane == u, tail, keeps)
                    else:
                        head = pltpu.roll(b[rt * 8:rt * 8 + 8], npack + u, 1)
                        keeps = jnp.where(lane == npack + u, head, keeps)
        keep_ref[...] = keeps if p == planes - 1 else keep_ref[...] + keeps

    axial(0, (1,))
    pl.when(near)(functools.partial(scan, 1))

    @pl.when(sides[0][4])
    def _():
        answered(ax_ready.at[0], functools.partial(send_ax, 0, range(CHUNKS)))
        packet_to(0, sec, ax - 1)

    @pl.when(reach)
    def _():
        pl.semaphore_wait(packet_ready.at[1], 1)
        packet_to(jnp.where(ax == 0, 1, 0), 0, 0)

    for side in (0, 1):
        pl.when(secs[side][4])(lambda side=side: answered(sec_ready.at[side], sec_copy(side).start))

    axial(0, (0,))
    pl.when(near)(functools.partial(scan, 0))

    sec_copy(1).wait_recv()
    sec_copy(0).wait_recv()
    before = sec_recv[0]
    behind = sec_recv[1]
    thin = lax.broadcasted_iota(jnp.int32, (rows, 128), 1)

    def edges(packed, slot, to):
        column = [pltpu.roll(packed, (to - slot - t) % 128, 1) for t in range(tiles)]
        return jnp.concatenate(column, axis=0) * inv_r[:, :128]

    for p in range(planes):
        for k in range(fields):
            slot = (k * planes + p) * tiles
            out_ref[k, p, :, :128] += jnp.where(thin == 0, edges(before, slot, 0), 0.0)
            out_ref[k, p, :, cells - 128:] -= jnp.where(thin == 127, edges(behind, slot, 127), 0.0)

    for c in range(1, CHUNKS):
        axial(c)

    pl.when(rads[0][3])(lambda: answered(rad_ready.at[0], rad_copy(0).start))
    for side in (0, 1):
        @pl.when(rads[side][0])
        def _():
            rad_copy(1 - side).wait_recv()
            row = 0 if side == 0 else rows - 1
            sign = 1.0 if side == 0 else -1.0
            for k in range(fields):
                for p in range(planes):
                    slot = k * planes + p
                    out_ref[k, p, row:row + 1, :] += (sign * inv_r[row:row + 1, :]) * rad_recv[side, slot:slot + 1, :]

    @pl.when(near)
    def _():
        group = lane // npack
        sum_f, sum_b, sum_x = zero, zero, zero
        all_packets(1).wait_recv()
        for side in (0, 1):
            pl.when(sides[side][0])(all_packets(2 * side).wait_recv)
        for m in range(nsec):
            sum_f += inbox[1, m] * weights[0, m]
            sum_b += inbox[1, m] * weights[1, m]
            sum_x += jnp.where(lane % 4 < 2, inbox[0, m], inbox[2, m]) * weights[2, m]

        def down(v, groups):
            return pltpu.roll(v, 128 - groups * npack, 1)

        sum_f = sum_f + down(sum_f, 2) + down(sum_f, 3)
        sum_b = sum_b + down(sum_b, 1) + down(sum_b, 2)
        total_in = jnp.where(group == 0, sum_f, sum_b) + down(sum_x, 4)
        inner = keep_ref[...] + rate_ref[...] * total_in
        for k in range(fields):
            for p in range(planes):
                for rt in (0, 1):
                    u = (k * planes + p) * 2 + rt
                    part = slice(rt * 8, rt * 8 + 8)
                    for half in (0, 1):
                        src_f, src_b = (total_in, inner) if half == 0 else (inner, total_in)
                        cf = jnp.broadcast_to(src_f[:, u:u + 1], (8, 128))
                        cb = jnp.broadcast_to(src_b[:, npack + u:npack + u + 1], (8, 128))
                        w = near_c[half, k, p, part, :] + spread[0, part, :] * cf + spread[1, part, :] * cb
                        out_ref[k, p, part, half * 128:(half + 1) * 128] = w

    @pl.when(near)
    def _():
        all_packets(1).wait_send()
        for side in (0, 1):
            pl.when(sides[side][0])(all_packets(2 * side).wait_send)

    sec_copy(0).wait_send()
    sec_copy(1).wait_send()
    for side in (0, 1):
        pl.when(rads[side][0])(lambda side=side: rad_copy(side).wait_send())
        for c in range(CHUNKS):
            pl.when(sides[side][0])(lambda side=side, c=c: ax_copy(side, c).wait_send())


def body(state, coarsen):
    fields, planes, rows, cells = state.shape
    nsec, nrad, nax = lax.axis_size("sec"), lax.axis_size("rad"), lax.axis_size("ax")
    block = (fields, planes, rows, cells)
    f32 = jnp.float32
    dma = pltpu.SemaphoreType.DMA
    return pl.pallas_call(
        functools.partial(kernel, nsec, nrad, nax),
        out_shape=pltpu.VMEM(block, f32),
        in_specs=[
            pl.BlockSpec(memory_space=pltpu.HBM),
            pl.BlockSpec(memory_space=pltpu.HBM),
        ],
        out_specs=pl.BlockSpec(memory_space=pltpu.VMEM),
        scratch_shapes=[
            pltpu.SMEM((NEAR,), jnp.int32),
            dma(()),
            pltpu.VMEM(block, f32),
            pltpu.VMEM(block, f32),
            pltpu.VMEM((fields, planes, rows + 16, cells), f32),
            pltpu.VMEM(block, f32),
            pltpu.VMEM((2, fields, rows, cells), f32),
            pltpu.VMEM((2, fields * planes, cells), f32),
            pltpu.VMEM((2, fields * planes, cells), f32),
            pltpu.VMEM((2, 8, 128), f32),
            pltpu.VMEM((2, 8, 128), f32),
            pltpu.VMEM((len(SHIFTS), NEAR, 128), f32),
            pltpu.VMEM((len(SHIFTS), NEAR, 128), f32),
            pltpu.VMEM((3, NEAR, cells), f32),
            pltpu.VMEM((3, NEAR, cells), f32),
            pltpu.VMEM((3, NEAR, 128), f32),
            pltpu.VMEM((8, 128), f32),
            pltpu.VMEM((3, nsec, 8, 128), f32),
            pltpu.VMEM((2, fields, planes, NEAR, 128), f32),
            pltpu.VMEM((8, 128), f32),
            pltpu.VMEM((8, 128), f32),
            pltpu.VMEM((3, nsec, 8, 128), f32),
            dma((CHUNKS,)),
            dma((2, CHUNKS)),
            dma((2, CHUNKS)),
            dma((2,)),
            dma((2,)),
            dma((2,)),
            dma((2,)),
            dma((3,)),
            dma((3,)),
            pltpu.SemaphoreType.REGULAR((2,)),
            pltpu.SemaphoreType.REGULAR((2,)),
            pltpu.SemaphoreType.REGULAR((2,)),
            pltpu.SemaphoreType.REGULAR((2,)),
        ],
        compiler_params=pltpu.CompilerParams(
            collective_id=0, has_side_effects=True, vmem_limit_bytes=32 * 1024 * 1024
        ),
        cost_estimate=pl.CostEstimate(flops=4_000_000, bytes_accessed=2_000_000, transcendentals=0),
    )(pltpu.with_memory_space_constraint(coarsen, pltpu.HBM), pltpu.with_memory_space_constraint(state, pltpu.HBM))


def solution(mesh):
    return jax.shard_map(
        body,
        mesh=mesh,
        in_specs=(P(None, "ax", "rad", "sec"), P()),
        out_specs=P(None, "ax", "rad", "sec"),
        check_vma=False,
    )
```

```python
import functools
import math

import jax
import jax.numpy as jnp
from jax import lax
from jax.experimental import pallas as pl
from jax.experimental.pallas import tpu as pltpu
from jax.sharding import PartitionSpec as P

GAMMA = 1.4
KAPPA = 1.44
NEAR = 16
FACTORS = (1, 2, 4, 8, 16)
SHIFTS = (1, 2, 4, 8, 16, 32, 64)
MESH = pl.DeviceIdType.MESH
CHUNKS = 4


def filter_constants(total_cells):
    dtheta = 2.0 * math.pi / total_cells
    out = {}
    for f in FACTORS:
        beta = KAPPA / (f * dtheta) ** 2
        half = 0.5 / beta
        gap = math.sqrt(half * (2.0 + half)) - half
        out[f] = (1.0 - gap, math.log1p(-gap), 1.0 / (1.0 + 2.0 * beta * gap))
    return out


def primitive(d, mx, mr, mt, e):
    inv = 1.0 / d
    ux, ur, ut = mx * inv, mr * inv, mt * inv
    p = (GAMMA - 1.0) * (e - 0.5 * (mx * ux + mr * ur + mt * ut))
    return ux, ur, ut, p


def by_factor(fv, values):
    out = jnp.full(fv.shape, values[0], jnp.float32)
    for f, v in zip(FACTORS[1:], values[1:]):
        out = jnp.where(fv == f, jnp.float32(v), out)
    return out


def kernel(
    nsec, nrad, nax,
    coarsen_hbm, state_ref, out_ref,
    coarsen_ref, coarsen_sem, st, fx, rg, hz, ghost, rad_send, rad_recv, sec_send, sec_recv,
    coef_f, coef_b, weigh_f, weigh_b, spread, rate_ref, weights, near_c, packet, keep_ref, inbox,
    load_sem, ax_ssem, ax_rsem, rad_ssem, rad_rsem, sec_ssem, sec_rsem, packet_ssem, packet_rsem,
    ax_ready, rad_ready, sec_ready, packet_ready,
):
    fields, planes, rows, cells = st.shape
    total = cells * nsec
    dtheta = 2.0 * math.pi / total
    tiles = rows // 8
    crow = rows // CHUNKS
    sec, rad, ax = lax.axis_index("sec"), lax.axis_index("rad"), lax.axis_index("ax")
    near = rad == 0

    loads = []
    for c in range(CHUNKS):
        part = pl.ds(c * crow, crow)
        copy = pltpu.make_async_copy(state_ref.at[:, :, part, :], st.at[:, :, part, :], load_sem.at[c])
        copy.start()
        loads.append(copy)

    factor_load = pltpu.make_async_copy(coarsen_hbm, coarsen_ref, coarsen_sem)
    pl.when(near)(factor_load.start)

    def slow(s, r, a):
        return (s == 0) & (r == 0) & (a == 0)

    def rank(s, a):
        turn = jnp.where(s < nsec // 2, s, nsec + nsec // 2 - 1 - s)
        step = jnp.where(a == 0, 3, jnp.where(a == 1, 0, jnp.where(a == 2, 2, 1)))
        return 4 * turn + step + jnp.where(slow(s, rad, a), 1000, 0)

    mine = rank(sec, ax)
    barrier = pltpu.get_barrier_semaphore()

    def signal(sem, where):
        pl.semaphore_signal(sem, inc=1, device_id=where, device_id_type=MESH)

    sides = [
        (there, {"ax": a}, there & (rank(sec, a) < mine), there & (rank(sec, a) > mine), there & slow(sec, rad, a))
        for there, a in ((ax > 0, ax - 1), (ax < nax - 1, ax + 1))
    ]
    rads = [
        (rad > 0, {"rad": rad - 1}, (rad > 0) & ~slow(sec, rad - 1, ax), slow(sec, rad - 1, ax)),
        (rad < nrad - 1, {"rad": rad + 1}, slow(sec, rad, ax), (rad < nrad - 1) & ~slow(sec, rad, ax)),
    ]
    secs = [
        (True, {"sec": s}, rank(s, ax) < mine, rank(s, ax) > mine, slow(s, rad, ax))
        for s in (lax.rem(sec + nsec - 1, nsec), lax.rem(sec + 1, nsec))
    ]
    far = ~near
    for _, where, _, later, *_ in rads + sides:
        pl.when(later)(functools.partial(signal, barrier, where))
    for _, where, _, later, _ in secs:
        pl.when(far & later)(functools.partial(signal, barrier, where))

    tardy = slow(sec, rad, ax)
    turn = jnp.where(sec < nsec // 2, sec, nsec + nsec // 2 - 1 - sec)
    reach = near & (ax <= 1) & (sec != 0)

    middle = turn == 3
    after = (turn >= 4) & (turn < 7)

    def spans(to, kind):
        first = jnp.where(tardy | (ax + to == 1), 1, 0)
        upto = jnp.where(tardy, nsec, turn)
        beyond = jnp.where(tardy, nsec, turn + 1)
        if kind == "greet":
            return (beyond, nsec), (jnp.where(after, 3, 0), jnp.where(after, 4, 0))
        if kind == "answer":
            return (first, jnp.where(after, 3, upto)), (jnp.where(after, 4, 0), jnp.where(after, turn, 0))
        if kind == "early":
            return (first, upto), (jnp.where(middle, 4, 0), jnp.where(middle, 7, 0))
        return (beyond, jnp.where(middle, 4, nsec)), (jnp.where(middle, 7, 0), jnp.where(middle, nsec, 0))

    def there(to):
        return near if to == 1 else near & sides[to // 2][0]

    def size(to, kind):
        return jnp.where(there(to), sum(jnp.maximum(hi - lo, 0) for lo, hi in spans(to, kind)), 0)

    def visit(kind, act):
        for to in (1, 0, 2):
            def step(t, carry):
                s = jnp.where(t < nsec // 2, t, nsec + nsec // 2 - 1 - t)
                act(to, s, ax + (to - 1))
                return carry

            @pl.when(there(to))
            def _():
                for lo, hi in spans(to, kind):
                    lax.fori_loop(lo, hi, step, 0)

    visit("greet", lambda to, s, a: signal(barrier, {"sec": s, "ax": a}))
    pl.when(reach)(lambda: signal(barrier, {"sec": 0, "ax": 0}))

    def ax_copy(side, c):
        part = pl.ds(c * crow, crow)
        return pltpu.make_async_remote_copy(
            src_ref=state_ref.at[:, (planes - 1) if side == 1 else 0, part, :],
            dst_ref=ghost.at[1 - side, :, part, :],
            send_sem=ax_ssem.at[side, c],
            recv_sem=ax_rsem.at[1 - side, c],
            device_id=sides[side][1],
            device_id_type=MESH,
        )

    def answered(ready, send):
        pl.semaphore_wait(ready, 1)
        send()

    def send_ax(side, chunks):
        for c in chunks:
            ax_copy(side, c).start()

    odd = ax % 2

    def enter():
        def number(flags):
            return sum(jnp.where(flag, 1, 0) for flag in flags)

        count = number(v[2] for v in rads + sides)
        count = count + jnp.where(near, sum(size(to, "early") for to in range(3)), number(v[2] for v in secs))
        pl.when(count > 0)(lambda: pl.semaphore_wait(barrier, count))

        for ready, pairs in ((ax_ready, sides), (sec_ready, secs), (rad_ready, rads)):
            for side in (0, 1):
                pl.when(pairs[side][2])(functools.partial(signal, ready.at[1 - side], pairs[side][1]))

        for side in (0, 1):
            pl.when(sides[side][2] & (odd != side))(functools.partial(send_ax, side, range(CHUNKS)))
        def answer(t, carry):
            s = jnp.where(t < nsec // 2, t, nsec + nsec // 2 - 1 - t)
            for to in (1, 0, 2):
                pl.when(there(to) & (t >= spans(to, "answer")[0][0]))(
                    functools.partial(signal, packet_ready.at[jnp.where(tardy, 1, 0)], {"sec": s, "ax": ax + (to - 1)})
                )
            return carry

        @pl.when(near)
        def _():
            for lo, hi in ((0, spans(1, "answer")[0][1]), spans(1, "answer")[1]):
                lax.fori_loop(lo, hi, answer, 0)

        for side in (0, 1):
            pl.when(sides[side][2] & (odd == side))(functools.partial(send_ax, side, range(CHUNKS)))

    pl.when(tardy)(enter)

    lane = lax.broadcasted_iota(jnp.int32, (8, 128), 1)
    consts = filter_constants(total)

    def factors():
        row16 = lax.broadcasted_iota(jnp.int32, (NEAR, 128), 0)
        fv = jnp.full((NEAR, 128), 1, jnp.int32)
        for i in range(NEAR):
            fv = jnp.where(row16 == i, coarsen_ref[i], fv)
        return fv

    @pl.when(near)
    def _():
        factor_load.wait()
        fv = factors()
        lane16 = lax.broadcasted_iota(jnp.int32, (NEAR, 128), 1)
        for n, d in enumerate(SHIFTS):
            step = by_factor(fv, [math.exp(consts[f][1] * (d // f)) if d >= f else 0.0 for f in FACTORS])
            coef_f[n] = jnp.where(lane16 >= d, step, 0.0)
            coef_b[n] = jnp.where(lane16 < 128 - d, step, 0.0)
        fw = jnp.concatenate([fv, fv], axis=1)
        share = by_factor(fw, [1.0 / f for f in FACTORS])
        logs = by_factor(fw, [consts[f][1] for f in FACTORS])
        block = lax.broadcasted_iota(jnp.int32, (NEAR, cells), 1).astype(jnp.float32)
        block = jnp.floor(block * share)
        wide = lax.broadcasted_iota(jnp.int32, (NEAR, cells), 1)
        inv_r = 1.0 / (lax.broadcasted_iota(jnp.int32, (NEAR, cells), 0).astype(jnp.float32) + 0.5)
        for ref, power in ((weigh_f, cells * share - 1.0 - block), (weigh_b, block)):
            w = share * jnp.exp(logs * power)
            ref[0] = w
            ref[1] = w * inv_r
            ref[2] = inv_r * (
                jnp.where(wide == cells - 1, 0.0, pltpu.roll(w, cells - 1, 1)) - jnp.where(wide == 0, 0.0, pltpu.roll(w, 1, 1))
            )
        scale = by_factor(fv, [consts[f][2] for f in FACTORS])
        share, logs, block = share[:, :128], logs[:, :128], block[:, :128]
        spread[0] = scale * jnp.exp(logs * (block + 1.0))
        spread[1] = scale * jnp.exp(logs * (128.0 * share - block))
        spread[2] = scale
        packed = jnp.where(lane % 2 == 0, fv[0:8], fv[8:16])
        rate_ref[...] = by_factor(packed, [math.exp(consts[f][1] * (128 // f)) for f in FACTORS])

        def by_distance(m):
            logs = [consts[f][1] * (cells // f) for f in FACTORS]
            return by_factor(packed, [math.exp(g * (m - 1)) / -math.expm1(g * nsec) for g in logs])

        ahead = [None] + [by_distance(m) for m in range(1, nsec + 1)]
        back = [None] + [ahead[nsec - m] for m in range(1, nsec)] + [ahead[nsec]]
        row = (lane % 2) * 8 + lax.broadcasted_iota(jnp.int32, (8, 128), 0)
        edge = by_factor(packed, [1.0 / f for f in FACTORS]) / (row.astype(jnp.float32) + 0.5)
        across = edge * by_factor(packed, [math.exp(consts[f][1] * (cells // f - 1)) for f in FACTORS])
        group = lane // (fields * planes * 2)
        direct = edge * by_factor(packed, [math.exp(-consts[f][1]) for f in FACTORS])
        for m in range(1, nsec + 1):
            prev, after_m = (m - 1) or nsec, m % nsec + 1
            k = m % nsec
            from_last, from_first = across * ahead[prev], -edge * ahead[after_m]
            to_last, to_first = edge * back[prev], -across * back[after_m]
            if m == 1:
                from_last = from_last + direct
            if m == nsec - 1:
                to_first = to_first - direct
            weights[0, k] = jnp.where(group == 0, ahead[m], jnp.where(group == 2, from_last, from_first))
            weights[1, k] = jnp.where(group == 1, back[m], jnp.where(group == 2, to_last, to_first))
            weights[2, k] = jnp.where(group == 4, ahead[m], back[m])
        for side in (0, 1):
            @pl.when(jnp.logical_not(sides[side][0]))
            def _():
                inbox[2 * side] = jnp.zeros((nsec, 8, 128), jnp.float32)

    for k in range(fields):
        for p in range(planes):
            for edge in (7, rows + 8):
                rg[k, p, edge:edge + 1, :] = jnp.zeros((1, cells), jnp.float32)

    for copy in loads[:2]:
        copy.wait()

    row8 = lax.broadcasted_iota(jnp.int32, (8, cells), 0)

    def radius(t):
        return (rad * rows + t * 8 + row8).astype(jnp.float32) + 0.5

    def fluxes(t, carry):
        first, last = carry
        part = pl.ds(pl.multiple_of(t * 8, 8), 8)
        padded = pl.ds(pl.multiple_of(t * 8 + 8, 8), 8)
        half_r = 0.5 * radius(t)
        for p in range(planes):
            d, mx, mr, mt, e = [st[k, p, part, :] for k in range(fields)]
            ux, ur, ut, pr = primitive(d, mx, mr, mt, e)
            ep = e + pr
            hx = 0.5 * ux
            for k, v in enumerate((0.5 * mx, mx * hx + 0.5 * pr, mr * hx, mt * hx, ep * hx)):
                fx[k, p, part, :] = v
            gr = half_r * ur
            for k, v in enumerate((half_r * mr, mx * gr, mr * gr + half_r * pr, mt * gr, ep * gr)):
                rg[k, p, padded, :] = v
            s = 0.5 / dtheta
            gt = s * ut
            for k, v in enumerate((s * mt, mx * gt, mr * gt, mt * gt + s * pr, ep * gt)):
                hz[k, p, part, :] = v
                slot = (k * planes + p) * tiles + t
                here = lane == slot
                first = jnp.where(here, pltpu.roll(v[:, :128], slot, 1), first)
                last = jnp.where(here, pltpu.roll(v[:, cells - 128:], slot + 1, 1), last)
        return first, last

    zero = jnp.zeros((8, 128), jnp.float32)
    first, last = lax.fori_loop(0, NEAR // 8 + 1, fluxes, (zero, zero))
    npack = fields * planes * 2

    def rhs(k, p, size, inv_r):
        part = slice(0, size)
        wide = lax.broadcasted_iota(jnp.int32, (size, cells), 1)
        h = hz[k, p, part, :]
        v = jnp.where(wide == 0, 0.0, pltpu.roll(h, 1, 1)) - jnp.where(wide == cells - 1, 0.0, pltpu.roll(h, cells - 1, 1))
        v = v + (rg[k, p, 7:size + 7, :] - rg[k, p, 9:size + 9, :])
        if k == 2:
            v = v + (2.0 * dtheta) * hz[3, p, part, :]
        if k == 3:
            v = v - (2.0 * dtheta) * hz[2, p, part, :]
        v = v * inv_r
        return v - fx[k, 1, part, :] if p == 0 else v + fx[k, 0, part, :]

    def inverse_radius(size):
        place = rad * rows + lax.broadcasted_iota(jnp.int32, (size, cells), 0)
        return 1.0 / (place.astype(jnp.float32) + 0.5)

    pl.when(~tardy)(enter)

    @pl.when(near)
    def _():
        pack = zero
        terms = {}

        def halves(v):
            return v[:, :128] + v[:, 128:]

        for k in range(fields):
            for p in range(planes):
                h = hz[k, p, 0:NEAR, :]
                g = rg[k, p, 7:NEAR + 7, :] - rg[k, p, 9:NEAR + 9, :]
                if k == 2:
                    g = g + (2.0 * dtheta) * hz[3, p, 0:NEAR, :]
                if k == 3:
                    g = g - (2.0 * dtheta) * hz[2, p, 0:NEAR, :]
                beside = fx[k, 1, 0:NEAR, :] if p == 0 else -fx[k, 0, 0:NEAR, :]
                sums = {}
                for n, w in enumerate((weigh_f, weigh_b)):
                    sums[4 + n] = halves(beside * w[0])
                    sums[n] = halves(g * w[1] + h * w[2]) - sums[4 + n]
                for rt in (0, 1):
                    u = (k * planes + p) * 2 + rt
                    part = slice(rt * 8, rt * 8 + 8)
                    for group, v_sum in sums.items():
                        terms[group * npack + u] = v_sum[part]
                    at = 2 * npack + u
                    pack = jnp.where(lane == at, pltpu.roll(h[part, cells - 128:], at + 1, 1), pack)
                    at = 3 * npack + u
                    pack = jnp.where(lane == at, pltpu.roll(h[part, :128], at, 1), pack)
        width = 1
        while width < 128:
            high = (lane & width) != 0
            merged = {}
            for i in range(64 // width):
                x, y = terms.get(2 * i), terms.get(2 * i + 1)
                if x is not None and y is not None:
                    merged[i] = jnp.where(high, y, x) + pltpu.roll(jnp.where(high, x, y), width, 1)
                elif x is not None or y is not None:
                    x = y if x is None else x
                    merged[i] = x + pltpu.roll(x, width, 1)
            terms, width = merged, width * 2
        middle = (lane >= 2 * npack) & (lane < 4 * npack)
        pack = jnp.where(middle, pack, terms[0])
        packet[...] = pack
        inbox[1, 0] = pack

    def packet_copy(to, s, a):
        return pltpu.make_async_remote_copy(
            src_ref=packet,
            dst_ref=inbox.at[2 - to, lax.rem(s - sec + nsec, nsec)],
            send_sem=packet_ssem.at[to],
            recv_sem=packet_rsem.at[2 - to],
            device_id={"sec": s, "ax": a},
            device_id_type=MESH,
        )

    def packet_to(to, s, a):
        packet_copy(to, s, a).start()

    def all_packets(to):
        box = inbox.at[to] if to != 1 else inbox.at[1, pl.ds(1, nsec - 1)]
        return pltpu.make_async_remote_copy(
            src_ref=box,
            dst_ref=box,
            send_sem=packet_ssem.at[to],
            recv_sem=packet_rsem.at[to],
            device_id={"sec": lax.rem(sec + 1, nsec)},
            device_id_type=MESH,
        )

    for side in (0, 1):
        pl.when(near & sides[side][2])(functools.partial(packet_to, 2 * side, sec, ax + 2 * side - 1))
    visit("early", packet_to)

    for copy in loads[2:]:
        copy.wait()
    first, last = lax.fori_loop(NEAR // 8 + 1, tiles, fluxes, (first, last))
    sec_send[0] = first
    sec_send[1] = last

    def sec_copy(side):
        return pltpu.make_async_remote_copy(
            src_ref=sec_send.at[side],
            dst_ref=sec_recv.at[1 - side],
            send_sem=sec_ssem.at[side],
            recv_sem=sec_rsem.at[1 - side],
            device_id=secs[side][1],
            device_id_type=MESH,
        )


    for k in range(fields):
        for p in range(planes):
            slot = k * planes + p
            rad_send[0, slot:slot + 1, :] = rg[k, p, 8:9, :]
            rad_send[1, slot:slot + 1, :] = rg[k, p, rows + 7:rows + 8, :]

    def rad_copy(side):
        return pltpu.make_async_remote_copy(
            src_ref=rad_send.at[side],
            dst_ref=rad_recv.at[1 - side],
            send_sem=rad_ssem.at[side],
            recv_sem=rad_rsem.at[1 - side],
            device_id=rads[side][1],
            device_id_type=MESH,
        )

    for side in (0, 1):
        pl.when(secs[side][2])(lambda side=side: sec_copy(side).start())
        pl.when(rads[side][2])(lambda side=side: rad_copy(side).start())
    for side in (0, 1):
        pl.when(sides[side][3] & (odd == side))(
            lambda side=side: answered(ax_ready.at[side], functools.partial(send_ax, side, range(CHUNKS)))
        )
    for side in (0, 1):
        pl.when(sides[side][3] & (odd != side) & ~sides[side][4])(
            lambda side=side: answered(ax_ready.at[side], functools.partial(send_ax, side, range(CHUNKS)))
        )
    for side in (0, 1):
        pl.when(secs[side][3] & ~secs[side][4])(lambda side=side: answered(sec_ready.at[side], sec_copy(side).start))

    inv_r = inverse_radius(rows)
    for p in range(planes):
        for k in range(fields):
            out_ref[k, p] = rhs(k, p, rows, inv_r)

    pl.when(rads[1][3])(lambda: answered(rad_ready.at[1], rad_copy(1).start))

    @pl.when(near)
    def _():
        for side in (0, 1):
            pl.when(sides[side][3] & ~sides[side][4])(functools.partial(packet_to, 2 * side, sec, ax + 2 * side - 1))
        answers = sum(size(to, "late") for to in range(3))
        pl.when(answers > 0)(lambda: pl.semaphore_wait(packet_ready.at[0], answers))

    visit("late", packet_to)

    def axial(c, both=(0, 1)):
        for side in both:
            @pl.when(sides[side][0])
            def _():
                ax_copy(1 - side, c).wait_recv()
                part = pl.ds(c * crow, crow)
                d, mx, mr, mt, e = [ghost[side, k, part, :] for k in range(fields)]
                ux, ur, ut, pr = primitive(d, mx, mr, mt, e)
                s = 0.5 if side == 0 else -0.5
                hx = s * ux
                for k, v in enumerate((s * mx, mx * hx + s * pr, mr * hx, mt * hx, (e + pr) * hx)):
                    out_ref[k, side, part, :] += v

    def scan(p):
        fv = factors()
        lane16 = lax.broadcasted_iota(jnp.int32, (NEAR, 128), 1)
        keeps = zero
        scale = spread[2]
        for k in range(fields):
            for half in (0, 1):
                x = out_ref[k, p, 0:NEAR, half * 128:(half + 1) * 128]
                for d in (1, 2, 4, 8):
                    swap = jnp.where((lane16 & d) == 0, pltpu.roll(x, 128 - d, 1), pltpu.roll(x, d, 1))
                    x = jnp.where(fv > d, 0.5 * (x + swap), x)
                a, b = x, x
                for n, d in enumerate(SHIFTS):
                    a = a + coef_f[n] * pltpu.roll(a, d, 1)
                    b = b + coef_b[n] * pltpu.roll(b, 128 - d, 1)
                near_c[half, k, p] = scale * (a + b - x)
                for rt in (0, 1):
                    u = (k * planes + p) * 2 + rt
                    if half == 0:
                        tail = pltpu.roll(a[rt * 8:rt * 8 + 8], (u + 1) % 128, 1)
                        keeps = jnp.where(lane == u, tail, keeps)
                    else:
                        head = pltpu.roll(b[rt * 8:rt * 8 + 8], npack + u, 1)
                        keeps = jnp.where(lane == npack + u, head, keeps)
        keep_ref[...] = keeps if p == planes - 1 else keep_ref[...] + keeps

    axial(0, (1,))
    pl.when(near)(functools.partial(scan, 1))

    @pl.when(sides[0][4])
    def _():
        answered(ax_ready.at[0], functools.partial(send_ax, 0, range(CHUNKS)))
        packet_to(0, sec, ax - 1)

    @pl.when(reach)
    def _():
        pl.semaphore_wait(packet_ready.at[1], 1)
        packet_to(jnp.where(ax == 0, 1, 0), 0, 0)

    for side in (0, 1):
        pl.when(secs[side][4])(lambda side=side: answered(sec_ready.at[side], sec_copy(side).start))

    axial(0, (0,))
    pl.when(near)(functools.partial(scan, 0))

    sec_copy(1).wait_recv()
    sec_copy(0).wait_recv()
    before = sec_recv[0]
    behind = sec_recv[1]
    thin = lax.broadcasted_iota(jnp.int32, (rows, 128), 1)

    def edges(packed, slot, to):
        column = [pltpu.roll(packed, (to - slot - t) % 128, 1) for t in range(tiles)]
        return jnp.concatenate(column, axis=0) * inv_r[:, :128]

    for p in range(planes):
        for k in range(fields):
            slot = (k * planes + p) * tiles
            out_ref[k, p, :, :128] += jnp.where(thin == 0, edges(before, slot, 0), 0.0)
            out_ref[k, p, :, cells - 128:] -= jnp.where(thin == 127, edges(behind, slot, 127), 0.0)

    for c in range(1, CHUNKS):
        axial(c)

    pl.when(rads[0][3])(lambda: answered(rad_ready.at[0], rad_copy(0).start))
    for side in (0, 1):
        @pl.when(rads[side][0])
        def _():
            rad_copy(1 - side).wait_recv()
            row = 0 if side == 0 else rows - 1
            sign = 1.0 if side == 0 else -1.0
            for k in range(fields):
                for p in range(planes):
                    slot = k * planes + p
                    out_ref[k, p, row:row + 1, :] += (sign * inv_r[row:row + 1, :]) * rad_recv[side, slot:slot + 1, :]

    @pl.when(near)
    def _():
        group = lane // npack
        sum_f, sum_b, sum_x = zero, zero, zero
        all_packets(1).wait_recv()
        for side in (0, 1):
            pl.when(sides[side][0])(all_packets(2 * side).wait_recv)
        for m in range(nsec):
            sum_f += inbox[1, m] * weights[0, m]
            sum_b += inbox[1, m] * weights[1, m]
            sum_x += jnp.where(lane % 4 < 2, inbox[0, m], inbox[2, m]) * weights[2, m]

        def down(v, groups):
            return pltpu.roll(v, 128 - groups * npack, 1)

        sum_f = sum_f + down(sum_f, 2) + down(sum_f, 3)
        sum_b = sum_b + down(sum_b, 1) + down(sum_b, 2)
        total_in = jnp.where(group == 0, sum_f, sum_b) + down(sum_x, 4)
        inner = keep_ref[...] + rate_ref[...] * total_in
        for k in range(fields):
            for p in range(planes):
                for rt in (0, 1):
                    u = (k * planes + p) * 2 + rt
                    part = slice(rt * 8, rt * 8 + 8)
                    for half in (0, 1):
                        src_f, src_b = (total_in, inner) if half == 0 else (inner, total_in)
                        cf = jnp.broadcast_to(src_f[:, u:u + 1], (8, 128))
                        cb = jnp.broadcast_to(src_b[:, npack + u:npack + u + 1], (8, 128))
                        w = near_c[half, k, p, part, :] + spread[0, part, :] * cf + spread[1, part, :] * cb
                        out_ref[k, p, part, half * 128:(half + 1) * 128] = w

    @pl.when(near)
    def _():
        all_packets(1).wait_send()
        for side in (0, 1):
            pl.when(sides[side][0])(all_packets(2 * side).wait_send)

    sec_copy(0).wait_send()
    sec_copy(1).wait_send()
    for side in (0, 1):
        pl.when(rads[side][0])(lambda side=side: rad_copy(side).wait_send())
        for c in range(CHUNKS):
            pl.when(sides[side][0])(lambda side=side, c=c: ax_copy(side, c).wait_send())


def body(state, coarsen):
    fields, planes, rows, cells = state.shape
    nsec, nrad, nax = lax.axis_size("sec"), lax.axis_size("rad"), lax.axis_size("ax")
    block = (fields, planes, rows, cells)
    f32 = jnp.float32
    dma = pltpu.SemaphoreType.DMA
    return pl.pallas_call(
        functools.partial(kernel, nsec, nrad, nax),
        out_shape=pltpu.VMEM(block, f32),
        in_specs=[
            pl.BlockSpec(memory_space=pltpu.HBM),
            pl.BlockSpec(memory_space=pltpu.HBM),
        ],
        out_specs=pl.BlockSpec(memory_space=pltpu.VMEM),
        scratch_shapes=[
            pltpu.SMEM((NEAR,), jnp.int32),
            dma(()),
            pltpu.VMEM(block, f32),
            pltpu.VMEM(block, f32),
            pltpu.VMEM((fields, planes, rows + 16, cells), f32),
            pltpu.VMEM(block, f32),
            pltpu.VMEM((2, fields, rows, cells), f32),
            pltpu.VMEM((2, fields * planes, cells), f32),
            pltpu.VMEM((2, fields * planes, cells), f32),
            pltpu.VMEM((2, 8, 128), f32),
            pltpu.VMEM((2, 8, 128), f32),
            pltpu.VMEM((len(SHIFTS), NEAR, 128), f32),
            pltpu.VMEM((len(SHIFTS), NEAR, 128), f32),
            pltpu.VMEM((3, NEAR, cells), f32),
            pltpu.VMEM((3, NEAR, cells), f32),
            pltpu.VMEM((3, NEAR, 128), f32),
            pltpu.VMEM((8, 128), f32),
            pltpu.VMEM((3, nsec, 8, 128), f32),
            pltpu.VMEM((2, fields, planes, NEAR, 128), f32),
            pltpu.VMEM((8, 128), f32),
            pltpu.VMEM((8, 128), f32),
            pltpu.VMEM((3, nsec, 8, 128), f32),
            dma((CHUNKS,)),
            dma((2, CHUNKS)),
            dma((2, CHUNKS)),
            dma((2,)),
            dma((2,)),
            dma((2,)),
            dma((2,)),
            dma((3,)),
            dma((3,)),
            pltpu.SemaphoreType.REGULAR((2,)),
            pltpu.SemaphoreType.REGULAR((2,)),
            pltpu.SemaphoreType.REGULAR((2,)),
            pltpu.SemaphoreType.REGULAR((2,)),
        ],
        compiler_params=pltpu.CompilerParams(
            collective_id=0, has_side_effects=True, vmem_limit_bytes=32 * 1024 * 1024
        ),
        cost_estimate=pl.CostEstimate(flops=4_000_000, bytes_accessed=2_000_000, transcendentals=0),
    )(pltpu.with_memory_space_constraint(coarsen, pltpu.HBM), pltpu.with_memory_space_constraint(state, pltpu.HBM))


def solution(mesh):
    return jax.shard_map(
        body,
        mesh=mesh,
        in_specs=(P(None, "ax", "rad", "sec"), P()),
        out_specs=P(None, "ax", "rad", "sec"),
        check_vma=False,
    )
```

```python
import functools
import math

import jax
import jax.numpy as jnp
from jax import lax
from jax.experimental import pallas as pl
from jax.experimental.pallas import tpu as pltpu
from jax.sharding import PartitionSpec as P

GAMMA = 1.4
KAPPA = 1.44
NEAR = 16
FACTORS = (1, 2, 4, 8, 16)
SHIFTS = (1, 2, 4, 8, 16, 32, 64)
MESH = pl.DeviceIdType.MESH
CHUNKS = 4


def filter_constants(total_cells):
    dtheta = 2.0 * math.pi / total_cells
    out = {}
    for f in FACTORS:
        beta = KAPPA / (f * dtheta) ** 2
        half = 0.5 / beta
        gap = math.sqrt(half * (2.0 + half)) - half
        out[f] = (1.0 - gap, math.log1p(-gap), 1.0 / (1.0 + 2.0 * beta * gap))
    return out


def primitive(d, mx, mr, mt, e):
    inv = 1.0 / d
    ux, ur, ut = mx * inv, mr * inv, mt * inv
    p = (GAMMA - 1.0) * (e - 0.5 * (mx * ux + mr * ur + mt * ut))
    return ux, ur, ut, p


def by_factor(fv, values):
    out = jnp.full(fv.shape, values[0], jnp.float32)
    for f, v in zip(FACTORS[1:], values[1:]):
        out = jnp.where(fv == f, jnp.float32(v), out)
    return out


def kernel(
    nsec, nrad, nax,
    coarsen_hbm, state_ref, out_ref,
    coarsen_ref, coarsen_sem, st, fx, rg, hz, ghost, rad_send, rad_recv, sec_send, sec_recv,
    coef_f, coef_b, weigh_f, weigh_b, spread, rate_ref, weights, near_c, packet, keep_ref, inbox,
    load_sem, ax_ssem, ax_rsem, rad_ssem, rad_rsem, sec_ssem, sec_rsem, packet_ssem, packet_rsem,
    ax_ready, rad_ready, sec_ready, packet_ready,
):
    fields, planes, rows, cells = st.shape
    total = cells * nsec
    dtheta = 2.0 * math.pi / total
    tiles = rows // 8
    crow = rows // CHUNKS
    sec, rad, ax = lax.axis_index("sec"), lax.axis_index("rad"), lax.axis_index("ax")
    near = rad == 0

    loads = []
    for c in range(CHUNKS):
        part = pl.ds(c * crow, crow)
        copy = pltpu.make_async_copy(state_ref.at[:, :, part, :], st.at[:, :, part, :], load_sem.at[c])
        copy.start()
        loads.append(copy)

    factor_load = pltpu.make_async_copy(coarsen_hbm, coarsen_ref, coarsen_sem)
    pl.when(near)(factor_load.start)

    def slow(s, r, a):
        return (s == 0) & (r == 0) & (a == 0)

    def rank(s, a):
        turn = jnp.where(s < nsec // 2, s, nsec + nsec // 2 - 1 - s)
        step = jnp.where(a == 0, 3, jnp.where(a == 1, 0, jnp.where(a == 2, 2, 1)))
        return 4 * turn + step + jnp.where(slow(s, rad, a), 1000, 0)

    mine = rank(sec, ax)
    barrier = pltpu.get_barrier_semaphore()

    def signal(sem, where):
        pl.semaphore_signal(sem, inc=1, device_id=where, device_id_type=MESH)

    sides = [
        (there, {"ax": a}, there & (rank(sec, a) < mine), there & (rank(sec, a) > mine), there & slow(sec, rad, a))
        for there, a in ((ax > 0, ax - 1), (ax < nax - 1, ax + 1))
    ]
    rads = [
        (rad > 0, {"rad": rad - 1}, (rad > 0) & ~slow(sec, rad - 1, ax), slow(sec, rad - 1, ax)),
        (rad < nrad - 1, {"rad": rad + 1}, slow(sec, rad, ax), (rad < nrad - 1) & ~slow(sec, rad, ax)),
    ]
    secs = [
        (True, {"sec": s}, rank(s, ax) < mine, rank(s, ax) > mine, slow(s, rad, ax))
        for s in (lax.rem(sec + nsec - 1, nsec), lax.rem(sec + 1, nsec))
    ]
    far = ~near
    for _, where, _, later, *_ in rads + sides:
        pl.when(later)(functools.partial(signal, barrier, where))
    for _, where, _, later, _ in secs:
        pl.when(far & later)(functools.partial(signal, barrier, where))

    tardy = slow(sec, rad, ax)
    turn = jnp.where(sec < nsec // 2, sec, nsec + nsec // 2 - 1 - sec)
    reach = near & (ax <= 1) & (sec != 0)

    middle = turn == 3
    after = (turn >= 4) & (turn < 7)

    def spans(to, kind):
        first = jnp.where(tardy | (ax + to == 1), 1, 0)
        upto = jnp.where(tardy, nsec, turn)
        beyond = jnp.where(tardy, nsec, turn + 1)
        if kind == "greet":
            return (beyond, nsec), (jnp.where(after, 3, 0), jnp.where(after, 4, 0))
        if kind == "answer":
            return (first, jnp.where(after, 3, upto)), (jnp.where(after, 4, 0), jnp.where(after, turn, 0))
        if kind == "early":
            return (first, upto), (jnp.where(middle, 4, 0), jnp.where(middle, 7, 0))
        return (beyond, jnp.where(middle, 4, nsec)), (jnp.where(middle, 7, 0), jnp.where(middle, nsec, 0))

    def there(to):
        return near if to == 1 else near & sides[to // 2][0]

    def size(to, kind):
        return jnp.where(there(to), sum(jnp.maximum(hi - lo, 0) for lo, hi in spans(to, kind)), 0)

    def visit(kind, act):
        for to in (1, 0, 2):
            def step(t, carry):
                s = jnp.where(t < nsec // 2, t, nsec + nsec // 2 - 1 - t)
                act(to, s, ax + (to - 1))
                return carry

            @pl.when(there(to))
            def _():
                for lo, hi in spans(to, kind):
                    lax.fori_loop(lo, hi, step, 0)

    visit("greet", lambda to, s, a: signal(barrier, {"sec": s, "ax": a}))
    pl.when(reach)(lambda: signal(barrier, {"sec": 0, "ax": 0}))

    def ax_copy(side, c):
        part = pl.ds(c * crow, crow)
        return pltpu.make_async_remote_copy(
            src_ref=state_ref.at[:, (planes - 1) if side == 1 else 0, part, :],
            dst_ref=ghost.at[1 - side, :, part, :],
            send_sem=ax_ssem.at[side, c],
            recv_sem=ax_rsem.at[1 - side, c],
            device_id=sides[side][1],
            device_id_type=MESH,
        )

    def answered(ready, send):
        pl.semaphore_wait(ready, 1)
        send()

    def send_ax(side, chunks):
        for c in chunks:
            ax_copy(side, c).start()

    odd = ax % 2

    def enter():
        def number(flags):
            return sum(jnp.where(flag, 1, 0) for flag in flags)

        count = number(v[2] for v in rads + sides)
        count = count + jnp.where(near, sum(size(to, "early") for to in range(3)), number(v[2] for v in secs))
        pl.when(count > 0)(lambda: pl.semaphore_wait(barrier, count))

        for ready, pairs in ((ax_ready, sides), (sec_ready, secs), (rad_ready, rads)):
            for side in (0, 1):
                pl.when(pairs[side][2])(functools.partial(signal, ready.at[1 - side], pairs[side][1]))

        for side in (0, 1):
            pl.when(sides[side][2] & (odd != side))(functools.partial(send_ax, side, range(CHUNKS)))
        def answer(t, carry):
            s = jnp.where(t < nsec // 2, t, nsec + nsec // 2 - 1 - t)
            for to in (1, 0, 2):
                pl.when(there(to) & (t >= spans(to, "answer")[0][0]))(
                    functools.partial(signal, packet_ready.at[jnp.where(tardy, 1, 0)], {"sec": s, "ax": ax + (to - 1)})
                )
            return carry

        @pl.when(near)
        def _():
            for lo, hi in ((0, spans(1, "answer")[0][1]), spans(1, "answer")[1]):
                lax.fori_loop(lo, hi, answer, 0)

        for side in (0, 1):
            pl.when(sides[side][2] & (odd == side))(functools.partial(send_ax, side, range(CHUNKS)))

    pl.when(tardy)(enter)

    lane = lax.broadcasted_iota(jnp.int32, (8, 128), 1)
    consts = filter_constants(total)

    def factors():
        row16 = lax.broadcasted_iota(jnp.int32, (NEAR, 128), 0)
        fv = jnp.full((NEAR, 128), 1, jnp.int32)
        for i in range(NEAR):
            fv = jnp.where(row16 == i, coarsen_ref[i], fv)
        return fv

    @pl.when(near)
    def _():
        factor_load.wait()
        fv = factors()
        lane16 = lax.broadcasted_iota(jnp.int32, (NEAR, 128), 1)
        for n, d in enumerate(SHIFTS):
            step = by_factor(fv, [math.exp(consts[f][1] * (d // f)) if d >= f else 0.0 for f in FACTORS])
            coef_f[n] = jnp.where(lane16 >= d, step, 0.0)
            coef_b[n] = jnp.where(lane16 < 128 - d, step, 0.0)
        fw = jnp.concatenate([fv, fv], axis=1)
        share = by_factor(fw, [1.0 / f for f in FACTORS])
        logs = by_factor(fw, [consts[f][1] for f in FACTORS])
        block = lax.broadcasted_iota(jnp.int32, (NEAR, cells), 1).astype(jnp.float32)
        block = jnp.floor(block * share)
        wide = lax.broadcasted_iota(jnp.int32, (NEAR, cells), 1)
        inv_r = 1.0 / (lax.broadcasted_iota(jnp.int32, (NEAR, cells), 0).astype(jnp.float32) + 0.5)
        for ref, power in ((weigh_f, cells * share - 1.0 - block), (weigh_b, block)):
            w = share * jnp.exp(logs * power)
            ref[0] = w
            ref[1] = w * inv_r
            ref[2] = inv_r * (
                jnp.where(wide == cells - 1, 0.0, pltpu.roll(w, cells - 1, 1)) - jnp.where(wide == 0, 0.0, pltpu.roll(w, 1, 1))
            )
        scale = by_factor(fv, [consts[f][2] for f in FACTORS])
        share, logs, block = share[:, :128], logs[:, :128], block[:, :128]
        spread[0] = scale * jnp.exp(logs * (block + 1.0))
        spread[1] = scale * jnp.exp(logs * (128.0 * share - block))
        spread[2] = scale
        packed = jnp.where(lane % 2 == 0, fv[0:8], fv[8:16])
        rate_ref[...] = by_factor(packed, [math.exp(consts[f][1] * (128 // f)) for f in FACTORS])

        def by_distance(m):
            logs = [consts[f][1] * (cells // f) for f in FACTORS]
            return by_factor(packed, [math.exp(g * (m - 1)) / -math.expm1(g * nsec) for g in logs])

        ahead = [None] + [by_distance(m) for m in range(1, nsec + 1)]
        back = [None] + [ahead[nsec - m] for m in range(1, nsec)] + [ahead[nsec]]
        row = (lane % 2) * 8 + lax.broadcasted_iota(jnp.int32, (8, 128), 0)
        edge = by_factor(packed, [1.0 / f for f in FACTORS]) / (row.astype(jnp.float32) + 0.5)
        across = edge * by_factor(packed, [math.exp(consts[f][1] * (cells // f - 1)) for f in FACTORS])
        group = lane // (fields * planes * 2)
        direct = edge * by_factor(packed, [math.exp(-consts[f][1]) for f in FACTORS])
        for m in range(1, nsec + 1):
            prev, after_m = (m - 1) or nsec, m % nsec + 1
            k = m % nsec
            from_last, from_first = across * ahead[prev], -edge * ahead[after_m]
            to_last, to_first = edge * back[prev], -across * back[after_m]
            if m == 1:
                from_last = from_last + direct
            if m == nsec - 1:
                to_first = to_first - direct
            weights[0, k] = jnp.where(group == 0, ahead[m], jnp.where(group == 2, from_last, from_first))
            weights[1, k] = jnp.where(group == 1, back[m], jnp.where(group == 2, to_last, to_first))
            weights[2, k] = jnp.where(group == 4, ahead[m], back[m])
        for side in (0, 1):
            @pl.when(jnp.logical_not(sides[side][0]))
            def _():
                inbox[2 * side] = jnp.zeros((nsec, 8, 128), jnp.float32)

    for k in range(fields):
        for p in range(planes):
            for edge in (7, rows + 8):
                rg[k, p, edge:edge + 1, :] = jnp.zeros((1, cells), jnp.float32)

    for copy in loads[:2]:
        copy.wait()

    row8 = lax.broadcasted_iota(jnp.int32, (8, cells), 0)

    def radius(t):
        return (rad * rows + t * 8 + row8).astype(jnp.float32) + 0.5

    def fluxes(t, carry):
        first, last = carry
        part = pl.ds(pl.multiple_of(t * 8, 8), 8)
        padded = pl.ds(pl.multiple_of(t * 8 + 8, 8), 8)
        half_r = 0.5 * radius(t)
        for p in range(planes):
            d, mx, mr, mt, e = [st[k, p, part, :] for k in range(fields)]
            ux, ur, ut, pr = primitive(d, mx, mr, mt, e)
            ep = e + pr
            hx = 0.5 * ux
            for k, v in enumerate((0.5 * mx, mx * hx + 0.5 * pr, mr * hx, mt * hx, ep * hx)):
                fx[k, p, part, :] = v
            gr = half_r * ur
            for k, v in enumerate((half_r * mr, mx * gr, mr * gr + half_r * pr, mt * gr, ep * gr)):
                rg[k, p, padded, :] = v
            s = 0.5 / dtheta
            gt = s * ut
            for k, v in enumerate((s * mt, mx * gt, mr * gt, mt * gt + s * pr, ep * gt)):
                hz[k, p, part, :] = v
                slot = (k * planes + p) * tiles + t
                here = lane == slot
                first = jnp.where(here, pltpu.roll(v[:, :128], slot, 1), first)
                last = jnp.where(here, pltpu.roll(v[:, cells - 128:], slot + 1, 1), last)
        return first, last

    zero = jnp.zeros((8, 128), jnp.float32)
    first, last = lax.fori_loop(0, NEAR // 8 + 1, fluxes, (zero, zero))
    npack = fields * planes * 2

    def rhs(k, p, size, inv_r):
        part = slice(0, size)
        wide = lax.broadcasted_iota(jnp.int32, (size, cells), 1)
        h = hz[k, p, part, :]
        v = jnp.where(wide == 0, 0.0, pltpu.roll(h, 1, 1)) - jnp.where(wide == cells - 1, 0.0, pltpu.roll(h, cells - 1, 1))
        v = v + (rg[k, p, 7:size + 7, :] - rg[k, p, 9:size + 9, :])
        if k == 2:
            v = v + (2.0 * dtheta) * hz[3, p, part, :]
        if k == 3:
            v = v - (2.0 * dtheta) * hz[2, p, part, :]
        v = v * inv_r
        return v - fx[k, 1, part, :] if p == 0 else v + fx[k, 0, part, :]

    def inverse_radius(size):
        place = rad * rows + lax.broadcasted_iota(jnp.int32, (size, cells), 0)
        return 1.0 / (place.astype(jnp.float32) + 0.5)

    pl.when(~tardy)(enter)

    @pl.when(near)
    def _():
        pack = zero
        terms = {}

        def halves(v):
            return v[:, :128] + v[:, 128:]

        for k in range(fields):
            for p in range(planes):
                h = hz[k, p, 0:NEAR, :]
                g = rg[k, p, 7:NEAR + 7, :] - rg[k, p, 9:NEAR + 9, :]
                if k == 2:
                    g = g + (2.0 * dtheta) * hz[3, p, 0:NEAR, :]
                if k == 3:
                    g = g - (2.0 * dtheta) * hz[2, p, 0:NEAR, :]
                beside = fx[k, 1, 0:NEAR, :] if p == 0 else -fx[k, 0, 0:NEAR, :]
                sums = {}
                for n, w in enumerate((weigh_f, weigh_b)):
                    sums[4 + n] = halves(beside * w[0])
                    sums[n] = halves(g * w[1] + h * w[2]) - sums[4 + n]
                for rt in (0, 1):
                    u = (k * planes + p) * 2 + rt
                    part = slice(rt * 8, rt * 8 + 8)
                    for group, v_sum in sums.items():
                        terms[group * npack + u] = v_sum[part]
                    at = 2 * npack + u
                    pack = jnp.where(lane == at, pltpu.roll(h[part, cells - 128:], at + 1, 1), pack)
                    at = 3 * npack + u
                    pack = jnp.where(lane == at, pltpu.roll(h[part, :128], at, 1), pack)
        width = 1
        while width < 128:
            high = (lane & width) != 0
            merged = {}
            for i in range(64 // width):
                x, y = terms.get(2 * i), terms.get(2 * i + 1)
                if x is not None and y is not None:
                    merged[i] = jnp.where(high, y, x) + pltpu.roll(jnp.where(high, x, y), width, 1)
                elif x is not None or y is not None:
                    x = y if x is None else x
                    merged[i] = x + pltpu.roll(x, width, 1)
            terms, width = merged, width * 2
        middle = (lane >= 2 * npack) & (lane < 4 * npack)
        pack = jnp.where(middle, pack, terms[0])
        packet[...] = pack
        inbox[1, 0] = pack

    def packet_copy(to, s, a):
        return pltpu.make_async_remote_copy(
            src_ref=packet,
            dst_ref=inbox.at[2 - to, lax.rem(s - sec + nsec, nsec)],
            send_sem=packet_ssem.at[to],
            recv_sem=packet_rsem.at[2 - to],
            device_id={"sec": s, "ax": a},
            device_id_type=MESH,
        )

    def packet_to(to, s, a):
        packet_copy(to, s, a).start()

    def all_packets(to):
        box = inbox.at[to] if to != 1 else inbox.at[1, pl.ds(1, nsec - 1)]
        return pltpu.make_async_remote_copy(
            src_ref=box,
            dst_ref=box,
            send_sem=packet_ssem.at[to],
            recv_sem=packet_rsem.at[to],
            device_id={"sec": lax.rem(sec + 1, nsec)},
            device_id_type=MESH,
        )

    for side in (0, 1):
        pl.when(near & sides[side][2])(functools.partial(packet_to, 2 * side, sec, ax + 2 * side - 1))
    visit("early", packet_to)

    for copy in loads[2:]:
        copy.wait()
    first, last = lax.fori_loop(NEAR // 8 + 1, tiles, fluxes, (first, last))
    sec_send[0] = first
    sec_send[1] = last

    def sec_copy(side):
        return pltpu.make_async_remote_copy(
            src_ref=sec_send.at[side],
            dst_ref=sec_recv.at[1 - side],
            send_sem=sec_ssem.at[side],
            recv_sem=sec_rsem.at[1 - side],
            device_id=secs[side][1],
            device_id_type=MESH,
        )


    for k in range(fields):
        for p in range(planes):
            slot = k * planes + p
            rad_send[0, slot:slot + 1, :] = rg[k, p, 8:9, :]
            rad_send[1, slot:slot + 1, :] = rg[k, p, rows + 7:rows + 8, :]

    def rad_copy(side):
        return pltpu.make_async_remote_copy(
            src_ref=rad_send.at[side],
            dst_ref=rad_recv.at[1 - side],
            send_sem=rad_ssem.at[side],
            recv_sem=rad_rsem.at[1 - side],
            device_id=rads[side][1],
            device_id_type=MESH,
        )

    for side in (0, 1):
        pl.when(secs[side][2])(lambda side=side: sec_copy(side).start())
        pl.when(rads[side][2])(lambda side=side: rad_copy(side).start())
    for side in (0, 1):
        pl.when(sides[side][3] & (odd == side))(
            lambda side=side: answered(ax_ready.at[side], functools.partial(send_ax, side, range(CHUNKS)))
        )
    for side in (0, 1):
        pl.when(sides[side][3] & (odd != side) & ~sides[side][4])(
            lambda side=side: answered(ax_ready.at[side], functools.partial(send_ax, side, range(CHUNKS)))
        )
    for side in (0, 1):
        pl.when(secs[side][3] & ~secs[side][4])(lambda side=side: answered(sec_ready.at[side], sec_copy(side).start))

    inv_r = inverse_radius(rows)
    for p in range(planes):
        for k in range(fields):
            out_ref[k, p] = rhs(k, p, rows, inv_r)

    pl.when(rads[1][3])(lambda: answered(rad_ready.at[1], rad_copy(1).start))

    def axial(c, both=(0, 1)):
        for side in both:
            @pl.when(sides[side][0])
            def _():
                ax_copy(1 - side, c).wait_recv()
                part = pl.ds(c * crow, crow)
                d, mx, mr, mt, e = [ghost[side, k, part, :] for k in range(fields)]
                ux, ur, ut, pr = primitive(d, mx, mr, mt, e)
                s = 0.5 if side == 0 else -0.5
                hx = s * ux
                for k, v in enumerate((s * mx, mx * hx + s * pr, mr * hx, mt * hx, (e + pr) * hx)):
                    out_ref[k, side, part, :] += v

    def scan(p):
        fv = factors()
        lane16 = lax.broadcasted_iota(jnp.int32, (NEAR, 128), 1)
        keeps = zero
        scale = spread[2]
        for k in range(fields):
            for half in (0, 1):
                x = out_ref[k, p, 0:NEAR, half * 128:(half + 1) * 128]
                for d in (1, 2, 4, 8):
                    swap = jnp.where((lane16 & d) == 0, pltpu.roll(x, 128 - d, 1), pltpu.roll(x, d, 1))
                    x = jnp.where(fv > d, 0.5 * (x + swap), x)
                a, b = x, x
                for n, d in enumerate(SHIFTS):
                    a = a + coef_f[n] * pltpu.roll(a, d, 1)
                    b = b + coef_b[n] * pltpu.roll(b, 128 - d, 1)
                near_c[half, k, p] = scale * (a + b - x)
                for rt in (0, 1):
                    u = (k * planes + p) * 2 + rt
                    if half == 0:
                        tail = pltpu.roll(a[rt * 8:rt * 8 + 8], (u + 1) % 128, 1)
                        keeps = jnp.where(lane == u, tail, keeps)
                    else:
                        head = pltpu.roll(b[rt * 8:rt * 8 + 8], npack + u, 1)
                        keeps = jnp.where(lane == npack + u, head, keeps)
        keep_ref[...] = keeps if p == planes - 1 else keep_ref[...] + keeps

    earliest = near & (turn == 0)

    def second_plane():
        axial(0, (1,))
        pl.when(near)(functools.partial(scan, 1))

    pl.when(earliest)(second_plane)

    @pl.when(near)
    def _():
        for side in (0, 1):
            pl.when(sides[side][3] & ~sides[side][4])(functools.partial(packet_to, 2 * side, sec, ax + 2 * side - 1))
        answers = sum(size(to, "late") for to in range(3))
        pl.when(answers > 0)(lambda: pl.semaphore_wait(packet_ready.at[0], answers))

    visit("late", packet_to)

    pl.when(~earliest)(second_plane)

    @pl.when(sides[0][4])
    def _():
        answered(ax_ready.at[0], functools.partial(send_ax, 0, range(CHUNKS)))
        packet_to(0, sec, ax - 1)

    @pl.when(reach)
    def _():
        pl.semaphore_wait(packet_ready.at[1], 1)
        packet_to(jnp.where(ax == 0, 1, 0), 0, 0)

    for side in (0, 1):
        pl.when(secs[side][4])(lambda side=side: answered(sec_ready.at[side], sec_copy(side).start))

    axial(0, (0,))
    pl.when(near)(functools.partial(scan, 0))

    sec_copy(1).wait_recv()
    sec_copy(0).wait_recv()
    before = sec_recv[0]
    behind = sec_recv[1]
    thin = lax.broadcasted_iota(jnp.int32, (rows, 128), 1)

    def edges(packed, slot, to):
        column = [pltpu.roll(packed, (to - slot - t) % 128, 1) for t in range(tiles)]
        return jnp.concatenate(column, axis=0) * inv_r[:, :128]

    for p in range(planes):
        for k in range(fields):
            slot = (k * planes + p) * tiles
            out_ref[k, p, :, :128] += jnp.where(thin == 0, edges(before, slot, 0), 0.0)
            out_ref[k, p, :, cells - 128:] -= jnp.where(thin == 127, edges(behind, slot, 127), 0.0)

    for c in range(1, CHUNKS):
        axial(c)

    pl.when(rads[0][3])(lambda: answered(rad_ready.at[0], rad_copy(0).start))
    for side in (0, 1):
        @pl.when(rads[side][0])
        def _():
            rad_copy(1 - side).wait_recv()
            row = 0 if side == 0 else rows - 1
            sign = 1.0 if side == 0 else -1.0
            for k in range(fields):
                for p in range(planes):
                    slot = k * planes + p
                    out_ref[k, p, row:row + 1, :] += (sign * inv_r[row:row + 1, :]) * rad_recv[side, slot:slot + 1, :]

    @pl.when(near)
    def _():
        group = lane // npack
        sum_f, sum_b, sum_x = zero, zero, zero
        all_packets(1).wait_recv()
        for side in (0, 1):
            pl.when(sides[side][0])(all_packets(2 * side).wait_recv)
        for m in range(nsec):
            sum_f += inbox[1, m] * weights[0, m]
            sum_b += inbox[1, m] * weights[1, m]
            sum_x += jnp.where(lane % 4 < 2, inbox[0, m], inbox[2, m]) * weights[2, m]

        def down(v, groups):
            return pltpu.roll(v, 128 - groups * npack, 1)

        sum_f = sum_f + down(sum_f, 2) + down(sum_f, 3)
        sum_b = sum_b + down(sum_b, 1) + down(sum_b, 2)
        total_in = jnp.where(group == 0, sum_f, sum_b) + down(sum_x, 4)
        inner = keep_ref[...] + rate_ref[...] * total_in
        for k in range(fields):
            for p in range(planes):
                for rt in (0, 1):
                    u = (k * planes + p) * 2 + rt
                    part = slice(rt * 8, rt * 8 + 8)
                    for half in (0, 1):
                        src_f, src_b = (total_in, inner) if half == 0 else (inner, total_in)
                        cf = jnp.broadcast_to(src_f[:, u:u + 1], (8, 128))
                        cb = jnp.broadcast_to(src_b[:, npack + u:npack + u + 1], (8, 128))
                        w = near_c[half, k, p, part, :] + spread[0, part, :] * cf + spread[1, part, :] * cb
                        out_ref[k, p, part, half * 128:(half + 1) * 128] = w

    @pl.when(near)
    def _():
        all_packets(1).wait_send()
        for side in (0, 1):
            pl.when(sides[side][0])(all_packets(2 * side).wait_send)

    sec_copy(0).wait_send()
    sec_copy(1).wait_send()
    for side in (0, 1):
        pl.when(rads[side][0])(lambda side=side: rad_copy(side).wait_send())
        for c in range(CHUNKS):
            pl.when(sides[side][0])(lambda side=side, c=c: ax_copy(side, c).wait_send())


def body(state, coarsen):
    fields, planes, rows, cells = state.shape
    nsec, nrad, nax = lax.axis_size("sec"), lax.axis_size("rad"), lax.axis_size("ax")
    block = (fields, planes, rows, cells)
    f32 = jnp.float32
    dma = pltpu.SemaphoreType.DMA
    return pl.pallas_call(
        functools.partial(kernel, nsec, nrad, nax),
        out_shape=pltpu.VMEM(block, f32),
        in_specs=[
            pl.BlockSpec(memory_space=pltpu.HBM),
            pl.BlockSpec(memory_space=pltpu.HBM),
        ],
        out_specs=pl.BlockSpec(memory_space=pltpu.VMEM),
        scratch_shapes=[
            pltpu.SMEM((NEAR,), jnp.int32),
            dma(()),
            pltpu.VMEM(block, f32),
            pltpu.VMEM(block, f32),
            pltpu.VMEM((fields, planes, rows + 16, cells), f32),
            pltpu.VMEM(block, f32),
            pltpu.VMEM((2, fields, rows, cells), f32),
            pltpu.VMEM((2, fields * planes, cells), f32),
            pltpu.VMEM((2, fields * planes, cells), f32),
            pltpu.VMEM((2, 8, 128), f32),
            pltpu.VMEM((2, 8, 128), f32),
            pltpu.VMEM((len(SHIFTS), NEAR, 128), f32),
            pltpu.VMEM((len(SHIFTS), NEAR, 128), f32),
            pltpu.VMEM((3, NEAR, cells), f32),
            pltpu.VMEM((3, NEAR, cells), f32),
            pltpu.VMEM((3, NEAR, 128), f32),
            pltpu.VMEM((8, 128), f32),
            pltpu.VMEM((3, nsec, 8, 128), f32),
            pltpu.VMEM((2, fields, planes, NEAR, 128), f32),
            pltpu.VMEM((8, 128), f32),
            pltpu.VMEM((8, 128), f32),
            pltpu.VMEM((3, nsec, 8, 128), f32),
            dma((CHUNKS,)),
            dma((2, CHUNKS)),
            dma((2, CHUNKS)),
            dma((2,)),
            dma((2,)),
            dma((2,)),
            dma((2,)),
            dma((3,)),
            dma((3,)),
            pltpu.SemaphoreType.REGULAR((2,)),
            pltpu.SemaphoreType.REGULAR((2,)),
            pltpu.SemaphoreType.REGULAR((2,)),
            pltpu.SemaphoreType.REGULAR((2,)),
        ],
        compiler_params=pltpu.CompilerParams(
            collective_id=0, has_side_effects=True, vmem_limit_bytes=32 * 1024 * 1024
        ),
        cost_estimate=pl.CostEstimate(flops=4_000_000, bytes_accessed=2_000_000, transcendentals=0),
    )(pltpu.with_memory_space_constraint(coarsen, pltpu.HBM), pltpu.with_memory_space_constraint(state, pltpu.HBM))


def solution(mesh):
    return jax.shard_map(
        body,
        mesh=mesh,
        in_specs=(P(None, "ax", "rad", "sec"), P()),
        out_specs=P(None, "ax", "rad", "sec"),
        check_vma=False,
    )
```

```python
import functools
import math

import jax
import jax.numpy as jnp
from jax import lax
from jax.experimental import pallas as pl
from jax.experimental.pallas import tpu as pltpu
from jax.sharding import PartitionSpec as P

GAMMA = 1.4
KAPPA = 1.44
NEAR = 16
FACTORS = (1, 2, 4, 8, 16)
SHIFTS = (1, 2, 4, 8, 16, 32, 64)
MESH = pl.DeviceIdType.MESH
CHUNKS = 4


def filter_constants(total_cells):
    dtheta = 2.0 * math.pi / total_cells
    out = {}
    for f in FACTORS:
        beta = KAPPA / (f * dtheta) ** 2
        half = 0.5 / beta
        gap = math.sqrt(half * (2.0 + half)) - half
        out[f] = (1.0 - gap, math.log1p(-gap), 1.0 / (1.0 + 2.0 * beta * gap))
    return out


def primitive(d, mx, mr, mt, e):
    inv = 1.0 / d
    ux, ur, ut = mx * inv, mr * inv, mt * inv
    p = (GAMMA - 1.0) * (e - 0.5 * (mx * ux + mr * ur + mt * ut))
    return ux, ur, ut, p


def by_factor(fv, values):
    out = jnp.full(fv.shape, values[0], jnp.float32)
    for f, v in zip(FACTORS[1:], values[1:]):
        out = jnp.where(fv == f, jnp.float32(v), out)
    return out


def kernel(
    nsec, nrad, nax,
    coarsen_hbm, state_ref, out_ref,
    coarsen_ref, coarsen_sem, st, fx, rg, hz, ghost, rad_send, rad_recv, sec_send, sec_recv,
    coef_f, coef_b, weigh_f, weigh_b, spread, rate_ref, weights, near_c, packet, keep_ref, inbox,
    load_sem, ax_ssem, ax_rsem, rad_ssem, rad_rsem, sec_ssem, sec_rsem, packet_ssem, packet_rsem,
    ax_ready, rad_ready, sec_ready, packet_ready,
):
    fields, planes, rows, cells = st.shape
    total = cells * nsec
    dtheta = 2.0 * math.pi / total
    tiles = rows // 8
    crow = rows // CHUNKS
    sec, rad, ax = lax.axis_index("sec"), lax.axis_index("rad"), lax.axis_index("ax")
    near = rad == 0

    loads = []
    for c in range(CHUNKS):
        part = pl.ds(c * crow, crow)
        copy = pltpu.make_async_copy(state_ref.at[:, :, part, :], st.at[:, :, part, :], load_sem.at[c])
        copy.start()
        loads.append(copy)

    factor_load = pltpu.make_async_copy(coarsen_hbm, coarsen_ref, coarsen_sem)
    pl.when(near)(factor_load.start)

    def slow(s, r, a):
        return (s == 0) & (r == 0) & (a == 0)

    def rank(s, a):
        turn = jnp.where(s < nsec // 2, s, nsec + nsec // 2 - 1 - s)
        step = jnp.where(a == 0, 3, jnp.where(a == 1, 0, jnp.where(a == 2, 2, 1)))
        return 4 * turn + step + jnp.where(slow(s, rad, a), 1000, 0)

    mine = rank(sec, ax)
    barrier = pltpu.get_barrier_semaphore()

    def signal(sem, where):
        pl.semaphore_signal(sem, inc=1, device_id=where, device_id_type=MESH)

    sides = [
        (there, {"ax": a}, there & (rank(sec, a) < mine), there & (rank(sec, a) > mine), there & slow(sec, rad, a))
        for there, a in ((ax > 0, ax - 1), (ax < nax - 1, ax + 1))
    ]
    rads = [
        (rad > 0, {"rad": rad - 1}, (rad > 0) & ~slow(sec, rad - 1, ax), slow(sec, rad - 1, ax)),
        (rad < nrad - 1, {"rad": rad + 1}, slow(sec, rad, ax), (rad < nrad - 1) & ~slow(sec, rad, ax)),
    ]
    secs = [
        (True, {"sec": s}, rank(s, ax) < mine, rank(s, ax) > mine, slow(s, rad, ax))
        for s in (lax.rem(sec + nsec - 1, nsec), lax.rem(sec + 1, nsec))
    ]
    far = ~near
    for _, where, _, later, *_ in rads + sides:
        pl.when(later)(functools.partial(signal, barrier, where))
    for _, where, _, later, _ in secs:
        pl.when(far & later)(functools.partial(signal, barrier, where))

    tardy = slow(sec, rad, ax)
    turn = jnp.where(sec < nsec // 2, sec, nsec + nsec // 2 - 1 - sec)
    reach = near & (ax <= 1) & (sec != 0)

    middle = turn == 3
    after = (turn >= 4) & (turn < 7)

    def spans(to, kind):
        first = jnp.where(tardy | (ax + to == 1), 1, 0)
        upto = jnp.where(tardy, nsec, turn)
        beyond = jnp.where(tardy, nsec, turn + 1)
        if kind == "greet":
            return (beyond, nsec), (jnp.where(after, 3, 0), jnp.where(after, 4, 0))
        if kind == "answer":
            return (first, jnp.where(after, 3, upto)), (jnp.where(after, 4, 0), jnp.where(after, turn, 0))
        if kind == "early":
            return (first, upto), (jnp.where(middle, 4, 0), jnp.where(middle, 7, 0))
        return (beyond, jnp.where(middle, 4, nsec)), (jnp.where(middle, 7, 0), jnp.where(middle, nsec, 0))

    def there(to):
        return near if to == 1 else near & sides[to // 2][0]

    def size(to, kind):
        return jnp.where(there(to), sum(jnp.maximum(hi - lo, 0) for lo, hi in spans(to, kind)), 0)

    def visit(kind, act):
        for to in (1, 0, 2):
            def step(t, carry):
                s = jnp.where(t < nsec // 2, t, nsec + nsec // 2 - 1 - t)
                act(to, s, ax + (to - 1))
                return carry

            @pl.when(there(to))
            def _():
                for lo, hi in spans(to, kind):
                    lax.fori_loop(lo, hi, step, 0)

    visit("greet", lambda to, s, a: signal(barrier, {"sec": s, "ax": a}))
    pl.when(reach)(lambda: signal(barrier, {"sec": 0, "ax": 0}))

    lane = lax.broadcasted_iota(jnp.int32, (8, 128), 1)
    consts = filter_constants(total)

    def factors():
        row16 = lax.broadcasted_iota(jnp.int32, (NEAR, 128), 0)
        fv = jnp.full((NEAR, 128), 1, jnp.int32)
        for i in range(NEAR):
            fv = jnp.where(row16 == i, coarsen_ref[i], fv)
        return fv

    @pl.when(near)
    def _():
        factor_load.wait()
        fv = factors()
        lane16 = lax.broadcasted_iota(jnp.int32, (NEAR, 128), 1)
        for n, d in enumerate(SHIFTS):
            step = by_factor(fv, [math.exp(consts[f][1] * (d // f)) if d >= f else 0.0 for f in FACTORS])
            coef_f[n] = jnp.where(lane16 >= d, step, 0.0)
            coef_b[n] = jnp.where(lane16 < 128 - d, step, 0.0)
        fw = jnp.concatenate([fv, fv], axis=1)
        share = by_factor(fw, [1.0 / f for f in FACTORS])
        logs = by_factor(fw, [consts[f][1] for f in FACTORS])
        block = lax.broadcasted_iota(jnp.int32, (NEAR, cells), 1).astype(jnp.float32)
        block = jnp.floor(block * share)
        wide = lax.broadcasted_iota(jnp.int32, (NEAR, cells), 1)
        inv_r = 1.0 / (lax.broadcasted_iota(jnp.int32, (NEAR, cells), 0).astype(jnp.float32) + 0.5)
        for ref, power in ((weigh_f, cells * share - 1.0 - block), (weigh_b, block)):
            w = share * jnp.exp(logs * power)
            ref[0] = w
            ref[1] = w * inv_r
            ref[2] = inv_r * (
                jnp.where(wide == cells - 1, 0.0, pltpu.roll(w, cells - 1, 1)) - jnp.where(wide == 0, 0.0, pltpu.roll(w, 1, 1))
            )
        scale = by_factor(fv, [consts[f][2] for f in FACTORS])
        share, logs, block = share[:, :128], logs[:, :128], block[:, :128]
        spread[0] = scale * jnp.exp(logs * (block + 1.0))
        spread[1] = scale * jnp.exp(logs * (128.0 * share - block))
        spread[2] = scale
        packed = jnp.where(lane % 2 == 0, fv[0:8], fv[8:16])
        rate_ref[...] = by_factor(packed, [math.exp(consts[f][1] * (128 // f)) for f in FACTORS])

        def by_distance(m):
            logs = [consts[f][1] * (cells // f) for f in FACTORS]
            return by_factor(packed, [math.exp(g * (m - 1)) / -math.expm1(g * nsec) for g in logs])

        ahead = [None] + [by_distance(m) for m in range(1, nsec + 1)]
        back = [None] + [ahead[nsec - m] for m in range(1, nsec)] + [ahead[nsec]]
        row = (lane % 2) * 8 + lax.broadcasted_iota(jnp.int32, (8, 128), 0)
        edge = by_factor(packed, [1.0 / f for f in FACTORS]) / (row.astype(jnp.float32) + 0.5)
        across = edge * by_factor(packed, [math.exp(consts[f][1] * (cells // f - 1)) for f in FACTORS])
        group = lane // (fields * planes * 2)
        direct = edge * by_factor(packed, [math.exp(-consts[f][1]) for f in FACTORS])
        for m in range(1, nsec + 1):
            prev, after_m = (m - 1) or nsec, m % nsec + 1
            k = m % nsec
            from_last, from_first = across * ahead[prev], -edge * ahead[after_m]
            to_last, to_first = edge * back[prev], -across * back[after_m]
            if m == 1:
                from_last = from_last + direct
            if m == nsec - 1:
                to_first = to_first - direct
            weights[0, k] = jnp.where(group == 0, ahead[m], jnp.where(group == 2, from_last, from_first))
            weights[1, k] = jnp.where(group == 1, back[m], jnp.where(group == 2, to_last, to_first))
            weights[2, k] = jnp.where(group == 4, ahead[m], back[m])
        for side in (0, 1):
            @pl.when(jnp.logical_not(sides[side][0]))
            def _():
                inbox[2 * side] = jnp.zeros((nsec, 8, 128), jnp.float32)

    for k in range(fields):
        for p in range(planes):
            for edge in (7, rows + 8):
                rg[k, p, edge:edge + 1, :] = jnp.zeros((1, cells), jnp.float32)

    for copy in loads[:2]:
        copy.wait()

    row8 = lax.broadcasted_iota(jnp.int32, (8, cells), 0)

    def radius(t):
        return (rad * rows + t * 8 + row8).astype(jnp.float32) + 0.5

    def fluxes(t, carry):
        first, last = carry
        part = pl.ds(pl.multiple_of(t * 8, 8), 8)
        padded = pl.ds(pl.multiple_of(t * 8 + 8, 8), 8)
        half_r = 0.5 * radius(t)
        for p in range(planes):
            d, mx, mr, mt, e = [st[k, p, part, :] for k in range(fields)]
            ux, ur, ut, pr = primitive(d, mx, mr, mt, e)
            ep = e + pr
            hx = 0.5 * ux
            for k, v in enumerate((0.5 * mx, mx * hx + 0.5 * pr, mr * hx, mt * hx, ep * hx)):
                fx[k, p, part, :] = v
            gr = half_r * ur
            for k, v in enumerate((half_r * mr, mx * gr, mr * gr + half_r * pr, mt * gr, ep * gr)):
                rg[k, p, padded, :] = v
            s = 0.5 / dtheta
            gt = s * ut
            for k, v in enumerate((s * mt, mx * gt, mr * gt, mt * gt + s * pr, ep * gt)):
                hz[k, p, part, :] = v
                slot = (k * planes + p) * tiles + t
                here = lane == slot
                first = jnp.where(here, pltpu.roll(v[:, :128], slot, 1), first)
                last = jnp.where(here, pltpu.roll(v[:, cells - 128:], slot + 1, 1), last)
        return first, last

    zero = jnp.zeros((8, 128), jnp.float32)
    first, last = lax.fori_loop(0, NEAR // 8 + 1, fluxes, (zero, zero))
    npack = fields * planes * 2

    def rhs(k, p, size, inv_r):
        part = slice(0, size)
        wide = lax.broadcasted_iota(jnp.int32, (size, cells), 1)
        h = hz[k, p, part, :]
        v = jnp.where(wide == 0, 0.0, pltpu.roll(h, 1, 1)) - jnp.where(wide == cells - 1, 0.0, pltpu.roll(h, cells - 1, 1))
        v = v + (rg[k, p, 7:size + 7, :] - rg[k, p, 9:size + 9, :])
        if k == 2:
            v = v + (2.0 * dtheta) * hz[3, p, part, :]
        if k == 3:
            v = v - (2.0 * dtheta) * hz[2, p, part, :]
        v = v * inv_r
        return v - fx[k, 1, part, :] if p == 0 else v + fx[k, 0, part, :]

    def inverse_radius(size):
        place = rad * rows + lax.broadcasted_iota(jnp.int32, (size, cells), 0)
        return 1.0 / (place.astype(jnp.float32) + 0.5)

    def number(flags):
        return sum(jnp.where(flag, 1, 0) for flag in flags)

    count = number(v[2] for v in rads + sides)
    count = count + jnp.where(near, sum(size(to, "early") for to in range(3)), number(v[2] for v in secs))
    pl.when(count > 0)(lambda: pl.semaphore_wait(barrier, count))

    for ready, pairs in ((ax_ready, sides), (sec_ready, secs), (rad_ready, rads)):
        for side in (0, 1):
            pl.when(pairs[side][2])(functools.partial(signal, ready.at[1 - side], pairs[side][1]))

    def ax_copy(side, c):
        part = pl.ds(c * crow, crow)
        return pltpu.make_async_remote_copy(
            src_ref=state_ref.at[:, (planes - 1) if side == 1 else 0, part, :],
            dst_ref=ghost.at[1 - side, :, part, :],
            send_sem=ax_ssem.at[side, c],
            recv_sem=ax_rsem.at[1 - side, c],
            device_id=sides[side][1],
            device_id_type=MESH,
        )

    def answered(ready, send):
        pl.semaphore_wait(ready, 1)
        send()

    def send_ax(side, chunks):
        for c in chunks:
            ax_copy(side, c).start()

    odd = ax % 2
    for side in (0, 1):
        pl.when(sides[side][2] & (odd != side))(functools.partial(send_ax, side, range(CHUNKS)))
    def answer(t, carry):
        s = jnp.where(t < nsec // 2, t, nsec + nsec // 2 - 1 - t)
        for to in (1, 0, 2):
            pl.when(there(to) & (t >= spans(to, "answer")[0][0]))(
                functools.partial(signal, packet_ready.at[jnp.where(tardy, 1, 0)], {"sec": s, "ax": ax + (to - 1)})
            )
        return carry

    @pl.when(near)
    def _():
        for lo, hi in ((0, spans(1, "answer")[0][1]), spans(1, "answer")[1]):
            lax.fori_loop(lo, hi, answer, 0)

    for side in (0, 1):
        pl.when(sides[side][2] & (odd == side))(functools.partial(send_ax, side, range(CHUNKS)))
    @pl.when(near)
    def _():
        pack = zero
        terms = {}

        def halves(v):
            return v[:, :128] + v[:, 128:]

        for k in range(fields):
            for p in range(planes):
                h = hz[k, p, 0:NEAR, :]
                g = rg[k, p, 7:NEAR + 7, :] - rg[k, p, 9:NEAR + 9, :]
                if k == 2:
                    g = g + (2.0 * dtheta) * hz[3, p, 0:NEAR, :]
                if k == 3:
                    g = g - (2.0 * dtheta) * hz[2, p, 0:NEAR, :]
                beside = fx[k, 1, 0:NEAR, :] if p == 0 else -fx[k, 0, 0:NEAR, :]
                sums = {}
                for n, w in enumerate((weigh_f, weigh_b)):
                    sums[4 + n] = halves(beside * w[0])
                    sums[n] = halves(g * w[1] + h * w[2]) - sums[4 + n]
                for rt in (0, 1):
                    u = (k * planes + p) * 2 + rt
                    part = slice(rt * 8, rt * 8 + 8)
                    for group, v_sum in sums.items():
                        terms[group * npack + u] = v_sum[part]
                    at = 2 * npack + u
                    pack = jnp.where(lane == at, pltpu.roll(h[part, cells - 128:], at + 1, 1), pack)
                    at = 3 * npack + u
                    pack = jnp.where(lane == at, pltpu.roll(h[part, :128], at, 1), pack)
        width = 1
        while width < 128:
            high = (lane & width) != 0
            merged = {}
            for i in range(64 // width):
                x, y = terms.get(2 * i), terms.get(2 * i + 1)
                if x is not None and y is not None:
                    merged[i] = jnp.where(high, y, x) + pltpu.roll(jnp.where(high, x, y), width, 1)
                elif x is not None or y is not None:
                    x = y if x is None else x
                    merged[i] = x + pltpu.roll(x, width, 1)
            terms, width = merged, width * 2
        middle = (lane >= 2 * npack) & (lane < 4 * npack)
        pack = jnp.where(middle, pack, terms[0])
        packet[...] = pack
        inbox[1, 0] = pack

    def packet_copy(to, s, a):
        return pltpu.make_async_remote_copy(
            src_ref=packet,
            dst_ref=inbox.at[2 - to, lax.rem(s - sec + nsec, nsec)],
            send_sem=packet_ssem.at[to],
            recv_sem=packet_rsem.at[2 - to],
            device_id={"sec": s, "ax": a},
            device_id_type=MESH,
        )

    def packet_to(to, s, a):
        packet_copy(to, s, a).start()

    def all_packets(to):
        box = inbox.at[to] if to != 1 else inbox.at[1, pl.ds(1, nsec - 1)]
        return pltpu.make_async_remote_copy(
            src_ref=box,
            dst_ref=box,
            send_sem=packet_ssem.at[to],
            recv_sem=packet_rsem.at[to],
            device_id={"sec": lax.rem(sec + 1, nsec)},
            device_id_type=MESH,
        )

    for side in (0, 1):
        pl.when(near & sides[side][2])(functools.partial(packet_to, 2 * side, sec, ax + 2 * side - 1))
    visit("early", packet_to)

    for copy in loads[2:]:
        copy.wait()
    first, last = lax.fori_loop(NEAR // 8 + 1, tiles, fluxes, (first, last))
    sec_send[0] = first
    sec_send[1] = last

    def sec_copy(side):
        return pltpu.make_async_remote_copy(
            src_ref=sec_send.at[side],
            dst_ref=sec_recv.at[1 - side],
            send_sem=sec_ssem.at[side],
            recv_sem=sec_rsem.at[1 - side],
            device_id=secs[side][1],
            device_id_type=MESH,
        )


    for k in range(fields):
        for p in range(planes):
            slot = k * planes + p
            rad_send[0, slot:slot + 1, :] = rg[k, p, 8:9, :]
            rad_send[1, slot:slot + 1, :] = rg[k, p, rows + 7:rows + 8, :]

    def rad_copy(side):
        return pltpu.make_async_remote_copy(
            src_ref=rad_send.at[side],
            dst_ref=rad_recv.at[1 - side],
            send_sem=rad_ssem.at[side],
            recv_sem=rad_rsem.at[1 - side],
            device_id=rads[side][1],
            device_id_type=MESH,
        )

    for side in (0, 1):
        pl.when(secs[side][2])(lambda side=side: sec_copy(side).start())
        pl.when(rads[side][2])(lambda side=side: rad_copy(side).start())
    for side in (0, 1):
        pl.when(sides[side][3] & (odd == side))(
            lambda side=side: answered(ax_ready.at[side], functools.partial(send_ax, side, range(CHUNKS)))
        )
    for side in (0, 1):
        pl.when(sides[side][3] & (odd != side) & ~sides[side][4])(
            lambda side=side: answered(ax_ready.at[side], functools.partial(send_ax, side, range(CHUNKS)))
        )
    for side in (0, 1):
        pl.when(secs[side][3] & ~secs[side][4])(lambda side=side: answered(sec_ready.at[side], sec_copy(side).start))

    inv_r = inverse_radius(rows)
    for p in range(planes):
        for k in range(fields):
            out_ref[k, p] = rhs(k, p, rows, inv_r)

    pl.when(rads[1][3])(lambda: answered(rad_ready.at[1], rad_copy(1).start))

    @pl.when(near)
    def _():
        for side in (0, 1):
            pl.when(sides[side][3] & ~sides[side][4])(functools.partial(packet_to, 2 * side, sec, ax + 2 * side - 1))
        answers = sum(size(to, "late") for to in range(3))
        pl.when(answers > 0)(lambda: pl.semaphore_wait(packet_ready.at[0], answers))

    visit("late", packet_to)

    def axial(c, both=(0, 1)):
        for side in both:
            @pl.when(sides[side][0])
            def _():
                ax_copy(1 - side, c).wait_recv()
                part = pl.ds(c * crow, crow)
                d, mx, mr, mt, e = [ghost[side, k, part, :] for k in range(fields)]
                ux, ur, ut, pr = primitive(d, mx, mr, mt, e)
                s = 0.5 if side == 0 else -0.5
                hx = s * ux
                for k, v in enumerate((s * mx, mx * hx + s * pr, mr * hx, mt * hx, (e + pr) * hx)):
                    out_ref[k, side, part, :] += v

    def scan(p):
        fv = factors()
        lane16 = lax.broadcasted_iota(jnp.int32, (NEAR, 128), 1)
        keeps = zero
        scale = spread[2]
        for k in range(fields):
            for half in (0, 1):
                x = out_ref[k, p, 0:NEAR, half * 128:(half + 1) * 128]
                for d in (1, 2, 4, 8):
                    swap = jnp.where((lane16 & d) == 0, pltpu.roll(x, 128 - d, 1), pltpu.roll(x, d, 1))
                    x = jnp.where(fv > d, 0.5 * (x + swap), x)
                a, b = x, x
                for n, d in enumerate(SHIFTS):
                    a = a + coef_f[n] * pltpu.roll(a, d, 1)
                    b = b + coef_b[n] * pltpu.roll(b, 128 - d, 1)
                near_c[half, k, p] = scale * (a + b - x)
                for rt in (0, 1):
                    u = (k * planes + p) * 2 + rt
                    if half == 0:
                        tail = pltpu.roll(a[rt * 8:rt * 8 + 8], (u + 1) % 128, 1)
                        keeps = jnp.where(lane == u, tail, keeps)
                    else:
                        head = pltpu.roll(b[rt * 8:rt * 8 + 8], npack + u, 1)
                        keeps = jnp.where(lane == npack + u, head, keeps)
        keep_ref[...] = keeps if p == planes - 1 else keep_ref[...] + keeps

    axial(0, (1,))
    pl.when(near)(functools.partial(scan, 1))

    @pl.when(sides[0][4])
    def _():
        answered(ax_ready.at[0], functools.partial(send_ax, 0, range(CHUNKS)))
        packet_to(0, sec, ax - 1)

    @pl.when(reach)
    def _():
        pl.semaphore_wait(packet_ready.at[1], 1)
        packet_to(jnp.where(ax == 0, 1, 0), 0, 0)

    for side in (0, 1):
        pl.when(secs[side][4])(lambda side=side: answered(sec_ready.at[side], sec_copy(side).start))

    axial(0, (0,))
    pl.when(near)(functools.partial(scan, 0))

    sec_copy(1).wait_recv()
    sec_copy(0).wait_recv()
    before = sec_recv[0]
    behind = sec_recv[1]
    thin = lax.broadcasted_iota(jnp.int32, (rows, 128), 1)

    def edges(packed, slot, to):
        column = [pltpu.roll(packed, (to - slot - t) % 128, 1) for t in range(tiles)]
        return jnp.concatenate(column, axis=0) * inv_r[:, :128]

    for p in range(planes):
        for k in range(fields):
            slot = (k * planes + p) * tiles
            out_ref[k, p, :, :128] += jnp.where(thin == 0, edges(before, slot, 0), 0.0)
            out_ref[k, p, :, cells - 128:] -= jnp.where(thin == 127, edges(behind, slot, 127), 0.0)

    for c in range(1, CHUNKS):
        axial(c)

    pl.when(rads[0][3])(lambda: answered(rad_ready.at[0], rad_copy(0).start))
    for side in (0, 1):
        @pl.when(rads[side][0])
        def _():
            rad_copy(1 - side).wait_recv()
            row = 0 if side == 0 else rows - 1
            sign = 1.0 if side == 0 else -1.0
            for k in range(fields):
                for p in range(planes):
                    slot = k * planes + p
                    out_ref[k, p, row:row + 1, :] += (sign * inv_r[row:row + 1, :]) * rad_recv[side, slot:slot + 1, :]

    @pl.when(near)
    def _():
        group = lane // npack
        sum_f, sum_b, sum_x = zero, zero, zero
        all_packets(1).wait_recv()
        for side in (0, 1):
            pl.when(sides[side][0])(all_packets(2 * side).wait_recv)
        for m in range(nsec):
            sum_f += inbox[1, m] * weights[0, m]
            sum_b += inbox[1, m] * weights[1, m]
            sum_x += jnp.where(lane % 4 < 2, inbox[0, m], inbox[2, m]) * weights[2, m]

        def down(v, groups):
            return pltpu.roll(v, 128 - groups * npack, 1)

        sum_f = sum_f + down(sum_f, 2) + down(sum_f, 3)
        sum_b = sum_b + down(sum_b, 1) + down(sum_b, 2)
        total_in = jnp.where(group == 0, sum_f, sum_b) + down(sum_x, 4)
        inner = keep_ref[...] + rate_ref[...] * total_in
        for k in range(fields):
            for p in range(planes):
                for rt in (0, 1):
                    u = (k * planes + p) * 2 + rt
                    part = slice(rt * 8, rt * 8 + 8)
                    for half in (0, 1):
                        src_f, src_b = (total_in, inner) if half == 0 else (inner, total_in)
                        cf = jnp.broadcast_to(src_f[:, u:u + 1], (8, 128))
                        cb = jnp.broadcast_to(src_b[:, npack + u:npack + u + 1], (8, 128))
                        w = near_c[half, k, p, part, :] + spread[0, part, :] * cf + spread[1, part, :] * cb
                        out_ref[k, p, part, half * 128:(half + 1) * 128] = w

    @pl.when(near)
    def _():
        all_packets(1).wait_send()
        for side in (0, 1):
            pl.when(sides[side][0])(all_packets(2 * side).wait_send)

    sec_copy(0).wait_send()
    sec_copy(1).wait_send()
    for side in (0, 1):
        pl.when(rads[side][0])(lambda side=side: rad_copy(side).wait_send())
        for c in range(CHUNKS):
            pl.when(sides[side][0])(lambda side=side, c=c: ax_copy(side, c).wait_send())


def body(state, coarsen):
    fields, planes, rows, cells = state.shape
    nsec, nrad, nax = lax.axis_size("sec"), lax.axis_size("rad"), lax.axis_size("ax")
    block = (fields, planes, rows, cells)
    f32 = jnp.float32
    dma = pltpu.SemaphoreType.DMA
    return pl.pallas_call(
        functools.partial(kernel, nsec, nrad, nax),
        out_shape=pltpu.VMEM(block, f32),
        in_specs=[
            pl.BlockSpec(memory_space=pltpu.HBM),
            pl.BlockSpec(memory_space=pltpu.HBM),
        ],
        out_specs=pl.BlockSpec(memory_space=pltpu.VMEM),
        scratch_shapes=[
            pltpu.SMEM((NEAR,), jnp.int32),
            dma(()),
            pltpu.VMEM(block, f32),
            pltpu.VMEM(block, f32),
            pltpu.VMEM((fields, planes, rows + 16, cells), f32),
            pltpu.VMEM(block, f32),
            pltpu.VMEM((2, fields, rows, cells), f32),
            pltpu.VMEM((2, fields * planes, cells), f32),
            pltpu.VMEM((2, fields * planes, cells), f32),
            pltpu.VMEM((2, 8, 128), f32),
            pltpu.VMEM((2, 8, 128), f32),
            pltpu.VMEM((len(SHIFTS), NEAR, 128), f32),
            pltpu.VMEM((len(SHIFTS), NEAR, 128), f32),
            pltpu.VMEM((3, NEAR, cells), f32),
            pltpu.VMEM((3, NEAR, cells), f32),
            pltpu.VMEM((3, NEAR, 128), f32),
            pltpu.VMEM((8, 128), f32),
            pltpu.VMEM((3, nsec, 8, 128), f32),
            pltpu.VMEM((2, fields, planes, NEAR, 128), f32),
            pltpu.VMEM((8, 128), f32),
            pltpu.VMEM((8, 128), f32),
            pltpu.VMEM((3, nsec, 8, 128), f32),
            dma((CHUNKS,)),
            dma((2, CHUNKS)),
            dma((2, CHUNKS)),
            dma((2,)),
            dma((2,)),
            dma((2,)),
            dma((2,)),
            dma((3,)),
            dma((3,)),
            pltpu.SemaphoreType.REGULAR((2,)),
            pltpu.SemaphoreType.REGULAR((2,)),
            pltpu.SemaphoreType.REGULAR((2,)),
            pltpu.SemaphoreType.REGULAR((2,)),
        ],
        compiler_params=pltpu.CompilerParams(
            collective_id=0, has_side_effects=True, vmem_limit_bytes=32 * 1024 * 1024
        ),
        cost_estimate=pl.CostEstimate(flops=4_000_000, bytes_accessed=2_000_000, transcendentals=0),
    )(pltpu.with_memory_space_constraint(coarsen, pltpu.HBM), pltpu.with_memory_space_constraint(state, pltpu.HBM))


def solution(mesh):
    return jax.shard_map(
        body,
        mesh=mesh,
        in_specs=(P(None, "ax", "rad", "sec"), P()),
        out_specs=P(None, "ax", "rad", "sec"),
        check_vma=False,
    )
```
